32 devices in a mesh: dp: 8 (over y, x, core), tensor: 4 (over z).
Axes of the slice: x: 2, y: 2, z: 4, core: 2. Of those that a mesh axis runs over, the one named last changes fastest.
Arguments:
- tokens: bfloat16 [8192, 2048], P('dp'), may hold values from -6 to 6
- cotangent: bfloat16 [8192, 2048], P('dp'), may hold values from -6 to 6
- lengths: int32 [8, 4], P('dp'), may hold values from 1 to 512, 1024 in all within a row
- counts: int32 [8, 8], replicated, may hold values from 0 to 256, as said below
- query_weight: float32 [2048, 2048], P('dp', 'tensor'), may hold values from -0.125 to 0.125
- query_moment: float32 [2048, 2048], P('dp', 'tensor'), may hold values from -0.00010681152 to 0.00010681152
- query_square: float32 [2048, 2048], P('dp', 'tensor'), may hold values from 1.2473528e-09 to 4.942341e-09
- shared_weight: float32 [2048, 256], P(('dp', 'tensor')), may hold values from -0.125 to 0.125
- shared_moment: float32 [2048, 256], P(('dp', 'tensor')), may hold values from -0.00010681152 to 0.00010681152
- shared_square: float32 [2048, 256], P(('dp', 'tensor')), may hold values from 6.119089e-10 to 9.884682e-09
- project_weight: float32 [2048, 2048], P('tensor', 'dp'), may hold values from -0.5 to 0.5
- project_moment: float32 [2048, 2048], P('tensor', 'dp'), may hold values from -0.00010681152 to 0.00010681152
- project_square: float32 [2048, 2048], P('tensor', 'dp'), may hold values from 1.2473528e-09 to 4.942341e-09
- expand_weight: float32 [2048, 8192], P('dp', 'tensor'), may hold values from -0.125 to 0.125
- expand_moment: float32 [2048, 8192], P('dp', 'tensor'), may hold values from -0.00010681152 to 0.00010681152
- expand_square: float32 [2048, 8192], P('dp', 'tensor'), may hold values from 1.2473528e-09 to 4.942341e-09
- shrink_weight: float32 [8192, 2048], P('tensor', 'dp'), may hold values from -0.0625 to 0.0625
- shrink_moment: float32 [8192, 2048], P('tensor', 'dp'), may hold values from -0.00010681152 to 0.00010681152
- shrink_square: float32 [8192, 2048], P('tensor', 'dp'), may hold values from 1.2473528e-09 to 4.942341e-09
- vectors_value: float32 [22656], replicated
- vectors_moment: float32 [22656], replicated, may hold values from -0.00048828125 to 0.00048828125
- vectors_square: float32 [22656], replicated, may hold values from 3.0595444e-08 to 1.2473528e-07
Outputs:
- block_output: bfloat16 [8192, 2048], P('dp')
- input_grad: bfloat16 [8192, 2048], P('dp')
- grad_norm: float32 [], replicated
- updated_query: float32 [2048, 2048], P('dp', 'tensor')
- moment_query: float32 [2048, 2048], P('dp', 'tensor')
- square_query: float32 [2048, 2048], P('dp', 'tensor')
- updated_shared: float32 [2048, 256], P(('dp', 'tensor'))
- moment_shared: float32 [2048, 256], P(('dp', 'tensor'))
- square_shared: float32 [2048, 256], P(('dp', 'tensor'))
- updated_project: float32 [2048, 2048], P('tensor', 'dp')
- moment_project: float32 [2048, 2048], P('tensor', 'dp')
- square_project: float32 [2048, 2048], P('tensor', 'dp')
- updated_expand: float32 [2048, 8192], P('dp', 'tensor')
- moment_expand: float32 [2048, 8192], P('dp', 'tensor')
- square_expand: float32 [2048, 8192], P('dp', 'tensor')
- updated_shrink: float32 [8192, 2048], P('tensor', 'dp')
- moment_shrink: float32 [8192, 2048], P('tensor', 'dp')
- square_shrink: float32 [8192, 2048], P('tensor', 'dp')
- updated_vectors: float32 [22656], replicated
- moment_vectors: float32 [22656], replicated
- square_vectors: float32 [22656], replicated
- clipped_vectors: float32 [22656], replicated
- token_rms: float32 [8192], P('dp')
The draws below stay inside these ranges and needn't reach their ends.
Inputs may be any that keep to these rules, and one draw needn't show every extreme that they name: counts[s, o] tokens of device s belong to owner o; every row and every column sums to 1024; a device's tokens for owners lie in order of owners, and an owner takes sources in order. `lengths`: each row lists the sequences of one owner in order and sums to 1024.
All inputs are finite; a program needn't handle non-finite values.
Results may differ from the reference program's by a relative error of at most 0.023.
Values may be sent and summed in bfloat16 or wider, within the bound.
A program may use at most 256 MiB of HBM per device.

```python
import math
import jax
import jax.numpy as jnp
import numpy as np
from jax import lax

D = 2048
HEADS = 16
HD = 128
FF = 8192
TOK_DEV = 1024
SEQS = 4
STEP = 10
MAXLEN = 512
TOKENS = 8192
VEC = 22656
NPARAMS = 42489984
N_DP = 8


def draw_counts(key, part):
    key = jax.random.fold_in(key, 11)
    key_order, key_delta, key_rows, key_cols = jax.random.split(key, 4)
    half_load = TOK_DEV // N_DP
    order = jax.random.permutation(key_order, N_DP)
    delta = jax.random.randint(key_delta, (N_DP // 2,), -half_load, half_load + 1)
    delta = delta.at[0].set(half_load)
    loads = jnp.full((N_DP,), half_load, jnp.int32)
    loads = loads.at[order[0::2]].add(delta).at[order[1::2]].add(-delta)
    row_perm = jax.random.permutation(key_rows, N_DP)
    col_perm = jax.random.permutation(key_cols, N_DP)
    picked = (row_perm[:, None] + col_perm[None, :]) % N_DP
    return loads[picked].astype(jnp.int32)


def draw_vectors_value(key, part):
    key = jax.random.fold_in(key, 7)
    key_noise, key_jitter = jax.random.split(key)
    position = jnp.arange(VEC)
    within = (position % D).astype(jnp.float32) / D
    is_gain = (position < D) | (position >= 2 * D) & (position < 3 * D)
    jitter = jax.random.uniform(key_jitter, (VEC,), jnp.float32, 0.8, 1.2)
    gains = (0.6 + 1.2 * within) * jitter
    others = 0.3 * jax.random.normal(key_noise, (VEC,), jnp.float32)
    return jnp.where(is_gain, gains, others).astype(jnp.float32)


def draw_shared_square(key, part):
    key = jax.random.fold_in(key, 13)
    lowest = 0.053
    factor = 4.0
    spread = jax.random.uniform(key, (D, 2 * HD), jnp.float32)
    return (lowest / NPARAMS * jnp.exp(spread * jnp.log(factor))).astype(jnp.float32)


def level_of(own_key, dims, shards, smallest, top_value):
    factor_of, own = 1.0, jax.random.fold_in(own_key, 6)
    for dim, parts in shards:
        steps = jnp.exp(jax.random.uniform(jax.random.fold_in(own, dim), (parts,), jnp.float32, smallest / len(shards), top_value / len(shards)))
        factor_of = factor_of * jnp.repeat(steps, dims[dim] // parts).reshape([-1 if axis == dim else 1 for axis in range(len(dims))])
    return factor_of


def length_profile(count, total, bound, skew):
    weights = [(1 << 20) // math.isqrt(standing ** skew) + 1 for standing in range(2, count + 1)]
    rest, given = total - bound - (count - 1), [1] * (count - 1)
    while rest > 0:
        free = [i for i in range(count - 1) if given[i] < bound]
        mass, budget = sum([weights[i] for i in free]), rest
        for i in free:
            more = min(bound - given[i], max(1, budget * weights[i] // mass), rest)
            given[i] = given[i] + more
            rest = rest - more
    return np.array([bound] + given)


def ragged_sizes(rng, count, total, limit, skew):
    if count == 2:
        one = jax.random.randint(rng, (), max(1, total - limit), min(limit, total - 1) + 1)
        return jnp.stack([one, total - one])
    sizes = jnp.asarray(length_profile(count, total, limit, skew), jnp.int32)
    twos = (count - 1) // 2
    donor, receiver = sizes[1:1 + 2 * twos:2], sizes[2:2 + 2 * twos:2]
    slack = jnp.minimum(donor - 1, limit - receiver)
    moved = jax.random.randint(jax.random.fold_in(rng, 1), (twos,), 0, 1 << 20) % (slack + 1)
    sizes = sizes.at[1:1 + 2 * twos:2].set(donor - moved).at[2:2 + 2 * twos:2].set(receiver + moved)
    return sizes[jax.random.permutation(jax.random.fold_in(rng, 2), count)]


def centred(rng, extent, width, limit, shards=(), kind=jnp.bfloat16):
    values = jax.random.normal(rng, extent, jnp.float32) * width
    if len(shards) > 0:
        values = level_of(rng, extent, shards, -0.22, 0.18) * values
    return jnp.clip(values, min=-limit, max=limit).astype(kind)


def setup_inputs(seed: int = 0) -> dict:
    splits = jax.random.split(jax.random.key(seed), 23)
    return {
        "tokens": centred(splits[0], (TOKENS, D), 1.0, 6.0, ((0, 8),)),
        "cotangent": centred(splits[1], (TOKENS, D), 1.0, 6.0, ((0, 8),)),
        "lengths": jax.vmap(lambda own: ragged_sizes(own, SEQS, TOK_DEV, MAXLEN, 1))(jax.random.split(splits[2], N_DP)).reshape((N_DP, SEQS)).astype(jnp.int32),
        "counts": draw_counts(jax.random.fold_in(splits[22], 71), 0),
        "query_weight": centred(splits[4], (D, D), D ** -0.5, 0.125, ((0, 8), (1, 4)), jnp.float32),
        "query_moment": centred(splits[5], (D, D), (0.11 * NPARAMS ** -0.5), 0.00010681152, ((0, 8), (1, 4)), jnp.float32),
        "query_square": jnp.clip(jnp.exp(math.log(4.9423412029625524e-09) - 1.37681562 * jax.random.uniform(splits[6], (D, D), jnp.float32) ** level_of(splits[6], (D, D), ((0, 8), (1, 4)), -0.2, 0.2)), 1.247352776623245e-09, 4.9423412029625524e-09),
        "shared_weight": centred(splits[7], (D, 2 * HD), D ** -0.5, 0.125, ((0, 32),), jnp.float32),
        "shared_moment": centred(splits[8], (D, 2 * HD), (0.11 * NPARAMS ** -0.5), 0.00010681152, ((0, 32),), jnp.float32),
        "shared_square": draw_shared_square(jax.random.fold_in(splits[22], 71), 0),
        "project_weight": centred(splits[10], (D, D), (D // 16) ** -0.5, 0.5, ((0, 4), (1, 8)), jnp.float32),
        "project_moment": centred(splits[11], (D, D), (0.11 * NPARAMS ** -0.5), 0.00010681152, ((0, 4), (1, 8)), jnp.float32),
        "project_square": jnp.clip(jnp.exp(math.log(4.9423412029625524e-09) - 1.37681562 * jax.random.uniform(splits[12], (D, D), jnp.float32) ** level_of(splits[12], (D, D), ((0, 4), (1, 8)), -0.2, 0.2)), 1.247352776623245e-09, 4.9423412029625524e-09),
        "expand_weight": centred(splits[13], (D, FF), D ** -0.5, 0.125, ((0, 8), (1, 4)), jnp.float32),
        "expand_moment": centred(splits[14], (D, FF), (0.11 * NPARAMS ** -0.5), 0.00010681152, ((0, 8), (1, 4)), jnp.float32),
        "expand_square": jnp.clip(jnp.exp(math.log(4.9423412029625524e-09) - 1.37681562 * jax.random.uniform(splits[15], (D, FF), jnp.float32) ** level_of(splits[15], (D, FF), ((0, 8), (1, 4)), -0.2, 0.2)), 1.247352776623245e-09, 4.9423412029625524e-09),
        "shrink_weight": centred(splits[16], (FF, D), FF ** -0.5, 0.0625, ((0, 4), (1, 8)), jnp.float32),
        "shrink_moment": centred(splits[17], (FF, D), (0.11 * NPARAMS ** -0.5), 0.00010681152, ((0, 4), (1, 8)), jnp.float32),
        "shrink_square": jnp.clip(jnp.exp(math.log(4.9423412029625524e-09) - 1.37681562 * jax.random.uniform(splits[18], (FF, D), jnp.float32) ** level_of(splits[18], (FF, D), ((0, 4), (1, 8)), -0.2, 0.2)), 1.247352776623245e-09, 4.9423412029625524e-09),
        "vectors_value": draw_vectors_value(jax.random.fold_in(splits[22], 71), 0),
        "vectors_moment": centred(splits[20], (VEC,), (0.5 * NPARAMS ** -0.5), 0.00048828125, (), jnp.float32),
        "vectors_square": jnp.clip(jnp.exp(jax.random.uniform(splits[21], (VEC,), jnp.float32, math.log(3.059544440020545e-08), math.log(1.2473527988277056e-07))), 3.059544440020545e-08, 1.2473527988277056e-07),
    }


@jax.custom_vjp
def low(v):
    return lax.optimization_barrier(v.astype(jnp.bfloat16)).astype(jnp.float32)

@jax.custom_vjp
def low_back(v):
    return v

def low_keep(v):
    return (low(v), None)

def low_pass(kept, grad):
    return (grad,)

def back_keep(v):
    return (v, None)

def back_low(kept, grad):
    return (low(grad),)
low.defvjp(low_keep, low_pass)
low_back.defvjp(back_keep, back_low)
beta_one = 0.9
beta_two = 0.95
adam_epsilon = 1e-08
decay_rate = 0.1
clip_level = 1.0
norm_epsilon = 1e-05
rate_matrix = 0.6
rate_attention = 2.4
rate_vector = 0.3
masked_score = -1e+30

def precise_dot(left, right):
    return jnp.dot(left, right, precision=lax.Precision.HIGHEST, preferred_element_type=jnp.float32)

def rounded(values):
    return low(low_back(values))

def layer_norm(values, scaling, offset):
    average = lax.optimization_barrier(jnp.mean(values, axis=-1, keepdims=True))
    centered = values - average
    variance = lax.optimization_barrier(jnp.mean(centered * centered, axis=-1, keepdims=True))
    return centered * lax.rsqrt(variance + norm_epsilon) * scaling + offset

def segment_ids(seq_lengths, row_count):
    position = jnp.arange(row_count, dtype=jnp.int32)
    starts = (jnp.cumsum(seq_lengths) - seq_lengths).astype(jnp.int32)
    segment = lax.optimization_barrier(jnp.sum((starts[None, :] <= position[:, None]).astype(jnp.int32), axis=1)).astype(jnp.int32)
    return (segment, position)

def arrival_rows(counts):
    out_start = (jnp.cumsum(counts, axis=1) - counts).astype(jnp.int32)
    in_start = (jnp.cumsum(counts, axis=0) - counts).astype(jnp.int32)
    position = jnp.arange(TOK_DEV, dtype=jnp.int32)
    owner_starts = in_start.T
    source = lax.optimization_barrier(jnp.sum((owner_starts[:, None, :] <= position[None, :, None]).astype(jnp.int32), axis=2)).astype(jnp.int32) - 1
    first_row = jnp.take_along_axis(owner_starts, source, axis=1)
    owners = jnp.arange(N_DP, dtype=jnp.int32)[:, None]
    base_row = out_start[source, owners]
    return (source * TOK_DEV + base_row + position[None, :] - first_row).reshape(-1).astype(jnp.int32)

def split_vectors(vector_all):
    return (vector_all[0:D], vector_all[D:2 * D], vector_all[2 * D:3 * D], vector_all[3 * D:4 * D], vector_all[4 * D:5 * D], vector_all[5 * D:6 * D], vector_all[6 * D:7 * D], vector_all[7 * D:7 * D + FF], vector_all[7 * D + FF:7 * D + FF + HD])

def device_forward(inputs_rows, seq_lengths, matrices, vector_all):
    query_mat, shared_mat, project_mat, expand_mat, shrink_mat = matrices
    gain_one, shift_one, gain_two, shift_two, query_bias, project_bias, shrink_bias, expand_bias, value_bias = split_vectors(vector_all)
    segment, position = segment_ids(seq_lengths, TOK_DEV)
    normed_one = low(layer_norm(inputs_rows, gain_one, shift_one))
    queries = rounded(precise_dot(normed_one, query_mat) + query_bias).reshape(TOK_DEV, HEADS, HD)
    shared_out = precise_dot(normed_one, shared_mat) + jnp.concatenate([jnp.zeros((HD,), jnp.float32), value_bias])
    key_rows = rounded(shared_out[:, :HD])
    value_rows = rounded(shared_out[:, HD:])
    block_rows = min(512, TOK_DEV)
    score_scale = HD ** (-0.5)

    def attend(block_index):
        row_start = block_index * block_rows
        query_block = lax.dynamic_slice_in_dim(queries, row_start, block_rows, 0)
        segment_rows = lax.dynamic_slice_in_dim(segment, row_start, block_rows, 0)
        position_rows = lax.dynamic_slice_in_dim(position, row_start, block_rows, 0)
        scores = low_back(jnp.einsum('bhd,kd->hbk', query_block, key_rows, precision=lax.Precision.HIGHEST) * score_scale)
        allowed = (segment_rows[:, None] == segment[None, :]) & (position_rows[:, None] >= position[None, :])
        scores = jnp.where(allowed[None], scores, masked_score)
        row_max = lax.optimization_barrier(jnp.max(scores, axis=-1, keepdims=True))
        expo = jnp.exp(scores - row_max)
        probs = expo / lax.optimization_barrier(jnp.sum(expo, axis=-1, keepdims=True))
        return jnp.einsum('hbk,kd->bhd', low(probs), value_rows, precision=lax.Precision.HIGHEST)
    heads_out = lax.map(jax.checkpoint(attend), jnp.arange(TOK_DEV // block_rows, dtype=jnp.int32))
    heads_out = rounded(heads_out.reshape(TOK_DEV, D))
    hidden_one = inputs_rows + low_back(precise_dot(heads_out, project_mat) + project_bias)
    normed_two = low(layer_norm(hidden_one, gain_two, shift_two))
    activated = low(jax.nn.gelu(low_back(precise_dot(normed_two, expand_mat) + expand_bias), approximate=True))
    return hidden_one + low_back(precise_dot(activated, shrink_mat) + shrink_bias)

def adamw_step(weight, moment, square, gradient, rate):
    moment_new = beta_one * moment + (1.0 - beta_one) * gradient
    square_new = beta_two * square + (1.0 - beta_two) * gradient * gradient
    moment_hat = moment_new / (1.0 - beta_one ** STEP)
    square_hat = square_new / (1.0 - beta_two ** STEP)
    weight_new = weight - rate * (moment_hat / (jnp.sqrt(square_hat) + adam_epsilon) + decay_rate * weight)
    return (weight_new, moment_new, square_new)

def reference(tokens, cotangent, lengths, counts, query_weight, query_moment, query_square, shared_weight, shared_moment, shared_square, project_weight, project_moment, project_square, expand_weight, expand_moment, expand_square, shrink_weight, shrink_moment, shrink_square, vectors_value, vectors_moment, vectors_square):
    arrival = arrival_rows(counts)

    def forward(inputs_all, query_mat, shared_mat, project_mat, expand_mat, shrink_mat, vector_all):
        matrices = (low(query_mat), low(shared_mat), low(project_mat), low(expand_mat), low(shrink_mat))
        owned = inputs_all[arrival].reshape(N_DP, TOK_DEV, D)

        def scan_step(carried, inputs):
            return (carried, jax.checkpoint(device_forward)(inputs[0], inputs[1], matrices, vector_all))
        carried, results = lax.scan(scan_step, jnp.zeros((), jnp.float32), (owned, lengths))
        return jnp.zeros((TOKENS, D), jnp.float32).at[arrival].set(results.reshape(TOKENS, D))
    outputs, pullback = jax.vjp(forward, tokens.astype(jnp.float32), query_weight, shared_weight, project_weight, expand_weight, shrink_weight, vectors_value)
    gradients = pullback(cotangent.astype(jnp.float32))
    input_grads = gradients[0]
    params = gradients[1:]
    overall = jnp.zeros((), jnp.float32)
    for param_grad in params:
        overall = overall + jnp.sum(param_grad * param_grad)
    grad_size = jnp.sqrt(overall)
    clip_factor = jnp.minimum(1.0, clip_level / (grad_size + 1e-06))
    weights = (query_weight, shared_weight, project_weight, expand_weight, shrink_weight, vectors_value)
    moments = (query_moment, shared_moment, project_moment, expand_moment, shrink_moment, vectors_moment)
    squares = (query_square, shared_square, project_square, expand_square, shrink_square, vectors_square)
    rates = (rate_matrix * D ** (-0.5), rate_attention * D ** (-0.5), rate_attention * D ** (-0.5), rate_matrix * D ** (-0.5), rate_matrix * FF ** (-0.5), rate_vector)
    updated = []
    for which in range(6):
        updated.extend(adamw_step(weights[which], moments[which], squares[which], clip_factor * params[which], rates[which]))
    clipped_vectors = clip_factor * params[5]
    output_low = outputs.astype(jnp.bfloat16)
    output_back = output_low.astype(jnp.float32)
    token_rms = jnp.sqrt(lax.optimization_barrier(jnp.mean(output_back * output_back, axis=1)))
    return (output_low, input_grads.astype(jnp.bfloat16), grad_size, updated[0], updated[1], updated[2], updated[3], updated[4], updated[5], updated[6], updated[7], updated[8], updated[9], updated[10], updated[11], updated[12], updated[13], updated[14], updated[15], updated[16], updated[17], clipped_vectors, token_rms)
```

```python
import functools

import jax
import jax.numpy as jnp
from jax import lax
from jax.experimental import pallas as pl
from jax.experimental.pallas import tpu as pltpu
from jax.sharding import PartitionSpec as P

STEP = 10


beta_one = 0.9
beta_two = 0.95
adam_epsilon = 1e-08
decay_rate = 0.1
clip_level = 1.0
norm_epsilon = 1e-05
rate_matrix = 0.6
rate_attention = 2.4
rate_vector = 0.3
masked_score = -1e30

MESH = pl.DeviceIdType.MESH
IN_PLACE = pl.BlockSpec(memory_space=pl.ANY)
IN_VMEM = pl.BlockSpec(memory_space=pltpu.VMEM)
DMA = pltpu.SemaphoreType.DMA
MIB = 2**20


def mul_plain(left, right):
    return jnp.dot(left, right, preferred_element_type=jnp.float32)


def mul_right_t(left, right):
    return lax.dot_general(
        left, right, (((1,), (1,)), ((), ())), preferred_element_type=jnp.float32
    )


def mul_left_t(left, right):
    return lax.dot_general(
        left, right, (((0,), (0,)), ((), ())), preferred_element_type=jnp.float32
    )


def layer_norm(values, scaling, offset):
    average = jnp.mean(values, axis=-1, keepdims=True)
    centered = values - average
    variance = jnp.mean(centered * centered, axis=-1, keepdims=True)
    return centered * lax.rsqrt(variance + norm_epsilon) * scaling + offset


def gelu_tanh(values):
    return jax.nn.gelu(values, approximate=True)


def exclusive_sum(table, axis_index):
    return jnp.cumsum(table, axis=axis_index) - table


def segment_ids(seq_lengths, row_count):
    position = jnp.arange(row_count, dtype=jnp.int32)
    starts = jnp.cumsum(seq_lengths) - seq_lengths
    segment = jnp.sum((starts[None, :] <= position[:, None]).astype(jnp.int32), axis=1)
    return (segment, position)


def slot_matrix(starts, amounts, slots, row_count):
    offsets = jnp.arange(slots, dtype=jnp.int32)
    picked = jnp.where(offsets[None, :] < amounts[:, None], starts[:, None] + offsets[None, :], -1)
    position = jnp.arange(row_count, dtype=jnp.int32)
    return (picked.reshape(-1)[:, None] == position[None, :]).astype(jnp.bfloat16)


def adamw_step(weight, moment, square, gradient, rate):
    moment_new = beta_one * moment + (1.0 - beta_one) * gradient
    square_new = beta_two * square + (1.0 - beta_two) * gradient * gradient
    moment_hat = moment_new / (1.0 - beta_one**STEP)
    square_hat = square_new / (1.0 - beta_two**STEP)
    weight_new = weight - rate * (
        moment_hat / (jnp.sqrt(square_hat) + adam_epsilon) + decay_rate * weight
    )
    return (weight_new, moment_new, square_new)


def along(place):
    return (lax.axis_index("dp"), place)


def greet_line(t, n):
    barrier = pltpu.get_barrier_semaphore()

    @pl.when(t > 0)
    def _():
        pl.semaphore_signal(barrier, inc=1, device_id=along(t - 1), device_id_type=MESH)

    @pl.when(t < n - 1)
    def _():
        pl.semaphore_signal(barrier, inc=1, device_id=along(t + 1), device_id_type=MESH)

    pl.semaphore_wait(barrier, (t > 0).astype(jnp.int32) + (t < n - 1).astype(jnp.int32))


def greet_all(t, n):
    barrier = pltpu.get_barrier_semaphore()
    for k in range(1, n):
        pl.semaphore_signal(
            barrier, inc=1, device_id=along(lax.rem(t + k, n)), device_id_type=MESH
        )
    pl.semaphore_wait(barrier, n - 1)


class LineGather:
    def __init__(self, t, n, chunks, first, place, sems):
        self.t, self.n, self.chunks, self.first, self.place = t, n, chunks, first, place
        self.sems = sems

    def copy(self, h, c, right):
        b = self.t - h if right else self.t + h
        dst = self.place(b, c)
        src = self.first(c) if h == 0 else dst
        s, r = self.sems[:2] if right else self.sems[2:]
        return pltpu.make_async_remote_copy(
            src,
            dst,
            s.at[h, c],
            r.at[h, c],
            device_id=along(self.t + 1 if right else self.t - 1),
            device_id_type=MESH,
        )

    def sends(self, h, right):
        t, n = self.t, self.n
        return (t >= h) & (t < n - 1) if right else (t + h <= n - 1) & (t > 0)

    def gets(self, h, right):
        return self.t - 1 - h >= 0 if right else self.t + 1 + h <= self.n - 1

    def receive(self, h, c, right):
        b = self.t - 1 - h if right else self.t + 1 + h
        dst = self.place(b, c)
        s, r = self.sems[:2] if right else self.sems[2:]
        pltpu.make_async_remote_copy(
            dst,
            dst,
            s.at[h, c],
            r.at[h, c],
            device_id=along(self.t - 1 if right else self.t + 1),
            device_id_type=MESH,
        ).wait_recv()

    def start(self):
        for c in range(self.chunks):
            for right in (True, False):

                @pl.when(self.sends(0, right))
                def _():
                    self.copy(0, c, right).start()

    def forward(self):
        for h in range(self.n - 1):
            for c in range(self.chunks):
                for right in (True, False):

                    @pl.when(self.gets(h, right))
                    def _():
                        self.receive(h, c, right)

                    if h + 1 < self.n - 1:

                        @pl.when(self.sends(h + 1, right))
                        def _():
                            self.copy(h + 1, c, right).start()

    def finish(self):
        for h in range(self.n - 1):
            for c in range(self.chunks):
                for right in (True, False):

                    @pl.when(self.sends(h, right))
                    def _():
                        self.copy(h, c, right).wait_send()


def gather_sems(n, chunks):
    return [DMA((n - 1, chunks))] * 4


def gather_rows_kernel(n, chunks, x_ref, o_ref, sa, ra, sb, rb, own_sem):
    t = lax.axis_index("tensor")
    rows = x_ref.shape[0]
    step = rows // chunks
    greet_line(t, n)
    job = LineGather(
        t,
        n,
        chunks,
        lambda c: x_ref.at[pl.ds(c * step, step)],
        lambda b, c: o_ref.at[pl.ds(b * rows + c * step, step)],
        (sa, ra, sb, rb),
    )
    job.start()
    own = pltpu.make_async_copy(x_ref, o_ref.at[pl.ds(t * rows, rows)], own_sem)
    own.start()
    job.forward()
    own.wait()
    job.finish()


def gather_rows(x, n, collective_id, chunks=4):
    rows, cols = x.shape
    return pl.pallas_call(
        functools.partial(gather_rows_kernel, n, chunks),
        out_shape=jax.ShapeDtypeStruct((n * rows, cols), x.dtype),
        in_specs=[IN_PLACE],
        out_specs=IN_PLACE,
        scratch_shapes=gather_sems(n, chunks) + [DMA],
        compiler_params=pltpu.CompilerParams(collective_id=collective_id, has_side_effects=True),
        name="gather_rows",
    )(x)


def gather_cols_kernel(n, chunks, count, x_ref, *refs):
    t = lax.axis_index("tensor")
    outs, sems = refs[:count], refs[count:]
    rows = x_ref.shape[0]
    cols = x_ref.shape[1] // count
    step = rows // chunks
    greet_line(t, n)
    jobs, owns = [], []
    for i, o_ref in enumerate(outs):
        jobs.append(
            LineGather(
                t,
                n,
                chunks,
                lambda c, i=i: x_ref.at[pl.ds(c * step, step), pl.ds(i * cols, cols)],
                lambda b, c, o_ref=o_ref: o_ref.at[
                    pl.ds(c * step, step), pl.ds(pl.multiple_of(b * cols, cols), cols)
                ],
                sems[5 * i : 5 * i + 4],
            )
        )
        owns.append(
            pltpu.make_async_copy(
                x_ref.at[:, pl.ds(i * cols, cols)],
                o_ref.at[:, pl.ds(pl.multiple_of(t * cols, cols), cols)],
                sems[5 * i + 4],
            )
        )
    for job, own in zip(jobs, owns):
        job.start()
        own.start()
    for job in jobs:
        job.forward()
    for job, own in zip(jobs, owns):
        own.wait()
        job.finish()


def gather_cols(x, count, n, collective_id, chunks=4):
    rows, cols = x.shape
    shape = jax.ShapeDtypeStruct((rows, n * cols // count), x.dtype)
    return pl.pallas_call(
        functools.partial(gather_cols_kernel, n, chunks, count),
        out_shape=(shape,) * count,
        in_specs=[IN_PLACE],
        out_specs=(IN_PLACE,) * count,
        scratch_shapes=(gather_sems(n, chunks) + [DMA]) * count,
        compiler_params=pltpu.CompilerParams(collective_id=collective_id, has_side_effects=True),
        name="gather_cols",
    )(x)


def split_in_kernel(n, chunks, x_ref, rows_ref, cols_ref, ss, rs, own_s, sa, ra, sb, rb, own_g):
    t = lax.axis_index("tensor")
    total = x_ref.shape[0]
    rows, cols = total // n, x_ref.shape[1] // 2
    step = total // chunks
    greet_all(t, n)
    mine = pl.ds(pl.multiple_of(t * cols, cols), cols)

    def block(p):
        return x_ref.at[pl.ds(p * rows, rows), pl.ds(0, cols)]

    copies = []
    for k in range(1, n):
        p = lax.rem(t + k, n)
        copies.append(
            pltpu.make_async_remote_copy(
                block(p),
                rows_ref.at[:, mine],
                ss.at[k - 1],
                rs.at[k - 1],
                device_id=along(p),
                device_id_type=MESH,
            )
        )
    for copy in copies:
        copy.start()
    owns = [
        pltpu.make_async_copy(block(t), rows_ref.at[:, mine], own_s),
        pltpu.make_async_copy(x_ref.at[:, pl.ds(cols, cols)], cols_ref.at[:, mine], own_g),
    ]
    job = LineGather(
        t,
        n,
        chunks,
        lambda c: x_ref.at[pl.ds(c * step, step), pl.ds(cols, cols)],
        lambda b, c: cols_ref.at[
            pl.ds(c * step, step), pl.ds(pl.multiple_of(b * cols, cols), cols)
        ],
        (sa, ra, sb, rb),
    )
    job.start()
    for own in owns:
        own.start()
    job.forward()
    for own in owns:
        own.wait()
    job.finish()
    for copy in copies:
        copy.wait()


def split_in(x, n, collective_id, chunks=4):
    total, both = x.shape
    cols = both // 2
    return pl.pallas_call(
        functools.partial(split_in_kernel, n, chunks),
        out_shape=(
            jax.ShapeDtypeStruct((total // n, n * cols), x.dtype),
            jax.ShapeDtypeStruct((total, n * cols), x.dtype),
        ),
        in_specs=[IN_PLACE],
        out_specs=(IN_PLACE, IN_PLACE),
        scratch_shapes=[DMA((n - 1,)), DMA((n - 1,)), DMA] + gather_sems(n, chunks) + [DMA],
        compiler_params=pltpu.CompilerParams(collective_id=collective_id, has_side_effects=True),
        name="split_in",
    )(x)


def split_out_kernel(n, count, *refs):
    t = lax.axis_index("tensor")
    xs, o_ref = refs[:count], refs[count]
    sends, receives, own_sems = refs[count + 1 :]
    rows = xs[0].shape[0]
    cols = xs[0].shape[1] // n
    greet_all(t, n)

    def source(i, p):
        return xs[i].at[:, pl.ds(pl.multiple_of(p * cols, cols), cols)]

    def target(i):
        return o_ref.at[pl.ds(t * rows, rows), pl.ds(i * cols, cols)]

    copies = []
    for i in range(count):
        for k in range(1, n):
            p = lax.rem(t + k, n)
            copies.append(
                pltpu.make_async_remote_copy(
                    source(i, p),
                    target(i),
                    sends.at[i, k - 1],
                    receives.at[i, k - 1],
                    device_id=along(p),
                    device_id_type=MESH,
                )
            )
    for copy in copies:
        copy.start()
    owns = [pltpu.make_async_copy(source(i, t), target(i), own_sems.at[i]) for i in range(count)]
    for own in owns:
        own.start()
    for own in owns:
        own.wait()
    for copy in copies:
        copy.wait()


def split_out(xs, n, collective_id):
    count = len(xs)
    rows, cols = xs[0].shape
    return pl.pallas_call(
        functools.partial(split_out_kernel, n, count),
        out_shape=jax.ShapeDtypeStruct((n * rows, count * cols // n), xs[0].dtype),
        in_specs=[IN_PLACE] * count,
        out_specs=IN_PLACE,
        scratch_shapes=[DMA((count, n - 1)), DMA((count, n - 1)), DMA((count,))],
        compiler_params=pltpu.CompilerParams(collective_id=collective_id, has_side_effects=True),
        name="split_out",
    )(*xs)


def scatter_rows_kernel(n, chunks, x_ref, o_ref, from_left, from_right, sa, ra, sb, rb):
    t = lax.axis_index("tensor")
    rows = x_ref.shape[0] // n
    step = rows // chunks
    greet_line(t, n)

    def parts(k, c, right):
        held, s, r = (from_left, sa, ra) if right else (from_right, sb, rb)
        return held.at[k, pl.ds(c * step, step)], s.at[k, c], r.at[k, c]

    def send(k, c, right, first):
        slot, s, r = parts(k, c, right)
        d = n - 1 - k if right else k
        return pltpu.make_async_remote_copy(
            x_ref.at[pl.ds(d * rows + c * step, step)] if first else slot,
            slot,
            s,
            r,
            device_id=along(t + 1 if right else t - 1),
            device_id_type=MESH,
        )

    def receive(k, c, right):
        slot, s, r = parts(k, c, right)
        pltpu.make_async_remote_copy(
            slot,
            slot,
            s,
            r,
            device_id=along(t - 1 if right else t + 1),
            device_id_type=MESH,
        ).wait_recv()

    every = [
        (k, c, right, n - 1 - k if right else k)
        for k in range(n - 1)
        for c in range(chunks)
        for right in (True, False)
    ]
    for k, c, right, d in every:

        @pl.when((t == (0 if right else n - 1)) & (t != d))
        def _():
            send(k, c, right, True).start()

    for k, c, right, d in every:

        @pl.when((t > 0) & (t < d) if right else (t < n - 1) & (t > d))
        def _():
            receive(k, c, right)
            slot = parts(k, c, right)[0]
            mine = x_ref[pl.ds(d * rows + c * step, step)]
            slot[...] = (slot[...].astype(jnp.float32) + mine.astype(jnp.float32)).astype(
                slot.dtype
            )
            send(k, c, right, False).start()

    for k, c, right, d in every:

        @pl.when(t == d)
        def _():
            receive(k, c, right)

    o_ref[...] = x_ref[pl.ds(pl.multiple_of(t * rows, rows), rows)].astype(jnp.float32)

    @pl.when(t > 0)
    def _():
        o_ref[...] += from_left[n - 1 - t].astype(jnp.float32)

    @pl.when(t < n - 1)
    def _():
        o_ref[...] += from_right[t].astype(jnp.float32)

    for k, c, right, d in every:

        @pl.when(t < d if right else t > d)
        def _():
            send(k, c, right, False).wait_send()


def scatter_rows(x, n, collective_id, chunks=4):
    rows, cols = x.shape[0] // n, x.shape[1]
    return pl.pallas_call(
        functools.partial(scatter_rows_kernel, n, chunks),
        out_shape=jax.ShapeDtypeStruct((rows, cols), jnp.float32),
        in_specs=[IN_VMEM],
        out_specs=IN_VMEM,
        scratch_shapes=[pltpu.VMEM((n - 1, rows, cols), x.dtype)] * 2
        + [DMA((n - 1, chunks))] * 4,
        compiler_params=pltpu.CompilerParams(
            collective_id=collective_id, has_side_effects=True, vmem_limit_bytes=40 * MIB
        ),
        name="scatter_rows",
    )(x)


def sum_all_kernel(n_dp, n, x_ref, o_ref, from_z, from_dp, part, s1, r1, s2, r2, s3, r3):
    g, t = lax.axis_index("dp"), lax.axis_index("tensor")
    rows = x_ref.shape[0] // n
    barrier = pltpu.get_barrier_semaphore()
    for k in range(1, n):
        pl.semaphore_signal(
            barrier, inc=1, device_id=(g, lax.rem(t + k, n)), device_id_type=MESH
        )
    for k in range(1, n_dp):
        pl.semaphore_signal(
            barrier, inc=1, device_id=(lax.rem(g + k, n_dp), t), device_id_type=MESH
        )
    pl.semaphore_wait(barrier, n - 1 + n_dp - 1)

    def piece(p):
        return pl.ds(pl.multiple_of(p * rows, rows), rows)

    first = []
    for k in range(1, n):
        p = lax.rem(t + k, n)
        first.append(
            pltpu.make_async_remote_copy(
                x_ref.at[piece(p)],
                from_z.at[k - 1],
                s1.at[k - 1],
                r1.at[k - 1],
                device_id=(g, p),
                device_id_type=MESH,
            )
        )
    for copy in first:
        copy.start()
    for copy in first:
        copy.wait()
    total = x_ref[piece(t)]
    for k in range(1, n):
        total = total + from_z[k - 1]
    part[...] = total
    second = []
    for k in range(1, n_dp):
        second.append(
            pltpu.make_async_remote_copy(
                part,
                from_dp.at[g],
                s2.at[k - 1],
                r2.at[k - 1],
                device_id=(lax.rem(g + k, n_dp), t),
                device_id_type=MESH,
            )
        )
    for copy in second:
        copy.start()
    from_dp[g] = part[...]
    for copy in second:
        copy.wait()
    total = from_dp[0]
    for k in range(1, n_dp):
        total = total + from_dp[k]
    o_ref[piece(t)] = total
    third = []
    for k in range(1, n):
        third.append(
            pltpu.make_async_remote_copy(
                o_ref.at[piece(t)],
                o_ref.at[piece(t)],
                s3.at[k - 1],
                r3.at[k - 1],
                device_id=(g, lax.rem(t + k, n)),
                device_id_type=MESH,
            )
        )
    for copy in third:
        copy.start()
    for copy in third:
        copy.wait()


def sum_all(x, n_dp, n, collective_id):
    rows = x.shape[0] // n
    return pl.pallas_call(
        functools.partial(sum_all_kernel, n_dp, n),
        out_shape=jax.ShapeDtypeStruct(x.shape, x.dtype),
        in_specs=[IN_VMEM],
        out_specs=IN_VMEM,
        scratch_shapes=[
            pltpu.VMEM((n - 1, rows, 128), x.dtype),
            pltpu.VMEM((n_dp, rows, 128), x.dtype),
            pltpu.VMEM((rows, 128), x.dtype),
        ]
        + [DMA((n - 1,))] * 2
        + [DMA((n_dp - 1,))] * 2
        + [DMA((n - 1,))] * 2,
        compiler_params=pltpu.CompilerParams(collective_id=collective_id, has_side_effects=True),
        name="sum_all",
    )(x)


def local(
    tokens,
    cotangent,
    lengths,
    counts,
    query_weight,
    query_moment,
    query_square,
    shared_weight,
    shared_moment,
    shared_square,
    project_weight,
    project_moment,
    project_square,
    expand_weight,
    expand_moment,
    expand_square,
    shrink_weight,
    shrink_moment,
    shrink_square,
    vectors_value,
    vectors_moment,
    vectors_square,
):
    device = lax.axis_index("dp")
    n_dp = lax.axis_size("dp")
    t = lax.axis_index("tensor")
    n = lax.axis_size("tensor")
    row_count, width = tokens.shape
    slots = 2 * row_count // n_dp
    part_rows, part_cols = row_count // n, width // n
    send_start = lax.dynamic_index_in_dim(exclusive_sum(counts, 1), device, 0, keepdims=False)
    send_amount = lax.dynamic_index_in_dim(counts, device, 0, keepdims=False)
    recv_start = lax.dynamic_index_in_dim(exclusive_sum(counts, 0), device, 1, keepdims=False)
    recv_amount = lax.dynamic_index_in_dim(counts, device, 1, keepdims=False)
    send_slots = slot_matrix(send_start, send_amount, slots, row_count)
    recv_slots = slot_matrix(recv_start, recv_amount, slots, row_count)

    def exchange(rows, out_slots, in_slots):
        packed = mul_plain(out_slots, rows).astype(jnp.bfloat16)
        arrived = lax.all_to_all(
            packed.reshape(n_dp, slots, rows.shape[1]), "dp", split_axis=0, concat_axis=0, tiled=True
        )
        return mul_left_t(in_slots, arrived.reshape(n_dp * slots, rows.shape[1])).astype(
            jnp.bfloat16
        )

    query_all = lax.all_gather(
        gather_cols(query_weight.astype(jnp.bfloat16), 1, n, 1, 1)[0], "dp", axis=0, tiled=True
    )
    shared_all = lax.all_gather(
        shared_weight.astype(jnp.bfloat16), ("dp", "tensor"), axis=0, tiled=True
    )
    project_all = lax.all_gather(
        gather_rows(project_weight.astype(jnp.bfloat16), n, 2, 1), "dp", axis=1, tiled=True
    )
    expand_cols = lax.all_gather(expand_weight.astype(jnp.bfloat16), "dp", axis=0, tiled=True)
    shrink_rows = lax.all_gather(shrink_weight.astype(jnp.bfloat16), "dp", axis=1, tiled=True)

    mine_cols = [
        lax.dynamic_slice_in_dim(a, t * part_cols, part_cols, 1) for a in (tokens, cotangent)
    ]
    owned = exchange(jnp.concatenate(mine_cols, axis=1), send_slots, recv_slots)
    owned_rows, owned_grad = split_in(owned, n, 3)

    head_size = shared_all.shape[1] // 2
    heads = width // head_size
    hidden_width = expand_cols.shape[1]
    hidden_total = hidden_width * n
    gain_one = vectors_value[0:width]
    shift_one = vectors_value[width : 2 * width]
    gain_two = vectors_value[2 * width : 3 * width]
    shift_two = vectors_value[3 * width : 4 * width]
    query_bias = vectors_value[4 * width : 5 * width]
    project_bias = vectors_value[5 * width : 6 * width]
    shrink_bias = vectors_value[6 * width : 7 * width]
    expand_bias = lax.dynamic_slice_in_dim(
        vectors_value, 7 * width + t * hidden_width, hidden_width, 0
    )
    value_bias = vectors_value[7 * width + hidden_total : 7 * width + hidden_total + head_size]

    inputs_float = owned_rows.astype(jnp.float32)
    normed_one, norm_one_back = jax.vjp(layer_norm, inputs_float, gain_one, shift_one)
    normed_low = normed_one.astype(jnp.bfloat16)
    queries = (mul_plain(normed_low, query_all) + query_bias).astype(jnp.bfloat16)
    shared_out = mul_plain(normed_low, shared_all) + jnp.concatenate(
        [jnp.zeros((head_size,), jnp.float32), value_bias]
    )
    shared_rows = gather_rows(shared_out.astype(jnp.bfloat16), n, 4, 1)
    key_rows, value_rows = shared_rows[:, :head_size], shared_rows[:, head_size:]
    query_heads = queries.reshape(part_rows, heads, head_size)
    segment, position = segment_ids(lengths[0], row_count)
    my_segment = lax.dynamic_slice_in_dim(segment, t * part_rows, part_rows, 0)
    my_position = lax.dynamic_slice_in_dim(position, t * part_rows, part_rows, 0)
    allowed = (my_segment[:, None] == segment[None, :]) & (
        my_position[:, None] >= position[None, :]
    )
    score_scale = head_size ** (-0.5)

    def masked_scores():
        scores = (
            jnp.einsum("bhd,kd->hbk", query_heads, key_rows, preferred_element_type=jnp.float32)
            * score_scale
        )
        return jnp.where(allowed[None], scores, masked_score)

    scores = masked_scores()
    row_max = jnp.max(scores, axis=-1, keepdims=True)
    expo = jnp.exp(scores - row_max)
    row_total = jnp.sum(expo, axis=-1, keepdims=True)
    probs = expo / row_total
    heads_out = (
        jnp.einsum(
            "hbk,kd->bhd",
            probs.astype(jnp.bfloat16),
            value_rows,
            preferred_element_type=jnp.float32,
        )
        .reshape(part_rows, width)
        .astype(jnp.bfloat16)
    )
    log_total = row_max + jnp.log(row_total)
    hidden_one = inputs_float + (mul_plain(heads_out, project_all) + project_bias)
    normed_two, norm_two_back = jax.vjp(layer_norm, hidden_one, gain_two, shift_two)

    normed_two_low = gather_rows(normed_two.astype(jnp.bfloat16), n, 5)
    expand_pre = mul_plain(normed_two_low, expand_cols) + expand_bias
    activated, gelu_back = jax.vjp(gelu_tanh, expand_pre)
    activated_low = activated.astype(jnp.bfloat16)
    ffn_partial = mul_plain(activated_low, shrink_rows).astype(jnp.bfloat16)
    shrink_grad = mul_left_t(activated_low, owned_grad)
    activated_grad = mul_right_t(owned_grad, shrink_rows)
    expand_pre_grad = gelu_back(activated_grad)[0].astype(jnp.bfloat16)
    expand_grad = mul_left_t(normed_two_low, expand_pre_grad)
    expand_bias_grad = jnp.sum(expand_pre_grad.astype(jnp.float32), axis=0)
    normed_two_part = mul_right_t(expand_pre_grad, expand_cols).astype(jnp.bfloat16)

    normed_two_grad = scatter_rows(normed_two_part, n, 6)
    ffn_branch = scatter_rows(ffn_partial, n, 7) + shrink_bias
    layer_result = (hidden_one + ffn_branch).astype(jnp.bfloat16)
    output_float = lax.dynamic_slice_in_dim(owned_grad, t * part_rows, part_rows, 0).astype(
        jnp.float32
    )
    shrink_bias_grad = jnp.sum(output_float, axis=0)
    hidden_from_norm, gain_two_grad, shift_two_grad = norm_two_back(normed_two_grad)
    hidden_grad = output_float + hidden_from_norm
    branch_grad = hidden_grad.astype(jnp.bfloat16)
    project_bias_grad = jnp.sum(branch_grad.astype(jnp.float32), axis=0)
    project_grad = mul_left_t(heads_out, branch_grad)
    heads_grad = (
        mul_right_t(branch_grad, project_all)
        .astype(jnp.bfloat16)
        .reshape(part_rows, heads, head_size)
    )
    probs = jnp.exp(masked_scores() - log_total)
    prob_grad = jnp.einsum(
        "bhd,kd->hbk", heads_grad, value_rows, preferred_element_type=jnp.float32
    )
    score_grad = (
        probs * (prob_grad - jnp.sum(probs * prob_grad, axis=-1, keepdims=True))
    ).astype(jnp.bfloat16)
    query_grad = (
        (
            jnp.einsum("hbk,kd->bhd", score_grad, key_rows, preferred_element_type=jnp.float32)
            * score_scale
        )
        .reshape(part_rows, width)
        .astype(jnp.bfloat16)
    )
    key_grad = (
        jnp.einsum("hbk,bhd->kd", score_grad, query_heads, preferred_element_type=jnp.float32)
        * score_scale
    )
    value_grad = jnp.einsum(
        "hbk,bhd->kd",
        probs.astype(jnp.bfloat16),
        heads_grad,
        preferred_element_type=jnp.float32,
    )
    shared_grad = scatter_rows(
        jnp.concatenate([key_grad, value_grad], axis=1).astype(jnp.bfloat16), n, 8, 1
    ).astype(jnp.bfloat16)
    query_bias_grad = jnp.sum(query_grad.astype(jnp.float32), axis=0)
    query_weight_grad = mul_left_t(normed_low, query_grad)
    normed_one_grad = mul_right_t(query_grad, query_all) + mul_right_t(shared_grad, shared_all)
    inputs_from_norm, gain_one_grad, shift_one_grad = norm_one_back(normed_one_grad)
    input_result = (hidden_grad + inputs_from_norm).astype(jnp.bfloat16)
    shared_weight_grad = mul_left_t(normed_low, shared_grad)
    value_bias_grad = jnp.sum(shared_grad[:, head_size:].astype(jnp.float32), axis=0)

    back = exchange(split_out((layer_result, input_result), n, 9), recv_slots, send_slots)
    output_rows, grad_rows = gather_cols(back, 2, n, 10)
    output_back = output_rows.astype(jnp.float32)
    token_rms = jnp.sqrt(jnp.mean(output_back * output_back, axis=1))

    def over_dp(partial, dimension):
        return lax.psum_scatter(
            partial.astype(jnp.bfloat16), "dp", scatter_dimension=dimension, tiled=True
        )

    def over_tensor(partial, dimension):
        return lax.psum_scatter(partial, "tensor", scatter_dimension=dimension, tiled=True).astype(
            jnp.float32
        )

    expand_part = over_dp(expand_grad, 0).astype(jnp.float32)
    shrink_part = over_dp(shrink_grad, 1).astype(jnp.float32)
    query_part = over_tensor(over_dp(query_weight_grad, 0), 1)
    project_part = over_tensor(over_dp(project_grad, 1), 0)
    shared_piece = over_tensor(over_dp(shared_weight_grad, 0), 0)
    split_part = lax.dynamic_update_slice_in_dim(
        jnp.zeros((hidden_total,), jnp.float32), expand_bias_grad, t * hidden_width, 0
    )
    vector_part = jnp.concatenate(
        [
            gain_one_grad,
            shift_one_grad,
            gain_two_grad,
            shift_two_grad,
            query_bias_grad,
            project_bias_grad,
            shrink_bias_grad,
            split_part,
            value_bias_grad,
        ]
    )
    local_squares = (
        jnp.sum(query_part * query_part)
        + jnp.sum(expand_part * expand_part)
        + jnp.sum(shared_piece * shared_piece)
        + jnp.sum(project_part * project_part)
        + jnp.sum(shrink_part * shrink_part)
    )
    length = vector_part.shape[0]
    unit = n * 8 * 128
    padded = -(-(length + 1) // unit) * unit
    everything = jnp.concatenate(
        [vector_part, local_squares[None], jnp.zeros((padded - length - 1,), jnp.float32)]
    )
    summed = sum_all(everything.reshape(padded // 128, 128), n_dp, n, 11).reshape(padded)
    vector_grad, weight_squares = summed[:length], summed[length]
    grad_size = jnp.sqrt(weight_squares + jnp.sum(vector_grad * vector_grad))
    clip_factor = jnp.minimum(1.0, clip_level / (grad_size + 1e-06))
    clipped_vectors = clip_factor * vector_grad
    query_new = adamw_step(
        query_weight,
        query_moment,
        query_square,
        clip_factor * query_part,
        rate_matrix * width ** (-0.5),
    )
    shared_new = adamw_step(
        shared_weight,
        shared_moment,
        shared_square,
        clip_factor * shared_piece,
        rate_attention * width ** (-0.5),
    )
    project_new = adamw_step(
        project_weight,
        project_moment,
        project_square,
        clip_factor * project_part,
        rate_attention * width ** (-0.5),
    )
    expand_new = adamw_step(
        expand_weight,
        expand_moment,
        expand_square,
        clip_factor * expand_part,
        rate_matrix * width ** (-0.5),
    )
    shrink_new = adamw_step(
        shrink_weight,
        shrink_moment,
        shrink_square,
        clip_factor * shrink_part,
        rate_matrix * hidden_total ** (-0.5),
    )
    vectors_new = adamw_step(
        vectors_value, vectors_moment, vectors_square, clipped_vectors, rate_vector
    )
    return (
        output_rows,
        grad_rows,
        grad_size,
        *query_new,
        *shared_new,
        *project_new,
        *expand_new,
        *shrink_new,
        *vectors_new,
        clipped_vectors,
        token_rms,
    )


def solution(mesh):
    by_rows = P("dp", None)
    query = P("dp", "tensor")
    shared = P(("dp", "tensor"), None)
    project = P("tensor", "dp")
    return jax.shard_map(
        local,
        mesh=mesh,
        in_specs=(
            *(by_rows,) * 3,
            P(),
            *(query,) * 3,
            *(shared,) * 3,
            *(project,) * 3,
            *(query,) * 3,
            *(project,) * 3,
            *(P(),) * 3,
        ),
        out_specs=(
            *(by_rows,) * 2,
            P(),
            *(query,) * 3,
            *(shared,) * 3,
            *(project,) * 3,
            *(query,) * 3,
            *(project,) * 3,
            *(P(),) * 4,
            P("dp"),
        ),
        check_vma=False,
    )
```

```python
import functools

import jax
import jax.numpy as jnp
from jax import lax
from jax.experimental import pallas as pl
from jax.experimental.pallas import tpu as pltpu
from jax.sharding import PartitionSpec as P

STEP = 10


beta_one = 0.9
beta_two = 0.95
adam_epsilon = 1e-08
decay_rate = 0.1
clip_level = 1.0
norm_epsilon = 1e-05
rate_matrix = 0.6
rate_attention = 2.4
rate_vector = 0.3
masked_score = -1e30

MESH = pl.DeviceIdType.MESH
IN_PLACE = pl.BlockSpec(memory_space=pl.ANY)
IN_VMEM = pl.BlockSpec(memory_space=pltpu.VMEM)
DMA = pltpu.SemaphoreType.DMA
MIB = 2**20


def mul_plain(left, right):
    return jnp.dot(left, right, preferred_element_type=jnp.float32)


def mul_right_t(left, right):
    return lax.dot_general(
        left, right, (((1,), (1,)), ((), ())), preferred_element_type=jnp.float32
    )


def mul_left_t(left, right):
    return lax.dot_general(
        left, right, (((0,), (0,)), ((), ())), preferred_element_type=jnp.float32
    )


def layer_norm(values, scaling, offset):
    average = jnp.mean(values, axis=-1, keepdims=True)
    centered = values - average
    variance = jnp.mean(centered * centered, axis=-1, keepdims=True)
    return centered * lax.rsqrt(variance + norm_epsilon) * scaling + offset


def gelu_tanh(values):
    return jax.nn.gelu(values, approximate=True)


def exclusive_sum(table, axis_index):
    return jnp.cumsum(table, axis=axis_index) - table


def segment_ids(seq_lengths, row_count):
    position = jnp.arange(row_count, dtype=jnp.int32)
    starts = jnp.cumsum(seq_lengths) - seq_lengths
    segment = jnp.sum((starts[None, :] <= position[:, None]).astype(jnp.int32), axis=1)
    return (segment, position)


def slot_matrix(starts, amounts, slots, row_count):
    offsets = jnp.arange(slots, dtype=jnp.int32)
    picked = jnp.where(offsets[None, :] < amounts[:, None], starts[:, None] + offsets[None, :], -1)
    position = jnp.arange(row_count, dtype=jnp.int32)
    return (picked.reshape(-1)[:, None] == position[None, :]).astype(jnp.bfloat16)


def adamw_step(weight, moment, square, gradient, rate):
    moment_new = beta_one * moment + (1.0 - beta_one) * gradient
    square_new = beta_two * square + (1.0 - beta_two) * gradient * gradient
    moment_hat = moment_new / (1.0 - beta_one**STEP)
    square_hat = square_new / (1.0 - beta_two**STEP)
    weight_new = weight - rate * (
        moment_hat / (jnp.sqrt(square_hat) + adam_epsilon) + decay_rate * weight
    )
    return (weight_new, moment_new, square_new)


def remote(src, dst, send_sem, recv_sem, device):
    return pltpu.make_async_remote_copy(
        src, dst, send_sem, recv_sem, device_id=device, device_id_type=MESH
    )


class Place:
    def __init__(self, n_dp, n):
        self.n, self.chips = n, n_dp // 2
        self.dp, self.t = lax.axis_index("dp"), lax.axis_index("tensor")
        self.core, chip = lax.rem(self.dp, 2), lax.div(self.dp, 2)
        side = round(self.chips**0.5)
        self.side = side if side * side == self.chips else self.chips
        self.pos = self.snake(chip)
        self.sign = 2 * self.core - 1
        self.sibling = (self.dp + 1 - 2 * self.core, self.t)
        self.after = (self.block(self.ring(self.pos - self.sign), self.core), self.t)
        self.before = (self.block(self.ring(self.pos + self.sign), self.core), self.t)
        self.left, self.right = (self.dp, self.t - 1), (self.dp, self.t + 1)

    def snake(self, index):
        row, col = lax.div(index, self.side), lax.rem(index, self.side)
        odd = lax.rem(row, 2)
        return row * self.side + col + odd * (self.side - 1 - 2 * col)

    def ring(self, pos):
        return lax.rem(pos + 2 * self.chips, self.chips)

    def block(self, pos, core):
        return self.snake(pos) * 2 + core

    def behind(self, steps, core):
        return self.block(self.ring(self.pos + (2 * core - 1) * steps), core)

    def greet(self, line=False, line_all=False, ring=False):
        barrier = pltpu.get_barrier_semaphore()
        peers = 0

        def call(device):
            pl.semaphore_signal(barrier, inc=1, device_id=device, device_id_type=MESH)

        if ring:
            for device in (self.sibling, self.after, self.before):
                call(device)
            peers += 3
        if line_all:
            for k in range(1, self.n):
                call((self.dp, lax.rem(self.t + k, self.n)))
            peers += self.n - 1
        elif line:
            pl.when(self.t > 0)(lambda: call(self.left))
            pl.when(self.t < self.n - 1)(lambda: call(self.right))
            peers += (self.t > 0).astype(jnp.int32) + (self.t < self.n - 1).astype(jnp.int32)
        pl.semaphore_wait(barrier, peers)


class LineGather:
    @staticmethod
    def sems(n, chunks):
        return [DMA((n - 1, chunks))] * 4 + [DMA]

    def __init__(self, at, chunks, first, place, sems, whole, unit=1.0):
        self.unit = unit
        self.at, self.chunks, self.first, self.place, self.sems = at, chunks, first, place, sems
        self.own = pltpu.make_async_copy(whole[0], whole[1], sems[4])

    def copy(self, h, c, right):
        at = self.at
        dst = self.place(at.t - h if right else at.t + h, c)
        src = self.first(c) if h == 0 else dst
        s, r = self.sems[0:2] if right else self.sems[2:4]
        return remote(src, dst, s.at[h, c], r.at[h, c], at.right if right else at.left)

    def receive(self, h, c, right):
        at = self.at
        dst = self.place(at.t - 1 - h if right else at.t + 1 + h, c)
        s, r = self.sems[0:2] if right else self.sems[2:4]
        remote(dst, dst, s.at[h, c], r.at[h, c], at.left if right else at.right).wait_recv()

    def sends(self, h, right):
        t, n = self.at.t, self.at.n
        return (t >= h) & (t < n - 1) if right else (t + h <= n - 1) & (t > 0)

    def gets(self, h, right):
        return self.at.t - 1 - h >= 0 if right else self.at.t + 1 + h <= self.at.n - 1

    def every(self):
        for h in range(self.at.n - 1):
            for c in range(self.chunks):
                for right in (True, False):
                    yield h, c, right

    def start(self):
        for h, c, right in self.every():
            if h == 0:
                pl.when(self.sends(h, right))(lambda: self.copy(h, c, right).start())
        self.own.start()

    def step(self, h, c, right):
        pl.when(self.gets(h, right))(lambda: self.receive(h, c, right))
        if h + 1 < self.at.n - 1:
            pl.when(self.sends(h + 1, right))(lambda: self.copy(h + 1, c, right).start())

    def steps(self):
        return [
            (self.unit * (which[0] + (which[1] + 1) / self.chunks), functools.partial(self.step, *which))
            for which in self.every()
        ]

    def finish(self):
        self.own.wait()
        for h, c, right in self.every():
            pl.when(self.sends(h, right))(lambda: self.copy(h, c, right).wait_send())


class LineScatter:
    @staticmethod
    def scratch(n, chunks, block, dtype):
        return [pltpu.VMEM((n - 1, *block), dtype)] * 2 + [DMA((n - 1, chunks))] * 4

    def __init__(self, at, chunks, own, out, scratch, unit=1.0):
        self.unit = unit
        self.at, self.chunks, self.own, self.out = at, chunks, own, out
        self.held, self.sems = scratch[:2], scratch[2:6]
        self.rows = self.held[0].shape[1] // chunks

    def parts(self, k, c, right):
        side = 0 if right else 1
        s, r = self.sems[2 * side : 2 * side + 2]
        return self.held[side].at[k, pl.ds(c * self.rows, self.rows)], s.at[k, c], r.at[k, c]

    def send(self, k, c, right, first):
        slot, s, r = self.parts(k, c, right)
        src = self.own(self.target(k, right), c) if first else slot
        return remote(src, slot, s, r, self.at.right if right else self.at.left)

    def receive(self, k, c, right):
        slot, s, r = self.parts(k, c, right)
        remote(slot, slot, s, r, self.at.left if right else self.at.right).wait_recv()

    def target(self, k, right):
        return self.at.n - 1 - k if right else k

    def every(self):
        for k in range(self.at.n - 1):
            for c in range(self.chunks):
                for right in (True, False):
                    yield k, c, right

    def start(self):
        t, n = self.at.t, self.at.n
        for k, c, right in self.every():
            first = (t == (0 if right else n - 1)) & (t != self.target(k, right))
            pl.when(first)(lambda: self.send(k, c, right, True).start())

    def add(self, k, c, right):
        self.receive(k, c, right)
        slot = self.parts(k, c, right)[0]
        mine = self.own(self.target(k, right), c)[...]
        slot[...] = (slot[...].astype(jnp.float32) + mine.astype(jnp.float32)).astype(slot.dtype)
        self.send(k, c, right, False).start()

    def step(self, k, c, right):
        t, n, d = self.at.t, self.at.n, self.target(k, right)
        passes = (t > 0) & (t < d) if right else (t < n - 1) & (t > d)
        pl.when(passes)(lambda: self.add(k, c, right))

    def steps(self):
        return [
            (self.unit * (which[0] + (which[1] + 1) / self.chunks), functools.partial(self.step, *which))
            for which in self.every()
        ]

    def finish(self):
        t, n = self.at.t, self.at.n
        for k, c, right in self.every():
            pl.when(t == self.target(k, right))(lambda: self.receive(k, c, right))
        for c in range(self.chunks):
            span = pl.ds(c * self.rows, self.rows)
            self.out[span] = self.own(t, c)[...].astype(self.out.dtype)

        def more(block):
            self.out[...] += block[...].astype(self.out.dtype)

        pl.when(t > 0)(lambda: more(self.held[0].at[n - 1 - t]))
        pl.when(t < n - 1)(lambda: more(self.held[1].at[t]))
        for k, c, right in self.every():
            d = self.target(k, right)
            pl.when(t < d if right else t > d)(lambda: self.send(k, c, right, False).wait_send())


class RingGather:
    @staticmethod
    def sems(chips, chunks):
        return [DMA((chips - 1, chunks))] * 2 + [DMA((chips, chunks))] * 2 + [DMA]

    def __init__(self, at, chunks, first, place, sems, whole, unit=1.0):
        self.unit = unit
        self.at, self.chunks, self.first, self.place, self.sems = at, chunks, first, place, sems
        self.own = pltpu.make_async_copy(whole[0], whole[1], sems[4])

    def held(self, h, c):
        return self.place(self.at.behind(h, self.at.core), c)

    def onward(self, h, c):
        src = self.first(c) if h == 0 else self.held(h, c)
        s, r = self.sems[0:2]
        return remote(src, self.held(h, c), s.at[h, c], r.at[h, c], self.at.after)

    def across(self, h, c):
        src = self.first(c) if h == 0 else self.held(h, c)
        s, r = self.sems[2:4]
        return remote(src, self.held(h, c), s.at[h, c], r.at[h, c], self.at.sibling)

    def start(self):
        for c in range(self.chunks):
            self.onward(0, c).start()
        for c in range(self.chunks):
            self.across(0, c).start()
        self.own.start()

    def step(self, h, c):
        dst = self.held(h + 1, c)
        s, r = self.sems[0:2]
        remote(dst, dst, s.at[h, c], r.at[h, c], self.at.before).wait_recv()
        if h + 1 < self.at.chips - 1:
            self.onward(h + 1, c).start()
        self.across(h + 1, c).start()

    def steps(self):
        return [
            (self.unit * (h + (c + 1) / self.chunks), functools.partial(self.step, h, c))
            for h in range(self.at.chips - 1)
            for c in range(self.chunks)
        ]

    def finish(self):
        self.own.wait()
        s, r = self.sems[2:4]
        for h in range(self.at.chips):
            for c in range(self.chunks):
                dst = self.place(self.at.behind(h, 1 - self.at.core), c)
                remote(dst, dst, s.at[h, c], r.at[h, c], self.at.sibling).wait_recv()
                self.across(h, c).wait_send()
                if h < self.at.chips - 1:
                    self.onward(h, c).wait_send()


class RingScatter:
    @staticmethod
    def scratch(chips, chunks, block, dtype):
        return (
            [pltpu.VMEM((chips, *block), dtype)] * 2
            + [pltpu.VMEM((chips - 1, *block), dtype)]
            + [DMA((chips, chunks))] * 3
            + [DMA((chips - 1, chunks))] * 2
        )

    def __init__(self, at, chunks, source, out, scratch, unit=1.0):
        self.unit = unit
        self.at, self.chunks, self.source, self.out = at, chunks, source, out
        self.mine, self.other, self.held = scratch[:3]
        self.load_sem, self.s1, self.r1, self.s2, self.r2 = scratch[3:8]
        self.rows = self.held.shape[1] // chunks

    def span(self, c):
        return pl.ds(c * self.rows, self.rows)

    def target(self, s, core):
        return self.at.behind(s + 1, core)

    def load(self, s, c):
        src = self.source(self.target(s, self.at.core), c)
        return pltpu.make_async_copy(src, self.mine.at[s, self.span(c)], self.load_sem.at[s, c])

    def across(self, s, c):
        src = self.source(self.target(s, 1 - self.at.core), c)
        dst = self.other.at[s, self.span(c)]
        return remote(src, dst, self.s1.at[s, c], self.r1.at[s, c], self.at.sibling)

    def onward(self, s, c):
        src, dst = self.mine.at[s, self.span(c)], self.held.at[s, self.span(c)]
        return remote(src, dst, self.s2.at[s, c], self.r2.at[s, c], self.at.after)

    def every(self):
        return [(s, c) for s in range(self.at.chips) for c in range(self.chunks)]

    def start(self):
        for s, c in self.every():
            self.across(s, c).start()
            self.load(s, c).start()

    def step(self, s, c):
        self.load(s, c).wait()
        self.across(s, c).wait_recv()
        total = self.mine[s, self.span(c)].astype(jnp.float32)
        total += self.other[s, self.span(c)].astype(jnp.float32)
        if s > 0:
            dst = self.held.at[s - 1, self.span(c)]
            remote(
                dst, dst, self.s2.at[s - 1, c], self.r2.at[s - 1, c], self.at.before
            ).wait_recv()
            total += self.held[s - 1, self.span(c)].astype(jnp.float32)
        if s < self.at.chips - 1:
            self.mine[s, self.span(c)] = total.astype(self.mine.dtype)
            self.onward(s, c).start()
        else:
            self.out[self.span(c)] = total.astype(self.out.dtype)

    def steps(self):
        return [
            (self.unit * (max(s - 1, -0.5) + (c + 1) / self.chunks), functools.partial(self.step, s, c))
            for s, c in self.every()
        ]

    def finish(self):
        for s, c in self.every():
            self.across(s, c).wait_send()
            if s < self.at.chips - 1:
                self.onward(s, c).wait_send()


class LineSwitch:
    @staticmethod
    def sems(n):
        return [DMA((n - 1,))] * 2 + [DMA]

    def __init__(self, at, source, target, sems):
        self.own = pltpu.make_async_copy(source(at.t), target, sems[2])
        self.copies = []
        for k in range(1, at.n):
            p = lax.rem(at.t + k, at.n)
            self.copies.append(
                remote(source(p), target, sems[0].at[k - 1], sems[1].at[k - 1], (at.dp, p))
            )

    def start(self):
        for copy in self.copies:
            copy.start()
        self.own.start()

    def steps(self):
        return []

    def finish(self):
        self.own.wait()
        for copy in self.copies:
            copy.wait()


def run_jobs(jobs):
    for job in jobs:
        job.start()
    ordered = []
    for i, job in enumerate(jobs):
        ordered += [(when, i, j, step) for j, (when, step) in enumerate(job.steps())]
    for _, _, _, step in sorted(ordered, key=lambda entry: entry[:3]):
        step()
    for job in jobs:
        job.finish()


def rows_of(ref, step):
    return lambda c: ref.at[pl.ds(c * step, step)]


def lanes(index, count):
    return pl.ds(pl.multiple_of(index * count, count), count)


def move(kernel, inputs, in_vmem, outs, out_vmem, scratch, collective_id, name):
    return pl.pallas_call(
        kernel,
        out_shape=tuple(outs),
        in_specs=[IN_VMEM if i < in_vmem else IN_PLACE for i in range(len(inputs))],
        out_specs=tuple(IN_VMEM if i < out_vmem else IN_PLACE for i in range(len(outs))),
        scratch_shapes=scratch,
        compiler_params=pltpu.CompilerParams(
            collective_id=collective_id, has_side_effects=True, vmem_limit_bytes=56 * MIB
        ),
        name=name,
    )(*inputs)


def line_gather(at, x, out, axis, chunks, sems, unit=1.0):
    rows, cols = x.shape
    step = rows // chunks
    if axis == 0:
        place = lambda b, c: out.at[pl.ds(b * rows + c * step, step)]
        whole = out.at[pl.ds(at.t * rows, rows)]
    else:
        place = lambda b, c: out.at[pl.ds(c * step, step), lanes(b, cols)]
        whole = out.at[:, lanes(at.t, cols)]
    return LineGather(at, chunks, rows_of(x, step), place, sems, (x, whole), unit)


def ring_gather(at, x, out, axis, chunks, sems, unit=1.0):
    rows, cols = x.shape
    step = rows // chunks
    if axis == 0:
        place = lambda b, c: out.at[pl.ds(b * rows + c * step, step)]
        whole = out.at[pl.ds(at.dp * rows, rows)]
    else:
        place = lambda b, c: out.at[pl.ds(c * step, step), lanes(b, cols)]
        whole = out.at[:, lanes(at.dp, cols)]
    return RingGather(at, chunks, rows_of(x, step), place, sems, (x, whole), unit)


def blocks_of(x, out, axis, chunks):
    rows, cols = out.shape
    step = rows // chunks
    if axis == 0:
        return lambda b, c: x.at[pl.ds(pl.multiple_of(b * rows + c * step, step), step)]
    return lambda b, c: x.at[pl.ds(c * step, step), lanes(b, cols)]


def line_scatter(at, x, out, axis, chunks, scratch, unit=1.0):
    return LineScatter(at, chunks, blocks_of(x, out, axis, chunks), out, scratch, unit)


def ring_scatter(at, x, out, axis, chunks, scratch, unit=1.0):
    return RingScatter(at, chunks, blocks_of(x, out, axis, chunks), out, scratch, unit)


def like(x, rows, cols, dtype=None):
    return jax.ShapeDtypeStruct((x.shape[0] * rows, x.shape[1] * cols), dtype or x.dtype)


def fold(x, parts):
    rows, cols = x.shape[0], x.shape[1] // parts
    if cols % 128 == 0:
        return x, 1
    return x.reshape(rows, parts, cols).swapaxes(0, 1).reshape(parts * rows * cols // 128, 128), 0


def unfold(x, rows, parts):
    if x.shape[0] == rows:
        return x
    cols = x.size // rows // parts
    return x.reshape(parts, rows, cols).swapaxes(0, 1).reshape(rows, parts * cols)


def like_over(x, parts, axis):
    return like(x, parts, 1) if axis == 0 else like(x, 1, parts)


def part_of(x, parts, axis):
    return (x.shape[0] // parts, x.shape[1]) if axis == 0 else (x.shape[0], x.shape[1] // parts)


def gather_lines(n_dp, n, query, shared):
    def kernel(a, b, a_out, b_out, *sems):
        at = Place(n_dp, n)
        at.greet(line=True)
        run_jobs(
            [
                line_gather(at, a, a_out, 1, 1, sems[0:5]),
                line_gather(at, b, b_out, 0, 1, sems[5:10]),
            ]
        )

    return move(
        kernel,
        (query, shared),
        0,
        (like(query, 1, n), like(shared, n, 1)),
        0,
        LineGather.sems(n, 1) * 2,
        1,
        "gather_lines",
    )


def rows_and_weights(n_dp, n, owned, project, query, shared):
    chips, chunks = n_dp // 2, 2
    total, cols = owned.shape
    rows = total // n

    def kernel(x, p, a, b, x_out, p_out, a_out, b_out, *sems):
        at = Place(n_dp, n)
        at.greet(line_all=True, ring=True)
        run_jobs(
            [
                LineSwitch(
                    at,
                    lambda p: x.at[pl.ds(pl.multiple_of(p * rows, rows), rows)],
                    x_out.at[:, lanes(at.t, cols)],
                    sems[0:3],
                ),
                ring_gather(at, a, a_out, 0, chunks, sems[3:8], 11.0),
                ring_gather(at, b, b_out, 0, 1, sems[8:13], 11.0),
                line_gather(at, p, p_out, 0, 1, sems[13:18], 12.0),
            ]
        )

    return move(
        kernel,
        (owned, project, query, shared),
        0,
        (
            jax.ShapeDtypeStruct((rows, n * cols), owned.dtype),
            like(project, n, 1),
            like(query, n_dp, 1),
            like(shared, n_dp, 1),
        ),
        0,
        LineSwitch.sems(n)
        + RingGather.sems(chips, chunks)
        + RingGather.sems(chips, 1)
        + LineGather.sems(n, 1),
        2,
        "rows_and_weights",
    )


def shared_and_project(n_dp, n, shared_rows, project):
    chips, chunks = n_dp // 2, 2
    tall = project.shape[0]
    project, axis = fold(project, 1)

    def kernel(x, a, x_out, a_out, *sems):
        at = Place(n_dp, n)
        at.greet(line=True, ring=True)
        run_jobs(
            [
                line_gather(at, x, x_out, 0, 1, sems[0:5], 4.0),
                ring_gather(at, a, a_out, axis, chunks, sems[5:10], 11.0),
            ]
        )

    rows, full = move(
        kernel,
        (shared_rows, project),
        0,
        (like(shared_rows, n, 1), like_over(project, n_dp, axis)),
        0,
        LineGather.sems(n, 1) + RingGather.sems(chips, chunks),
        3,
        "shared_and_project",
    )
    return rows, unfold(full, tall, n_dp)


def rows_and_expanded(n_dp, n, x, expand, shrink):
    chips, chunks, halves = n_dp // 2, 4, 2
    tall = shrink.shape[0]
    shrink, axis = fold(shrink, 1)

    def kernel(x_ref, a, b, x_out, a_out, b_out, *sems):
        at = Place(n_dp, n)
        at.greet(line=True, ring=True)
        run_jobs(
            [
                line_gather(at, x_ref, x_out, 0, chunks, sems[0:5], 22.0),
                ring_gather(at, a, a_out, 0, halves, sems[5:10], 22.0),
                ring_gather(at, b, b_out, axis, halves, sems[10:15], 22.0),
            ]
        )

    rows, expand_full, shrink_full = move(
        kernel,
        (x, expand, shrink),
        0,
        (like(x, n, 1), like(expand, n_dp, 1), like_over(shrink, n_dp, axis)),
        0,
        LineGather.sems(n, chunks) + RingGather.sems(chips, halves) * 2,
        4,
        "rows_and_expanded",
    )
    return rows, expand_full, unfold(shrink_full, tall, n_dp)


def scatter_expanded(n_dp, n, x, expand, shrink):
    chips, chunks = n_dp // 2, 4
    block = (x.shape[0] // n, x.shape[1])
    tall = shrink.shape[0]
    shrink, axis = fold(shrink, n_dp)
    a_block = (expand.shape[0] // n_dp, expand.shape[1])
    b_block = part_of(shrink, n_dp, axis)

    def kernel(x_ref, a, b, x_out, a_out, b_out, *scratch):
        at = Place(n_dp, n)
        at.greet(line=True, ring=True)
        run_jobs(
            [
                line_scatter(at, x_ref, x_out, 0, chunks, scratch[0:6], 20.0),
                ring_scatter(at, a, a_out, 0, chunks, scratch[6:14], 24.0),
                ring_scatter(at, b, b_out, axis, chunks, scratch[14:22], 24.0),
            ]
        )

    rows, expand_part, shrink_part = move(
        kernel,
        (x, expand, shrink),
        1,
        [jax.ShapeDtypeStruct(shape, jnp.float32) for shape in (block, a_block, b_block)],
        3,
        LineScatter.scratch(n, chunks, block, x.dtype)
        + RingScatter.scratch(chips, chunks, a_block, x.dtype)
        + RingScatter.scratch(chips, chunks, b_block, x.dtype),
        5,
        "scatter_expanded",
    )
    return rows, expand_part, shrink_part.reshape(tall, -1)


def scatter_shared(n_dp, n, x, project):
    chips, chunks = n_dp // 2, 4
    block = (x.shape[0] // n, x.shape[1])
    tall = project.shape[0]
    project, axis = fold(project, n_dp)
    a_block = part_of(project, n_dp, axis)

    def kernel(x_ref, a, x_out, a_out, *scratch):
        at = Place(n_dp, n)
        at.greet(line=True, ring=True)
        run_jobs(
            [
                line_scatter(at, x_ref, x_out, 0, 1, scratch[0:6], 4.0),
                ring_scatter(at, a, a_out, axis, chunks, scratch[6:14], 11.0),
            ]
        )

    rows, part = move(
        kernel,
        (x, project),
        1,
        (jax.ShapeDtypeStruct(block, jnp.float32), jax.ShapeDtypeStruct(a_block, x.dtype)),
        2,
        LineScatter.scratch(n, 1, block, x.dtype)
        + RingScatter.scratch(chips, chunks, a_block, x.dtype),
        6,
        "scatter_shared",
    )
    return rows, part.reshape(tall, -1)


def cols_and_grads(n_dp, n, rows, project, query, shared):
    chips, chunks = n_dp // 2, 4
    count, width = rows.shape
    cols = width // n
    p_block = (project.shape[0] // n, project.shape[1])
    a_block = (query.shape[0] // n_dp, query.shape[1])
    b_block = (shared.shape[0] // n_dp, shared.shape[1])

    def kernel(p, x, a, b, p_out, a_out, b_out, x_out, *scratch):
        at = Place(n_dp, n)
        at.greet(line_all=True, ring=True)
        run_jobs(
            [
                LineSwitch(
                    at,
                    lambda p: x.at[:, lanes(p, cols)],
                    x_out.at[pl.ds(at.t * count, count)],
                    scratch[0:3],
                ),
                line_scatter(at, p, p_out, 0, 1, scratch[3:9], 12.0),
                ring_scatter(at, a, a_out, 0, chunks, scratch[9:17], 11.0),
                ring_scatter(at, b, b_out, 0, 1, scratch[17:25], 11.0),
            ]
        )

    return move(
        kernel,
        (project, rows, query, shared),
        1,
        [
            jax.ShapeDtypeStruct(p_block, jnp.float32),
            jax.ShapeDtypeStruct(a_block, query.dtype),
            jax.ShapeDtypeStruct(b_block, query.dtype),
            jax.ShapeDtypeStruct((n * count, cols), rows.dtype),
        ],
        3,
        LineSwitch.sems(n)
        + LineScatter.scratch(n, 1, p_block, project.dtype)
        + RingScatter.scratch(chips, chunks, a_block, query.dtype)
        + RingScatter.scratch(chips, 1, b_block, query.dtype),
        7,
        "cols_and_grads",
    )


def scatter_grads(n_dp, n, query, shared):
    a_block = (query.shape[0], query.shape[1] // n)
    b_block = (shared.shape[0] // n, shared.shape[1])

    def kernel(a, b, a_out, b_out, *scratch):
        at = Place(n_dp, n)
        at.greet(line=True)
        run_jobs(
            [
                line_scatter(at, a, a_out, 1, 1, scratch[0:6]),
                line_scatter(at, b, b_out, 0, 1, scratch[6:12]),
            ]
        )

    return move(
        kernel,
        (query, shared),
        2,
        [jax.ShapeDtypeStruct(block, jnp.float32) for block in (a_block, b_block)],
        2,
        LineScatter.scratch(n, 1, a_block, query.dtype)
        + LineScatter.scratch(n, 1, b_block, query.dtype),
        8,
        "scatter_grads",
    )


def sum_all_kernel(n_dp, n, x_ref, o_ref, from_z, from_dp, part, s1, r1, s2, r2, s3, r3):
    g, t = lax.axis_index("dp"), lax.axis_index("tensor")
    rows = x_ref.shape[0] // n
    barrier = pltpu.get_barrier_semaphore()
    for k in range(1, n):
        pl.semaphore_signal(
            barrier, inc=1, device_id=(g, lax.rem(t + k, n)), device_id_type=MESH
        )
    for k in range(1, n_dp):
        pl.semaphore_signal(
            barrier, inc=1, device_id=(lax.rem(g + k, n_dp), t), device_id_type=MESH
        )
    pl.semaphore_wait(barrier, n - 1 + n_dp - 1)

    def piece(p):
        return pl.ds(pl.multiple_of(p * rows, rows), rows)

    first = []
    for k in range(1, n):
        p = lax.rem(t + k, n)
        first.append(
            pltpu.make_async_remote_copy(
                x_ref.at[piece(p)],
                from_z.at[k - 1],
                s1.at[k - 1],
                r1.at[k - 1],
                device_id=(g, p),
                device_id_type=MESH,
            )
        )
    for copy in first:
        copy.start()
    for copy in first:
        copy.wait()
    total = x_ref[piece(t)]
    for k in range(1, n):
        total = total + from_z[k - 1]
    part[...] = total
    second = []
    for k in range(1, n_dp):
        second.append(
            pltpu.make_async_remote_copy(
                part,
                from_dp.at[g],
                s2.at[k - 1],
                r2.at[k - 1],
                device_id=(lax.rem(g + k, n_dp), t),
                device_id_type=MESH,
            )
        )
    for copy in second:
        copy.start()
    from_dp[g] = part[...]
    for copy in second:
        copy.wait()
    total = from_dp[0]
    for k in range(1, n_dp):
        total = total + from_dp[k]
    o_ref[piece(t)] = total
    third = []
    for k in range(1, n):
        third.append(
            pltpu.make_async_remote_copy(
                o_ref.at[piece(t)],
                o_ref.at[piece(t)],
                s3.at[k - 1],
                r3.at[k - 1],
                device_id=(g, lax.rem(t + k, n)),
                device_id_type=MESH,
            )
        )
    for copy in third:
        copy.start()
    for copy in third:
        copy.wait()


def sum_all(x, n_dp, n, collective_id):
    rows = x.shape[0] // n
    return pl.pallas_call(
        functools.partial(sum_all_kernel, n_dp, n),
        out_shape=jax.ShapeDtypeStruct(x.shape, x.dtype),
        in_specs=[IN_VMEM],
        out_specs=IN_VMEM,
        scratch_shapes=[
            pltpu.VMEM((n - 1, rows, 128), x.dtype),
            pltpu.VMEM((n_dp, rows, 128), x.dtype),
            pltpu.VMEM((rows, 128), x.dtype),
        ]
        + [DMA((n - 1,))] * 2
        + [DMA((n_dp - 1,))] * 2
        + [DMA((n - 1,))] * 2,
        compiler_params=pltpu.CompilerParams(collective_id=collective_id, has_side_effects=True),
        name="sum_all",
    )(x)


def local(
    tokens,
    cotangent,
    lengths,
    counts,
    query_weight,
    query_moment,
    query_square,
    shared_weight,
    shared_moment,
    shared_square,
    project_weight,
    project_moment,
    project_square,
    expand_weight,
    expand_moment,
    expand_square,
    shrink_weight,
    shrink_moment,
    shrink_square,
    vectors_value,
    vectors_moment,
    vectors_square,
):
    device = lax.axis_index("dp")
    n_dp = lax.axis_size("dp")
    t = lax.axis_index("tensor")
    n = lax.axis_size("tensor")
    row_count, width = tokens.shape
    slots = 2 * row_count // n_dp
    part_rows, part_cols = row_count // n, width // n
    send_start = lax.dynamic_index_in_dim(exclusive_sum(counts, 1), device, 0, keepdims=False)
    send_amount = lax.dynamic_index_in_dim(counts, device, 0, keepdims=False)
    recv_start = lax.dynamic_index_in_dim(exclusive_sum(counts, 0), device, 1, keepdims=False)
    recv_amount = lax.dynamic_index_in_dim(counts, device, 1, keepdims=False)
    send_slots = slot_matrix(send_start, send_amount, slots, row_count)
    recv_slots = slot_matrix(recv_start, recv_amount, slots, row_count)

    def low(x):
        return x.astype(jnp.bfloat16)

    def pack(rows, out_slots):
        return low(mul_plain(out_slots, rows)).reshape(n_dp, slots, rows.shape[1])

    def exchange(packed):
        return lax.all_to_all(packed, "dp", split_axis=0, concat_axis=0, tiled=True)

    def unpack(arrived, in_slots):
        return low(mul_left_t(in_slots, arrived.reshape(n_dp * slots, arrived.shape[2])))

    mine_cols = [
        lax.dynamic_slice_in_dim(a, t * part_cols, part_cols, 1) for a in (tokens, cotangent)
    ]
    packed, query_low, project_low, shared_low = lax.optimization_barrier(
        (
            pack(jnp.concatenate(mine_cols, axis=1), send_slots),
            low(query_weight),
            low(project_weight),
            low(shared_weight),
        )
    )
    query_line, shared_line = gather_lines(n_dp, n, query_low, shared_low)
    owned = unpack(exchange(packed), recv_slots)
    owned_rows, project_line, query_all, shared_all = rows_and_weights(
        n_dp, n, owned[:, :part_cols], project_low, query_line, shared_line
    )
    owned_grad = lax.all_gather(owned[:, part_cols:], "tensor", axis=1, tiled=True)

    head_size = shared_all.shape[1] // 2
    heads = width // head_size
    hidden_width = expand_weight.shape[1]
    hidden_total = hidden_width * n
    gain_one = vectors_value[0:width]
    shift_one = vectors_value[width : 2 * width]
    gain_two = vectors_value[2 * width : 3 * width]
    shift_two = vectors_value[3 * width : 4 * width]
    query_bias = vectors_value[4 * width : 5 * width]
    project_bias = vectors_value[5 * width : 6 * width]
    shrink_bias = vectors_value[6 * width : 7 * width]
    expand_bias = lax.dynamic_slice_in_dim(
        vectors_value, 7 * width + t * hidden_width, hidden_width, 0
    )
    value_bias = vectors_value[7 * width + hidden_total : 7 * width + hidden_total + head_size]

    inputs_float = owned_rows.astype(jnp.float32)
    normed_one, norm_one_back = jax.vjp(layer_norm, inputs_float, gain_one, shift_one)
    normed_low = normed_one.astype(jnp.bfloat16)
    queries = (mul_plain(normed_low, query_all) + query_bias).astype(jnp.bfloat16)
    shared_out = mul_plain(normed_low, shared_all) + jnp.concatenate(
        [jnp.zeros((head_size,), jnp.float32), value_bias]
    )
    shared_rows, project_all = shared_and_project(
        n_dp, n, shared_out.astype(jnp.bfloat16), project_line
    )
    key_rows, value_rows = shared_rows[:, :head_size], shared_rows[:, head_size:]
    query_heads = queries.reshape(part_rows, heads, head_size)
    segment, position = segment_ids(lengths[0], row_count)
    my_segment = lax.dynamic_slice_in_dim(segment, t * part_rows, part_rows, 0)
    my_position = lax.dynamic_slice_in_dim(position, t * part_rows, part_rows, 0)
    allowed = (my_segment[:, None] == segment[None, :]) & (
        my_position[:, None] >= position[None, :]
    )
    score_scale = head_size ** (-0.5)

    def masked_scores():
        scores = (
            jnp.einsum("bhd,kd->hbk", query_heads, key_rows, preferred_element_type=jnp.float32)
            * score_scale
        )
        return jnp.where(allowed[None], scores, masked_score)

    scores = masked_scores()
    row_max = jnp.max(scores, axis=-1, keepdims=True)
    expo = jnp.exp(scores - row_max)
    row_total = jnp.sum(expo, axis=-1, keepdims=True)
    probs = expo / row_total
    heads_out = (
        jnp.einsum(
            "hbk,kd->bhd",
            probs.astype(jnp.bfloat16),
            value_rows,
            preferred_element_type=jnp.float32,
        )
        .reshape(part_rows, width)
        .astype(jnp.bfloat16)
    )
    log_total = row_max + jnp.log(row_total)
    hidden_one = inputs_float + (mul_plain(heads_out, project_all) + project_bias)
    normed_two, norm_two_back = jax.vjp(layer_norm, hidden_one, gain_two, shift_two)

    normed_two_here, owned_grad = lax.optimization_barrier((low(normed_two), owned_grad))
    normed_two_low, expand_cols, shrink_rows = rows_and_expanded(
        n_dp, n, normed_two_here, low(expand_weight), low(shrink_weight)
    )
    expand_pre = mul_plain(normed_two_low, expand_cols) + expand_bias
    activated, gelu_back = jax.vjp(gelu_tanh, expand_pre)
    activated_low = activated.astype(jnp.bfloat16)
    skipped = lax.dynamic_update_slice_in_dim(
        jnp.zeros((row_count, width), jnp.float32), hidden_one + shrink_bias, t * part_rows, 0
    )
    result_part = low(mul_plain(activated_low, shrink_rows) + skipped)
    result_part, owned_grad = lax.optimization_barrier((result_part, owned_grad))
    layer_cols = lax.psum_scatter(result_part, "tensor", scatter_dimension=1, tiled=True)
    shrink_grad = low(mul_left_t(activated_low, owned_grad))
    activated_grad = mul_right_t(owned_grad, shrink_rows)
    expand_pre_grad = gelu_back(activated_grad)[0].astype(jnp.bfloat16)
    expand_grad = low(mul_left_t(normed_two_low, expand_pre_grad))
    expand_bias_grad = jnp.sum(expand_pre_grad.astype(jnp.float32), axis=0)
    normed_two_part = mul_right_t(expand_pre_grad, expand_cols).astype(jnp.bfloat16)

    normed_two_grad, expand_part, shrink_part = scatter_expanded(
        n_dp, n, normed_two_part, expand_grad, shrink_grad
    )
    output_cols = unpack(exchange(pack(layer_cols, recv_slots)), send_slots)
    output_float = lax.dynamic_slice_in_dim(owned_grad, t * part_rows, part_rows, 0).astype(
        jnp.float32
    )
    shrink_bias_grad = jnp.sum(output_float, axis=0)
    hidden_from_norm, gain_two_grad, shift_two_grad = norm_two_back(normed_two_grad)
    hidden_grad = output_float + hidden_from_norm
    branch_grad = hidden_grad.astype(jnp.bfloat16)
    project_bias_grad = jnp.sum(branch_grad.astype(jnp.float32), axis=0)
    project_grad = low(mul_left_t(heads_out, branch_grad))
    heads_grad = (
        mul_right_t(branch_grad, project_all)
        .astype(jnp.bfloat16)
        .reshape(part_rows, heads, head_size)
    )
    probs = jnp.exp(masked_scores() - log_total)
    prob_grad = jnp.einsum(
        "bhd,kd->hbk", heads_grad, value_rows, preferred_element_type=jnp.float32
    )
    score_grad = (
        probs * (prob_grad - jnp.sum(probs * prob_grad, axis=-1, keepdims=True))
    ).astype(jnp.bfloat16)
    query_grad = (
        (
            jnp.einsum("hbk,kd->bhd", score_grad, key_rows, preferred_element_type=jnp.float32)
            * score_scale
        )
        .reshape(part_rows, width)
        .astype(jnp.bfloat16)
    )
    key_grad = (
        jnp.einsum("hbk,bhd->kd", score_grad, query_heads, preferred_element_type=jnp.float32)
        * score_scale
    )
    value_grad = jnp.einsum(
        "hbk,bhd->kd",
        probs.astype(jnp.bfloat16),
        heads_grad,
        preferred_element_type=jnp.float32,
    )
    shared_part, output_cols = lax.optimization_barrier(
        (low(jnp.concatenate([key_grad, value_grad], axis=1)), output_cols)
    )
    shared_grad, project_sum = scatter_shared(n_dp, n, shared_part, project_grad)
    shared_grad = low(shared_grad)
    output_rows = lax.all_gather(output_cols, "tensor", axis=1, tiled=True)
    query_bias_grad = jnp.sum(query_grad.astype(jnp.float32), axis=0)
    query_weight_grad = mul_left_t(normed_low, query_grad)
    normed_one_grad = mul_right_t(query_grad, query_all) + mul_right_t(shared_grad, shared_all)
    inputs_from_norm, gain_one_grad, shift_one_grad = norm_one_back(normed_one_grad)
    input_result = (hidden_grad + inputs_from_norm).astype(jnp.bfloat16)
    shared_weight_grad = mul_left_t(normed_low, shared_grad)
    value_bias_grad = jnp.sum(shared_grad[:, head_size:].astype(jnp.float32), axis=0)

    project_part, query_sum, shared_sum, input_cols = cols_and_grads(
        n_dp, n, input_result, project_sum, low(query_weight_grad), low(shared_weight_grad)
    )
    input_cols, output_rows = lax.optimization_barrier(
        (unpack(exchange(pack(input_cols, recv_slots)), send_slots), output_rows)
    )
    grad_rows = lax.all_gather(input_cols, "tensor", axis=1, tiled=True)
    query_part, shared_piece = scatter_grads(n_dp, n, query_sum, shared_sum)
    output_back = output_rows.astype(jnp.float32)
    token_rms = jnp.sqrt(jnp.mean(output_back * output_back, axis=1))

    split_part = lax.dynamic_update_slice_in_dim(
        jnp.zeros((hidden_total,), jnp.float32), expand_bias_grad, t * hidden_width, 0
    )
    vector_part = jnp.concatenate(
        [
            gain_one_grad,
            shift_one_grad,
            gain_two_grad,
            shift_two_grad,
            query_bias_grad,
            project_bias_grad,
            shrink_bias_grad,
            split_part,
            value_bias_grad,
        ]
    )
    local_squares = (
        jnp.sum(query_part * query_part)
        + jnp.sum(expand_part * expand_part)
        + jnp.sum(shared_piece * shared_piece)
        + jnp.sum(project_part * project_part)
        + jnp.sum(shrink_part * shrink_part)
    )
    length = vector_part.shape[0]
    unit = n * 8 * 128
    padded = -(-(length + 1) // unit) * unit
    everything = jnp.concatenate(
        [vector_part, local_squares[None], jnp.zeros((padded - length - 1,), jnp.float32)]
    )
    summed = sum_all(everything.reshape(padded // 128, 128), n_dp, n, 9).reshape(padded)
    vector_grad, weight_squares = summed[:length], summed[length]
    grad_size = jnp.sqrt(weight_squares + jnp.sum(vector_grad * vector_grad))
    clip_factor = jnp.minimum(1.0, clip_level / (grad_size + 1e-06))
    clipped_vectors = clip_factor * vector_grad
    query_new = adamw_step(
        query_weight,
        query_moment,
        query_square,
        clip_factor * query_part,
        rate_matrix * width ** (-0.5),
    )
    shared_new = adamw_step(
        shared_weight,
        shared_moment,
        shared_square,
        clip_factor * shared_piece,
        rate_attention * width ** (-0.5),
    )
    project_new = adamw_step(
        project_weight,
        project_moment,
        project_square,
        clip_factor * project_part,
        rate_attention * width ** (-0.5),
    )
    expand_new = adamw_step(
        expand_weight,
        expand_moment,
        expand_square,
        clip_factor * expand_part,
        rate_matrix * width ** (-0.5),
    )
    shrink_new = adamw_step(
        shrink_weight,
        shrink_moment,
        shrink_square,
        clip_factor * shrink_part,
        rate_matrix * hidden_total ** (-0.5),
    )
    vectors_new = adamw_step(
        vectors_value, vectors_moment, vectors_square, clipped_vectors, rate_vector
    )
    return (
        output_rows,
        grad_rows,
        grad_size,
        *query_new,
        *shared_new,
        *project_new,
        *expand_new,
        *shrink_new,
        *vectors_new,
        clipped_vectors,
        token_rms,
    )


def solution(mesh):
    by_rows = P("dp", None)
    query = P("dp", "tensor")
    shared = P(("dp", "tensor"), None)
    project = P("tensor", "dp")
    return jax.shard_map(
        local,
        mesh=mesh,
        in_specs=(
            *(by_rows,) * 3,
            P(),
            *(query,) * 3,
            *(shared,) * 3,
            *(project,) * 3,
            *(query,) * 3,
            *(project,) * 3,
            *(P(),) * 3,
        ),
        out_specs=(
            *(by_rows,) * 2,
            P(),
            *(query,) * 3,
            *(shared,) * 3,
            *(project,) * 3,
            *(query,) * 3,
            *(project,) * 3,
            *(P(),) * 4,
            P("dp"),
        ),
        check_vma=False,
    )
```

```python
import functools

import jax
import jax.numpy as jnp
from jax import lax
from jax.experimental.layout import Layout, with_layout_constraint
from jax.experimental import pallas as pl
from jax.experimental.pallas import tpu as pltpu
from jax.sharding import PartitionSpec as P

STEP = 10


beta_one = 0.9
beta_two = 0.95
adam_epsilon = 1e-08
decay_rate = 0.1
clip_level = 1.0
norm_epsilon = 1e-05
rate_matrix = 0.6
rate_attention = 2.4
rate_vector = 0.3
masked_score = -1e30
longest = 512

MESH = pl.DeviceIdType.MESH
IN_PLACE = pl.BlockSpec(memory_space=pl.ANY)
IN_VMEM = pl.BlockSpec(memory_space=pltpu.VMEM)
DMA = pltpu.SemaphoreType.DMA
MIB = 2**20


def mul_plain(left, right):
    return jnp.dot(left, right, preferred_element_type=jnp.float32)


def mul_right_t(left, right):
    return lax.dot_general(
        left, right, (((1,), (1,)), ((), ())), preferred_element_type=jnp.float32
    )


def mul_left_t(left, right):
    return lax.dot_general(
        left, right, (((0,), (0,)), ((), ())), preferred_element_type=jnp.float32
    )


def layer_norm(values, scaling, offset):
    average = jnp.mean(values, axis=-1, keepdims=True)
    centered = values - average
    variance = jnp.mean(centered * centered, axis=-1, keepdims=True)
    return centered * lax.rsqrt(variance + norm_epsilon) * scaling + offset


def gelu_tanh(values):
    return jax.nn.gelu(values, approximate=True)


def exclusive_sum(table, axis_index):
    return jnp.cumsum(table, axis=axis_index) - table


def segment_ids(seq_lengths, row_count):
    position = jnp.arange(row_count, dtype=jnp.int32)
    starts = jnp.cumsum(seq_lengths) - seq_lengths
    segment = jnp.sum((starts[None, :] <= position[:, None]).astype(jnp.int32), axis=1)
    return (segment, position)


def slot_matrix(starts, amounts, slots, row_count):
    offsets = jnp.arange(slots, dtype=jnp.int32)
    picked = jnp.where(offsets[None, :] < amounts[:, None], starts[:, None] + offsets[None, :], -1)
    position = jnp.arange(row_count, dtype=jnp.int32)
    return (picked.reshape(-1)[:, None] == position[None, :]).astype(jnp.bfloat16)


def turned(x):
    return with_layout_constraint(x.T, Layout(major_to_minor=(0, 1)))


def adamw_step(weight, moment, square, gradient, rate):
    moment_new = beta_one * moment + (1.0 - beta_one) * gradient
    square_new = beta_two * square + (1.0 - beta_two) * gradient * gradient
    moment_hat = moment_new / (1.0 - beta_one**STEP)
    square_hat = square_new / (1.0 - beta_two**STEP)
    weight_new = weight - rate * (
        moment_hat / (jnp.sqrt(square_hat) + adam_epsilon) + decay_rate * weight
    )
    return (weight_new, moment_new, square_new)


def remote(src, dst, send_sem, recv_sem, device):
    return pltpu.make_async_remote_copy(
        src, dst, send_sem, recv_sem, device_id=device, device_id_type=MESH
    )


class Place:
    def __init__(self, n_dp, n):
        self.n, self.chips = n, n_dp // 2
        self.dp, self.t = lax.axis_index("dp"), lax.axis_index("tensor")
        self.core, chip = lax.rem(self.dp, 2), lax.div(self.dp, 2)
        side = round(self.chips**0.5)
        self.side = side if side * side == self.chips else self.chips
        self.pos = self.snake(chip)
        self.sibling = (self.dp + 1 - 2 * self.core, self.t)
        self.after = (self.block(self.ring(self.pos + 1), self.core), self.t)
        self.before = (self.block(self.ring(self.pos - 1), self.core), self.t)
        self.left, self.right = (self.dp, self.t - 1), (self.dp, self.t + 1)

    def snake(self, index):
        row, col = lax.div(index, self.side), lax.rem(index, self.side)
        odd = lax.rem(row, 2)
        return row * self.side + col + odd * (self.side - 1 - 2 * col)

    def ring(self, pos):
        return lax.rem(pos + 2 * self.chips, self.chips)

    def block(self, pos, core):
        return self.snake(pos) * 2 + core

    def greet(self, line=False, line_all=False, ring=False):
        barrier = pltpu.get_barrier_semaphore()
        peers = 0

        def call(device):
            pl.semaphore_signal(barrier, inc=1, device_id=device, device_id_type=MESH)

        if ring:
            for device in (self.sibling, self.after, self.before):
                call(device)
            peers += 3
        if line_all:
            for k in range(1, self.n):
                call((self.dp, lax.rem(self.t + k, self.n)))
            peers += self.n - 1
        elif line:
            pl.when(self.t > 0)(lambda: call(self.left))
            pl.when(self.t < self.n - 1)(lambda: call(self.right))
            peers += (self.t > 0).astype(jnp.int32) + (self.t < self.n - 1).astype(jnp.int32)
        return lambda: pl.semaphore_wait(barrier, peers)


class LineGather:
    @staticmethod
    def sems(n, chunks):
        return [DMA((n - 1, chunks))] * 4 + [DMA]

    def __init__(self, at, chunks, first, place, sems, whole, unit=1.0):
        self.unit = unit
        self.at, self.chunks, self.first, self.place, self.sems = at, chunks, first, place, sems
        self.own = pltpu.make_async_copy(whole[0], whole[1], sems[4])

    def copy(self, h, c, right):
        at = self.at
        dst = self.place(at.t - h if right else at.t + h, c)
        src = self.first(c) if h == 0 else dst
        s, r = self.sems[0:2] if right else self.sems[2:4]
        return remote(src, dst, s.at[h, c], r.at[h, c], at.right if right else at.left)

    def receive(self, h, c, right):
        at = self.at
        dst = self.place(at.t - 1 - h if right else at.t + 1 + h, c)
        s, r = self.sems[0:2] if right else self.sems[2:4]
        remote(dst, dst, s.at[h, c], r.at[h, c], at.left if right else at.right).wait_recv()

    def sends(self, h, right):
        t, n = self.at.t, self.at.n
        return (t >= h) & (t < n - 1) if right else (t + h <= n - 1) & (t > 0)

    def gets(self, h, right):
        return self.at.t - 1 - h >= 0 if right else self.at.t + 1 + h <= self.at.n - 1

    def every(self):
        for h in range(self.at.n - 1):
            for c in range(self.chunks):
                for right in (True, False):
                    yield h, c, right

    def prepare(self):
        self.own.start()

    def prepared(self):
        self.own.wait()

    def start(self):
        for h, c, right in self.every():
            if h == 0:
                pl.when(self.sends(h, right))(lambda: self.copy(h, c, right).start())

    def step(self, h, c, right):
        pl.when(self.gets(h, right))(lambda: self.receive(h, c, right))
        if h + 1 < self.at.n - 1:
            pl.when(self.sends(h + 1, right))(lambda: self.copy(h + 1, c, right).start())

    def steps(self):
        return [
            (self.unit * (which[0] + (which[1] + 1) / self.chunks), functools.partial(self.step, *which))
            for which in self.every()
        ]

    def finish(self):
        for h, c, right in self.every():
            pl.when(self.sends(h, right))(lambda: self.copy(h, c, right).wait_send())


class LineScatter:
    @staticmethod
    def scratch(n, chunks, block, dtype):
        return [pltpu.VMEM((n - 1, *block), dtype)] * 2 + [DMA((n - 1, chunks))] * 4

    def __init__(self, at, chunks, own, out, scratch, unit=1.0):
        self.unit = unit
        self.at, self.chunks, self.own, self.out = at, chunks, own, out
        self.held, self.sems = scratch[:2], scratch[2:6]
        self.rows = self.held[0].shape[1] // chunks

    def parts(self, k, c, right):
        side = 0 if right else 1
        s, r = self.sems[2 * side : 2 * side + 2]
        return self.held[side].at[k, pl.ds(c * self.rows, self.rows)], s.at[k, c], r.at[k, c]

    def send(self, k, c, right, first):
        slot, s, r = self.parts(k, c, right)
        src = self.own(self.target(k, right), c) if first else slot
        return remote(src, slot, s, r, self.at.right if right else self.at.left)

    def receive(self, k, c, right):
        slot, s, r = self.parts(k, c, right)
        remote(slot, slot, s, r, self.at.left if right else self.at.right).wait_recv()

    def target(self, k, right):
        return self.at.n - 1 - k if right else k

    def every(self):
        for k in range(self.at.n - 1):
            for c in range(self.chunks):
                for right in (True, False):
                    yield k, c, right

    def prepare(self):
        pass

    def prepared(self):
        pass

    def start(self):
        t, n = self.at.t, self.at.n
        for k, c, right in self.every():
            first = (t == (0 if right else n - 1)) & (t != self.target(k, right))
            pl.when(first)(lambda: self.send(k, c, right, True).start())

    def add(self, k, c, right):
        self.receive(k, c, right)
        slot = self.parts(k, c, right)[0]
        mine = self.own(self.target(k, right), c)[...]
        slot[...] = (slot[...].astype(jnp.float32) + mine.astype(jnp.float32)).astype(slot.dtype)
        self.send(k, c, right, False).start()

    def step(self, k, c, right):
        t, n, d = self.at.t, self.at.n, self.target(k, right)
        passes = (t > 0) & (t < d) if right else (t < n - 1) & (t > d)
        pl.when(passes)(lambda: self.add(k, c, right))

    def steps(self):
        return [
            (self.unit * (which[0] + (which[1] + 1) / self.chunks), functools.partial(self.step, *which))
            for which in self.every()
        ]

    def finish(self):
        t, n = self.at.t, self.at.n
        for k, c, right in self.every():
            pl.when(t == self.target(k, right))(lambda: self.receive(k, c, right))
        for c in range(self.chunks):
            span = pl.ds(c * self.rows, self.rows)
            self.out[span] = self.own(t, c)[...].astype(self.out.dtype)

        def more(block):
            self.out[...] += block[...].astype(self.out.dtype)

        pl.when(t > 0)(lambda: more(self.held[0].at[n - 1 - t]))
        pl.when(t < n - 1)(lambda: more(self.held[1].at[t]))
        for k, c, right in self.every():
            d = self.target(k, right)
            pl.when(t < d if right else t > d)(lambda: self.send(k, c, right, False).wait_send())


class LineExchange:
    @staticmethod
    def scratch(n, block, dtype):
        return [pltpu.VMEM((n - 1, *block), dtype)] + [DMA((n - 1,))] * 2

    def __init__(self, at, source, out, scratch):
        self.at, self.source, self.out = at, source, out
        self.held = scratch[0]
        self.copies = []
        for k in range(1, at.n):
            p = lax.rem(at.t + k, at.n)
            self.copies.append(
                remote(
                    source(p),
                    self.held.at[k - 1],
                    scratch[1].at[k - 1],
                    scratch[2].at[k - 1],
                    (at.dp, p),
                )
            )

    def prepare(self):
        pass

    def prepared(self):
        pass

    def start(self):
        for copy in self.copies:
            copy.start()

    def steps(self):
        return []

    def finish(self):
        for copy in self.copies:
            copy.wait()
        total = self.source(self.at.t)[...].astype(jnp.float32)
        for k in range(self.at.n - 1):
            total = total + self.held[k].astype(jnp.float32)
        self.out[...] = total.astype(self.out.dtype)


class RingGather:
    @staticmethod
    def sems(chips, chunks):
        hops = chips // 2
        return [DMA((2, hops, chunks))] * 4 + [DMA((chunks,))] * 2 + [DMA]

    def __init__(self, at, chunks, first, place, sems, whole, unit=1.0):
        self.unit = unit
        self.at, self.chunks, self.first, self.place, self.sems = at, chunks, first, place, sems
        self.hops = at.chips // 2
        self.own = pltpu.make_async_copy(whole[0], whole[1], sems[6])

    def every(self):
        for h in range(self.hops):
            for c in range(self.chunks):
                for way in (0, 1):
                    if h < self.hops - 1 or c % 2 == way:
                        yield h, c, way

    def origin(self, steps, way, core):
        return self.at.block(self.at.ring(self.at.pos + (steps if way else -steps)), core)

    def onward(self, h, c, way):
        dst = self.place(self.origin(h, way, self.at.core), c)
        src = self.first(c) if h == 0 else dst
        s, r = self.sems[0:2]
        device = self.at.before if way else self.at.after
        return remote(src, dst, s.at[way, h, c], r.at[way, h, c], device)

    def arrival(self, h, c, way):
        dst = self.place(self.origin(h + 1, way, self.at.core), c)
        s, r = self.sems[0:2]
        device = self.at.after if way else self.at.before
        return remote(dst, dst, s.at[way, h, c], r.at[way, h, c], device)

    def across(self, h, c, way, core):
        dst = self.place(self.origin(h + 1, way, core), c)
        s, r = self.sems[2:4]
        return remote(dst, dst, s.at[way, h, c], r.at[way, h, c], self.at.sibling)

    def across_own(self, c, core):
        dst = self.place(self.origin(0, 0, core), c)
        s, r = self.sems[4:6]
        return remote(self.first(c), dst, s.at[c], r.at[c], self.at.sibling)

    def prepare(self):
        self.own.start()

    def prepared(self):
        self.own.wait()

    def start(self):
        for h, c, way in self.every():
            if h == 0:
                self.onward(h, c, way).start()
        for c in range(self.chunks):
            self.across_own(c, self.at.core).start()

    def step(self, h, c, way):
        self.arrival(h, c, way).wait_recv()
        if (h + 1, c, way) in list(self.every()):
            self.onward(h + 1, c, way).start()
        self.across(h, c, way, self.at.core).start()

    def steps(self):
        when = 0.0
        for h, c, way in self.every():
            when += self.unit / self.chunks / 2
            yield when, functools.partial(self.step, h, c, way)

    def finish(self):
        other = 1 - self.at.core
        for c in range(self.chunks):
            self.across_own(c, other).wait_recv()
            self.across_own(c, self.at.core).wait_send()
        for h, c, way in self.every():
            self.across(h, c, way, other).wait_recv()
            self.across(h, c, way, self.at.core).wait_send()
            self.onward(h, c, way).wait_send()


class RingScatter:
    @staticmethod
    def scratch(chips, chunks, block, dtype):
        hops = chips // 2
        return (
            [pltpu.VMEM((chips, *block), dtype)] * 2
            + [pltpu.VMEM((2, hops, *block), dtype)]
            + [DMA((chips, chunks))] * 3
            + [DMA((2, hops, chunks))] * 2
        )

    def __init__(self, at, chunks, source, out, scratch, unit=1.0):
        self.unit = unit
        self.at, self.chunks, self.source, self.out = at, chunks, source, out
        self.hops = at.chips // 2
        self.mine, self.other, self.held = scratch[:3]
        self.load_sem, self.s1, self.r1, self.s2, self.r2 = scratch[3:8]
        self.rows = self.held.shape[2] // chunks

    def span(self, c):
        return pl.ds(c * self.rows, self.rows)

    def target(self, place, core):
        return self.at.block(self.at.ring(self.at.pos + place), core)

    def load(self, place, c):
        src = self.source(self.target(place, self.at.core), c)
        dst = self.mine.at[place, self.span(c)]
        return pltpu.make_async_copy(src, dst, self.load_sem.at[place, c])

    def across(self, place, c):
        src = self.source(self.target(place, 1 - self.at.core), c)
        dst = self.other.at[place, self.span(c)]
        return remote(src, dst, self.s1.at[place, c], self.r1.at[place, c], self.at.sibling)

    def sent(self, e, c, way):
        return e < self.hops or c % 2 == way

    def onward(self, e, c, way):
        place = self.at.chips - e if way else e
        src, dst = self.mine.at[place, self.span(c)], self.held.at[way, e - 1, self.span(c)]
        device = self.at.before if way else self.at.after
        return remote(src, dst, self.s2.at[way, e - 1, c], self.r2.at[way, e - 1, c], device)

    def arrival(self, e, c, way):
        dst = self.held.at[way, e, self.span(c)]
        device = self.at.after if way else self.at.before
        return remote(dst, dst, self.s2.at[way, e, c], self.r2.at[way, e, c], device)

    def places(self):
        order = []
        for e in range(self.hops, 0, -1):
            order += [e] if e == self.hops else [e, self.at.chips - e]
        return order + [0]

    def prepare(self):
        for place in self.places():
            for c in range(self.chunks):
                self.load(place, c).start()

    def prepared(self):
        for place in self.places():
            for c in range(self.chunks):
                self.load(place, c).wait()

    def start(self):
        for place in self.places():
            for c in range(self.chunks):
                self.across(place, c).start()

    def base(self, place, c):
        self.across(place, c).wait_recv()
        total = self.mine[place, self.span(c)].astype(jnp.float32)
        return total + self.other[place, self.span(c)].astype(jnp.float32)

    def arrived(self, e, c, way):
        self.arrival(e, c, way).wait_recv()
        return self.held[way, e, self.span(c)].astype(jnp.float32)

    def step(self, e, c, way):
        place = self.at.chips - e if way else e
        total = self.base(place, c)
        if e < self.hops and self.sent(e + 1, c, way):
            total += self.arrived(e, c, way)
        self.mine[place, self.span(c)] = total.astype(self.mine.dtype)
        self.onward(e, c, way).start()

    def last(self, c):
        total = self.base(0, c)
        for way in (0, 1):
            if self.sent(1, c, way):
                total += self.arrived(0, c, way)
        self.out[self.span(c)] = total.astype(self.out.dtype)

    def every(self):
        for e in range(self.hops, 0, -1):
            for c in range(self.chunks):
                for way in (0, 1):
                    if self.sent(e, c, way):
                        yield e, c, way

    def steps(self):
        when = 0.0
        for e, c, way in self.every():
            yield when, functools.partial(self.step, e, c, way)
            when += self.unit / self.chunks / 2
        for c in range(self.chunks):
            yield when + self.unit * (c + 1) / self.chunks, functools.partial(self.last, c)

    def finish(self):
        for place in self.places():
            for c in range(self.chunks):
                self.across(place, c).wait_send()
        for e, c, way in self.every():
            self.onward(e, c, way).wait_send()


class LineSwitch:
    @staticmethod
    def sems(n):
        return [DMA((n - 1,))] * 2 + [DMA]

    def __init__(self, at, source, target, sems):
        self.own = pltpu.make_async_copy(source(at.t), target, sems[2])
        self.copies = []
        for k in range(1, at.n):
            p = lax.rem(at.t + k, at.n)
            self.copies.append(
                remote(source(p), target, sems[0].at[k - 1], sems[1].at[k - 1], (at.dp, p))
            )

    def prepare(self):
        self.own.start()

    def prepared(self):
        self.own.wait()

    def start(self):
        for copy in self.copies:
            copy.start()

    def steps(self):
        return []

    def finish(self):
        for copy in self.copies:
            copy.wait()


def run_jobs(met, jobs):
    for job in jobs:
        job.prepare()
    for job in jobs:
        job.prepared()
    met()
    for job in jobs:
        job.start()
    ordered = []
    for i, job in enumerate(jobs):
        ordered += [(when, i, j, step) for j, (when, step) in enumerate(job.steps())]
    for _, _, _, step in sorted(ordered, key=lambda entry: entry[:3]):
        step()
    for job in jobs:
        job.finish()


def rows_of(ref, step):
    return lambda c: ref.at[pl.ds(c * step, step)]


def lanes(index, count):
    return pl.ds(pl.multiple_of(index * count, count), count)


def move(kernel, inputs, in_vmem, outs, out_vmem, scratch, collective_id, name, aliases=None):
    return pl.pallas_call(
        kernel,
        out_shape=tuple(outs),
        in_specs=[IN_VMEM if i < in_vmem else IN_PLACE for i in range(len(inputs))],
        out_specs=tuple(IN_VMEM if i < out_vmem else IN_PLACE for i in range(len(outs))),
        scratch_shapes=scratch,
        compiler_params=pltpu.CompilerParams(
            collective_id=collective_id, has_side_effects=True, vmem_limit_bytes=56 * MIB
        ),
        input_output_aliases=aliases or {},
        name=name,
    )(*inputs)


def line_gather(at, x, out, axis, chunks, sems, unit=1.0):
    rows, cols = x.shape
    step = rows // chunks
    if axis == 0:
        place = lambda b, c: out.at[pl.ds(b * rows + c * step, step)]
        whole = out.at[pl.ds(at.t * rows, rows)]
    else:
        place = lambda b, c: out.at[pl.ds(c * step, step), lanes(b, cols)]
        whole = out.at[:, lanes(at.t, cols)]
    return LineGather(at, chunks, rows_of(x, step), place, sems, (x, whole), unit)


def ring_gather(at, x, out, axis, chunks, sems, unit=1.0):
    rows, cols = x.shape
    step = rows // chunks
    if axis == 0:
        place = lambda b, c: out.at[pl.ds(b * rows + c * step, step)]
        whole = out.at[pl.ds(at.dp * rows, rows)]
    else:
        place = lambda b, c: out.at[pl.ds(c * step, step), lanes(b, cols)]
        whole = out.at[:, lanes(at.dp, cols)]
    return RingGather(at, chunks, rows_of(x, step), place, sems, (x, whole), unit)


def blocks_of(x, out, axis, chunks):
    rows, cols = out.shape
    step = rows // chunks
    if axis == 0:
        return lambda b, c: x.at[pl.ds(pl.multiple_of(b * rows + c * step, step), step)]
    return lambda b, c: x.at[pl.ds(c * step, step), lanes(b, cols)]


def line_exchange(at, x, out, axis, scratch):
    block = blocks_of(x, out, axis, 1)
    return LineExchange(at, lambda p: block(p, 0), out, scratch)


def line_scatter(at, x, out, axis, chunks, scratch, unit=1.0):
    return LineScatter(at, chunks, blocks_of(x, out, axis, chunks), out, scratch, unit)


def ring_scatter(at, x, out, axis, chunks, scratch, unit=1.0):
    return RingScatter(at, chunks, blocks_of(x, out, axis, chunks), out, scratch, unit)


def like(x, rows, cols, dtype=None):
    return jax.ShapeDtypeStruct((x.shape[0] * rows, x.shape[1] * cols), dtype or x.dtype)


class Parts:
    def __init__(self, refs):
        self.refs = list(refs)

    def take(self, shapes):
        taken, self.refs = self.refs[: len(shapes)], self.refs[len(shapes) :]
        return taken


def gather_lines(n_dp, n, query, project, shared):
    sems = LineGather.sems(n, 1)

    def kernel(a, b, c, a_out, b_out, c_out, *refs):
        parts = Parts(refs)
        at = Place(n_dp, n)
        run_jobs(
            at.greet(line=True),
            [
                line_gather(at, a, a_out, 1, 1, parts.take(sems), 6.0),
                line_gather(at, c, c_out, 0, 1, parts.take(sems), 6.5),
                line_gather(at, b, b_out, 1, 1, parts.take(sems), 12.0),
            ],
        )

    return move(
        kernel,
        (query, project, shared),
        3,
        (like(query, 1, n), like(project, 1, n), like(shared, n, 1)),
        0,
        sems * 3,
        1,
        "gather_lines",
    )


def rows_and_weights(n_dp, n, owned, query, shared):
    chips, chunks = n_dp // 2, 2
    total, cols = owned.shape[0], owned.shape[1] // 2
    rows, half = total // n, total // 2
    switch, line = LineSwitch.sems(n), LineGather.sems(n, chunks)
    ring = RingGather.sems(chips, chunks)

    def kernel(x, a, b, x_out, y_out, a_out, b_out, *refs):
        parts = Parts(refs)
        at = Place(n_dp, n)
        run_jobs(
            at.greet(line_all=True, ring=True),
            [
                LineSwitch(
                    at,
                    lambda p: x.at[pl.ds(pl.multiple_of(p * rows, rows), rows), pl.ds(0, cols)],
                    x_out.at[:, lanes(at.t, cols)],
                    parts.take(switch),
                ),
                ring_gather(at, b, b_out, 0, chunks, parts.take(ring), 4.0),
                ring_gather(at, a, a_out, 0, chunks, parts.take(ring), 22.0),
                line_gather(
                    at,
                    x.at[pl.ds(0, half), pl.ds(cols, cols)],
                    y_out.at[pl.ds(0, half)],
                    1,
                    chunks,
                    parts.take(line),
                    16.0,
                ),
            ],
        )

    return move(
        kernel,
        (owned, query, shared),
        3,
        (
            jax.ShapeDtypeStruct((rows, n * cols), owned.dtype),
            jax.ShapeDtypeStruct((total, n * cols), owned.dtype),
            like(query, n_dp, 1),
            like(shared, n_dp, 1),
        ),
        0,
        switch + ring * 2 + line,
        2,
        "rows_and_weights",
    )


def shared_and_project(n_dp, n, owned, shared_rows, project, gathered):
    chips, chunks = n_dp // 2, 2
    total, cols = owned.shape[0], owned.shape[1] // 2
    half = total // 2
    small, line = LineGather.sems(n, 1), LineGather.sems(n, chunks)
    ring = RingGather.sems(chips, chunks)

    def kernel(y, x, a, _, x_out, a_out, y_out, *refs):
        parts = Parts(refs)
        at = Place(n_dp, n)
        lower = pl.ds(half, half)
        run_jobs(
            at.greet(line=True, ring=True),
            [
                line_gather(at, x, x_out, 0, 1, parts.take(small), 4.0),
                ring_gather(at, a, a_out, 0, chunks, parts.take(ring), 22.0),
                line_gather(
                    at,
                    y.at[lower, pl.ds(cols, cols)],
                    y_out.at[lower],
                    1,
                    chunks,
                    parts.take(line),
                    13.0,
                ),
            ],
        )

    return move(
        kernel,
        (owned, shared_rows, project, gathered),
        3,
        (like(shared_rows, n, 1), like(project, n_dp, 1), like(gathered, 1, 1)),
        0,
        small + ring + line,
        3,
        "shared_and_project",
        {3: 2},
    )


def rows_and_expanded(n_dp, n, x, expand, shrink):
    chips, chunks, halves = n_dp // 2, 4, 2
    line, ring = LineGather.sems(n, chunks), RingGather.sems(chips, halves)

    def kernel(x_ref, a, b, x_out, a_out, b_out, *refs):
        parts = Parts(refs)
        at = Place(n_dp, n)
        run_jobs(
            at.greet(line=True, ring=True),
            [
                line_gather(at, x_ref, x_out, 0, chunks, parts.take(line), 22.0),
                ring_gather(at, a, a_out, 0, halves, parts.take(ring), 44.0),
                ring_gather(at, b, b_out, 0, halves, parts.take(ring), 44.0),
            ],
        )

    return move(
        kernel,
        (x, expand, shrink),
        3,
        (like(x, n, 1), like(expand, n_dp, 1), like(shrink, n_dp, 1)),
        0,
        line + ring * 2,
        4,
        "rows_and_expanded",
    )


def scatter_expanded(n_dp, n, x, expand, shrink):
    chips, chunks = n_dp // 2, 4
    block = (x.shape[0] // n, x.shape[1])
    w_block = (expand.shape[0] // n_dp, expand.shape[1])
    line = LineScatter.scratch(n, chunks, block, x.dtype)
    ring = RingScatter.scratch(chips, chunks, w_block, x.dtype)

    def kernel(x_ref, a, b, x_out, a_out, b_out, *refs):
        parts = Parts(refs)
        at = Place(n_dp, n)
        run_jobs(
            at.greet(line=True, ring=True),
            [
                line_scatter(at, x_ref, x_out, 0, chunks, parts.take(line), 26.0),
                ring_scatter(at, a, a_out, 0, chunks, parts.take(ring), 22.0),
                ring_scatter(at, b, b_out, 0, chunks, parts.take(ring), 22.0),
            ],
        )

    return move(
        kernel,
        (x, expand, shrink),
        1,
        [jax.ShapeDtypeStruct(shape, jnp.float32) for shape in (block, w_block, w_block)],
        3,
        line + ring * 2,
        5,
        "scatter_expanded",
    )


def scatter_shared(n_dp, n, x, result, query, project):
    chips, chunks = n_dp // 2, 4
    block = (x.shape[0] // n, x.shape[1])
    w_block = (project.shape[0] // n_dp, project.shape[1])
    small = LineExchange.scratch(n, block, x.dtype)
    line = LineGather.sems(n, chunks)
    ring = RingScatter.scratch(chips, chunks, w_block, x.dtype)

    def kernel(x_ref, y, a, b, x_out, a_out, b_out, y_out, *refs):
        parts = Parts(refs)
        at = Place(n_dp, n)
        run_jobs(
            at.greet(line_all=True, ring=True),
            [
                line_exchange(at, x_ref, x_out, 0, parts.take(small)),
                line_gather(at, y, y_out, 1, chunks, parts.take(line), 22.0),
                ring_scatter(at, a, a_out, 0, chunks, parts.take(ring), 24.0),
                ring_scatter(at, b, b_out, 0, chunks, parts.take(ring), 24.0),
            ],
        )

    return move(
        kernel,
        (x, result, query, project),
        2,
        (
            jax.ShapeDtypeStruct(block, jnp.float32),
            jax.ShapeDtypeStruct(w_block, x.dtype),
            jax.ShapeDtypeStruct(w_block, x.dtype),
            like(result, 1, n),
        ),
        3,
        small + line + ring * 2,
        6,
        "scatter_shared",
    )


def cols_and_shared(n_dp, n, rows, shared):
    chips = n_dp // 2
    count, width = rows.shape
    cols = width // n
    s_block = (shared.shape[0] // n_dp, shared.shape[1])
    switch = LineSwitch.sems(n)
    ring = RingScatter.scratch(chips, 1, s_block, shared.dtype)

    def kernel(x, c, c_out, x_out, *refs):
        parts = Parts(refs)
        at = Place(n_dp, n)
        run_jobs(
            at.greet(line_all=True, ring=True),
            [
                LineSwitch(
                    at,
                    lambda p: x.at[:, lanes(p, cols)],
                    x_out.at[pl.ds(at.t * count, count)],
                    parts.take(switch),
                ),
                ring_scatter(at, c, c_out, 0, 1, parts.take(ring), 4.0),
            ],
        )

    return move(
        kernel,
        (rows, shared),
        1,
        [
            jax.ShapeDtypeStruct(s_block, shared.dtype),
            jax.ShapeDtypeStruct((n * count, cols), rows.dtype),
        ],
        1,
        switch + ring,
        7,
        "cols_and_shared",
    )


def scatter_grads(n_dp, n, query, project, shared):
    w_block = (query.shape[0], query.shape[1] // n)
    s_block = (shared.shape[0] // n, shared.shape[1])
    line = LineScatter.scratch(n, 1, w_block, query.dtype)
    small = LineExchange.scratch(n, s_block, shared.dtype)

    def kernel(a, b, c, a_out, b_out, c_out, *refs):
        parts = Parts(refs)
        at = Place(n_dp, n)
        run_jobs(
            at.greet(line_all=True),
            [
                line_scatter(at, a, a_out, 1, 1, parts.take(line), 12.0),
                line_scatter(at, b, b_out, 1, 1, parts.take(line), 12.0),
                line_exchange(at, c, c_out, 0, parts.take(small)),
            ],
        )

    return move(
        kernel,
        (query, project, shared),
        3,
        [jax.ShapeDtypeStruct(block, jnp.float32) for block in (w_block, w_block, s_block)],
        3,
        line * 2 + small,
        8,
        "scatter_grads",
    )


def product(left, right, left_dim, right_dim):
    return lax.dot_general(
        left, right, (((left_dim,), (right_dim,)), ((), ())), preferred_element_type=jnp.float32
    )


def fill_bias(bias, seg_row, seg_col, pos_row, pos_col):
    @pl.when(pl.program_id(0) == 0)
    def _():
        allowed = (seg_row[...] == seg_col[...]) & (pos_row[...] >= pos_col[...])
        bias[...] = jnp.where(allowed, 0.0, masked_score)


def attend_kernel(scale, q, k, v, seg_row, seg_col, pos_row, pos_col, o, log_total, bias):
    fill_bias(bias, seg_row, seg_col, pos_row, pos_col)
    scores = product(q[...], k[...], 1, 1) * scale + bias[...]
    row_max = jnp.max(scores, axis=1, keepdims=True)
    expo = jnp.exp(scores - row_max)
    row_total = jnp.sum(expo, axis=1, keepdims=True)
    probs = (expo / row_total).astype(jnp.bfloat16)
    o[...] = product(probs, v[...], 1, 0).astype(jnp.bfloat16)
    log_total[...] = jnp.broadcast_to(row_max + jnp.log(row_total), log_total.shape)


def attend_back_kernel(
    scale, q, do, log_total, k, v, seg_row, seg_col, pos_row, pos_col, dq, dk, dv, bias
):
    fill_bias(bias, seg_row, seg_col, pos_row, pos_col)

    @pl.when(pl.program_id(0) == 0)
    def _():
        dk[...] = jnp.zeros_like(dk)
        dv[...] = jnp.zeros_like(dv)

    scores = product(q[...], k[...], 1, 1) * scale + bias[...]
    probs = jnp.exp(scores - log_total[:, :1])
    prob_grad = product(do[...], v[...], 1, 1)
    inner = jnp.sum(probs * prob_grad, axis=1, keepdims=True)
    score_grad = (probs * (prob_grad - inner)).astype(jnp.bfloat16)
    dq[...] = (product(score_grad, k[...], 1, 0) * scale).astype(jnp.bfloat16)
    dk[...] += product(score_grad, q[...], 0, 0) * scale
    dv[...] += product(probs.astype(jnp.bfloat16), do[...], 0, 0)


def attention_specs(rows, keys, size):
    head = pl.BlockSpec((rows, size), lambda h: (0, h))
    whole = lambda *shape: pl.BlockSpec(shape, lambda h: (0, 0))
    masks = [whole(rows, 1), whole(1, keys), whole(rows, 1), whole(1, keys)]
    return head, whole(keys, size), masks


def attend(q, k, v, masks):
    rows, width = q.shape
    keys, size = k.shape
    head, shared, mask_specs = attention_specs(rows, keys, size)
    return pl.pallas_call(
        functools.partial(attend_kernel, size**-0.5),
        grid=(width // size,),
        in_specs=[head, shared, shared, *mask_specs],
        out_specs=(head, head),
        out_shape=(
            jax.ShapeDtypeStruct(q.shape, jnp.bfloat16),
            jax.ShapeDtypeStruct(q.shape, jnp.float32),
        ),
        scratch_shapes=[pltpu.VMEM((rows, keys), jnp.float32)],
        compiler_params=pltpu.CompilerParams(vmem_limit_bytes=32 * 2**20),
        name="attend",
    )(q, k, v, *masks)


def attend_back(q, do, log_total, k, v, masks):
    rows, width = q.shape
    keys, size = k.shape
    head, shared, mask_specs = attention_specs(rows, keys, size)
    grad = jax.ShapeDtypeStruct((keys, size), jnp.float32)
    return pl.pallas_call(
        functools.partial(attend_back_kernel, size**-0.5),
        grid=(width // size,),
        in_specs=[head, head, head, shared, shared, *mask_specs],
        out_specs=(head, shared, shared),
        out_shape=(jax.ShapeDtypeStruct(q.shape, jnp.bfloat16), grad, grad),
        scratch_shapes=[pltpu.VMEM((rows, keys), jnp.float32)],
        compiler_params=pltpu.CompilerParams(vmem_limit_bytes=32 * 2**20),
        name="attend_back",
    )(q, do, log_total, k, v, *masks)


def sum_all_kernel(n_dp, n, x_ref, o_ref, from_z, from_dp, part, s1, r1, s2, r2, s3, r3):
    g, t = lax.axis_index("dp"), lax.axis_index("tensor")
    rows = x_ref.shape[0] // n
    barrier = pltpu.get_barrier_semaphore()
    for k in range(1, n):
        pl.semaphore_signal(
            barrier, inc=1, device_id=(g, lax.rem(t + k, n)), device_id_type=MESH
        )
    for k in range(1, n_dp):
        pl.semaphore_signal(
            barrier, inc=1, device_id=(lax.rem(g + k, n_dp), t), device_id_type=MESH
        )
    pl.semaphore_wait(barrier, n - 1 + n_dp - 1)

    def piece(p):
        return pl.ds(pl.multiple_of(p * rows, rows), rows)

    first = []
    for k in range(1, n):
        p = lax.rem(t + k, n)
        first.append(
            pltpu.make_async_remote_copy(
                x_ref.at[piece(p)],
                from_z.at[k - 1],
                s1.at[k - 1],
                r1.at[k - 1],
                device_id=(g, p),
                device_id_type=MESH,
            )
        )
    for copy in first:
        copy.start()
    for copy in first:
        copy.wait()
    total = x_ref[piece(t)]
    for k in range(1, n):
        total = total + from_z[k - 1]
    part[...] = total
    second = []
    for k in range(1, n_dp):
        second.append(
            pltpu.make_async_remote_copy(
                part,
                from_dp.at[g],
                s2.at[k - 1],
                r2.at[k - 1],
                device_id=(lax.rem(g + k, n_dp), t),
                device_id_type=MESH,
            )
        )
    for copy in second:
        copy.start()
    from_dp[g] = part[...]
    for copy in second:
        copy.wait()
    total = from_dp[0]
    for k in range(1, n_dp):
        total = total + from_dp[k]
    o_ref[piece(t)] = total
    third = []
    for k in range(1, n):
        third.append(
            pltpu.make_async_remote_copy(
                o_ref.at[piece(t)],
                o_ref.at[piece(t)],
                s3.at[k - 1],
                r3.at[k - 1],
                device_id=(g, lax.rem(t + k, n)),
                device_id_type=MESH,
            )
        )
    for copy in third:
        copy.start()
    for copy in third:
        copy.wait()


def sum_all(x, n_dp, n, collective_id):
    rows = x.shape[0] // n
    return pl.pallas_call(
        functools.partial(sum_all_kernel, n_dp, n),
        out_shape=jax.ShapeDtypeStruct(x.shape, x.dtype),
        in_specs=[IN_VMEM],
        out_specs=IN_VMEM,
        scratch_shapes=[
            pltpu.VMEM((n - 1, rows, 128), x.dtype),
            pltpu.VMEM((n_dp, rows, 128), x.dtype),
            pltpu.VMEM((rows, 128), x.dtype),
        ]
        + [DMA((n - 1,))] * 2
        + [DMA((n_dp - 1,))] * 2
        + [DMA((n - 1,))] * 2,
        compiler_params=pltpu.CompilerParams(collective_id=collective_id, has_side_effects=True),
        name="sum_all",
    )(x)


def local(
    tokens,
    cotangent,
    lengths,
    counts,
    query_weight,
    query_moment,
    query_square,
    shared_weight,
    shared_moment,
    shared_square,
    project_weight,
    project_moment,
    project_square,
    expand_weight,
    expand_moment,
    expand_square,
    shrink_weight,
    shrink_moment,
    shrink_square,
    vectors_value,
    vectors_moment,
    vectors_square,
):
    device = lax.axis_index("dp")
    n_dp = lax.axis_size("dp")
    t = lax.axis_index("tensor")
    n = lax.axis_size("tensor")
    row_count, width = tokens.shape
    slots = 2 * row_count // n_dp
    part_rows, part_cols = row_count // n, width // n
    send_start = lax.dynamic_index_in_dim(exclusive_sum(counts, 1), device, 0, keepdims=False)
    send_amount = lax.dynamic_index_in_dim(counts, device, 0, keepdims=False)
    recv_start = lax.dynamic_index_in_dim(exclusive_sum(counts, 0), device, 1, keepdims=False)
    recv_amount = lax.dynamic_index_in_dim(counts, device, 1, keepdims=False)
    send_slots = slot_matrix(send_start, send_amount, slots, row_count)
    recv_slots = slot_matrix(recv_start, recv_amount, slots, row_count)

    def low(x):
        return x.astype(jnp.bfloat16)

    def pack(rows, out_slots):
        return low(mul_plain(out_slots, rows)).reshape(n_dp, slots, rows.shape[1])

    def exchange(packed):
        return lax.all_to_all(packed, "dp", split_axis=0, concat_axis=0, tiled=True)

    def unpack(arrived, in_slots):
        return low(mul_left_t(in_slots, arrived.reshape(n_dp * slots, arrived.shape[2])))

    mine_cols = [
        lax.dynamic_slice_in_dim(a, t * part_cols, part_cols, 1) for a in (tokens, cotangent)
    ]
    packed, query_here, project_here, shared_here = lax.optimization_barrier(
        (
            pack(jnp.concatenate(mine_cols, axis=1), send_slots),
            query_weight,
            project_weight,
            shared_weight,
        )
    )
    query_line, project_line, shared_line = gather_lines(
        n_dp, n, low(query_here), low(project_here).T, low(shared_here)
    )
    arrived, query_line, shared_line = lax.optimization_barrier(
        (exchange(packed), query_line, shared_line)
    )
    owned = unpack(arrived, recv_slots)
    owned_rows, owned_grad, query_all, shared_all = rows_and_weights(
        n_dp, n, owned, query_line, shared_line
    )

    head_size = shared_all.shape[1] // 2
    hidden_width = expand_weight.shape[1]
    hidden_total = hidden_width * n
    gain_one = vectors_value[0:width]
    shift_one = vectors_value[width : 2 * width]
    gain_two = vectors_value[2 * width : 3 * width]
    shift_two = vectors_value[3 * width : 4 * width]
    query_bias = vectors_value[4 * width : 5 * width]
    project_bias = vectors_value[5 * width : 6 * width]
    shrink_bias = vectors_value[6 * width : 7 * width]
    expand_bias = lax.dynamic_slice_in_dim(
        vectors_value, 7 * width + t * hidden_width, hidden_width, 0
    )
    value_bias = vectors_value[7 * width + hidden_total : 7 * width + hidden_total + head_size]

    inputs_float = owned_rows.astype(jnp.float32)
    normed_one, norm_one_back = jax.vjp(layer_norm, inputs_float, gain_one, shift_one)
    normed_low = normed_one.astype(jnp.bfloat16)
    queries = (mul_plain(normed_low, query_all) + query_bias).astype(jnp.bfloat16)
    shared_out = mul_plain(normed_low, shared_all) + jnp.concatenate(
        [jnp.zeros((head_size,), jnp.float32), value_bias]
    )
    shared_rows, project_all_t, owned_grad = shared_and_project(
        n_dp, n, owned, low(shared_out), project_line, owned_grad
    )
    window = min(row_count, part_rows + longest)
    window_start = jnp.clip((t + 1) * part_rows - window, 0, row_count - window)
    shared_window = lax.dynamic_slice_in_dim(shared_rows, window_start, window, 0)
    key_rows, value_rows = shared_window[:, :head_size], shared_window[:, head_size:]
    segment, position = segment_ids(lengths[0], row_count)
    masks = (
        lax.dynamic_slice_in_dim(segment, t * part_rows, part_rows, 0)[:, None],
        lax.dynamic_slice_in_dim(segment, window_start, window, 0)[None, :],
        lax.dynamic_slice_in_dim(position, t * part_rows, part_rows, 0)[:, None],
        lax.dynamic_slice_in_dim(position, window_start, window, 0)[None, :],
    )
    heads_out, log_total = attend(queries, key_rows, value_rows, masks)
    hidden_one = inputs_float + (mul_right_t(heads_out, project_all_t) + project_bias)
    normed_two, norm_two_back = jax.vjp(layer_norm, hidden_one, gain_two, shift_two)

    normed_two_low, expand_cols, shrink_rows_t = rows_and_expanded(
        n_dp, n, low(normed_two), low(expand_weight), low(shrink_weight).T
    )
    expand_pre = mul_plain(normed_two_low, expand_cols) + expand_bias
    activated, gelu_back = jax.vjp(gelu_tanh, expand_pre)
    activated_low = activated.astype(jnp.bfloat16)
    skipped = lax.dynamic_update_slice_in_dim(
        jnp.zeros((row_count, width), jnp.float32), hidden_one + shrink_bias, t * part_rows, 0
    )
    result_part = low(mul_right_t(activated_low, shrink_rows_t) + skipped)
    result_part, owned_grad = lax.optimization_barrier((result_part, owned_grad))
    layer_cols = lax.psum_scatter(result_part, "tensor", scatter_dimension=1, tiled=True)
    shrink_grad_t = low(mul_left_t(owned_grad, activated_low))
    activated_grad = mul_plain(owned_grad, shrink_rows_t)
    expand_pre_grad = gelu_back(activated_grad)[0].astype(jnp.bfloat16)
    expand_grad = low(mul_left_t(normed_two_low, expand_pre_grad))
    expand_bias_grad = jnp.sum(expand_pre_grad.astype(jnp.float32), axis=0)
    normed_two_part = mul_right_t(expand_pre_grad, expand_cols).astype(jnp.bfloat16)

    normed_two_grad, expand_part, shrink_part_t = scatter_expanded(
        n_dp, n, normed_two_part, expand_grad, shrink_grad_t
    )
    shrink_part = turned(shrink_part_t)
    output_cols = unpack(exchange(pack(layer_cols, recv_slots)), send_slots)
    output_float = lax.dynamic_slice_in_dim(owned_grad, t * part_rows, part_rows, 0).astype(
        jnp.float32
    )
    shrink_bias_grad = jnp.sum(output_float, axis=0)
    hidden_from_norm, gain_two_grad, shift_two_grad = norm_two_back(normed_two_grad)
    hidden_grad = output_float + hidden_from_norm
    branch_grad = hidden_grad.astype(jnp.bfloat16)
    project_bias_grad = jnp.sum(branch_grad.astype(jnp.float32), axis=0)
    project_grad_t = low(mul_left_t(branch_grad, heads_out))
    heads_grad = low(mul_plain(branch_grad, project_all_t))
    query_grad, key_grad, value_grad = attend_back(
        queries, heads_grad, log_total, key_rows, value_rows, masks
    )
    query_weight_grad = low(mul_left_t(normed_low, query_grad))
    shared_part = lax.dynamic_update_slice_in_dim(
        jnp.zeros((row_count, 2 * head_size), jnp.bfloat16),
        low(jnp.concatenate([key_grad, value_grad], axis=1)),
        window_start,
        0,
    )
    shared_grad, query_sum, project_sum, output_rows = scatter_shared(
        n_dp, n, shared_part, output_cols, query_weight_grad, project_grad_t
    )
    shared_grad = low(shared_grad)
    query_bias_grad = jnp.sum(query_grad.astype(jnp.float32), axis=0)
    normed_one_grad = mul_right_t(query_grad, query_all) + mul_right_t(shared_grad, shared_all)
    inputs_from_norm, gain_one_grad, shift_one_grad = norm_one_back(normed_one_grad)
    input_result = (hidden_grad + inputs_from_norm).astype(jnp.bfloat16)
    shared_weight_grad = mul_left_t(normed_low, shared_grad)
    value_bias_grad = jnp.sum(shared_grad[:, head_size:].astype(jnp.float32), axis=0)

    shared_sum, input_cols = cols_and_shared(n_dp, n, input_result, low(shared_weight_grad))
    packed, query_sum, project_sum, shared_sum = lax.optimization_barrier(
        (pack(input_cols, recv_slots), query_sum, project_sum, shared_sum)
    )
    query_part, project_part_t, shared_piece = scatter_grads(
        n_dp, n, query_sum, project_sum, shared_sum
    )
    project_part = turned(project_part_t)
    arrived, query_part = lax.optimization_barrier((exchange(packed), query_part))
    grad_rows = lax.all_gather(unpack(arrived, send_slots), "tensor", axis=1, tiled=True)
    output_back = output_rows.astype(jnp.float32)
    token_rms = jnp.sqrt(jnp.mean(output_back * output_back, axis=1))

    split_part = lax.dynamic_update_slice_in_dim(
        jnp.zeros((hidden_total,), jnp.float32), expand_bias_grad, t * hidden_width, 0
    )
    vector_part = jnp.concatenate(
        [
            gain_one_grad,
            shift_one_grad,
            gain_two_grad,
            shift_two_grad,
            query_bias_grad,
            project_bias_grad,
            shrink_bias_grad,
            split_part,
            value_bias_grad,
        ]
    )
    local_squares = (
        jnp.sum(query_part * query_part)
        + jnp.sum(expand_part * expand_part)
        + jnp.sum(shared_piece * shared_piece)
        + jnp.sum(project_part * project_part)
        + jnp.sum(shrink_part * shrink_part)
    )
    length = vector_part.shape[0]
    unit = n * 8 * 128
    padded = -(-(length + 1) // unit) * unit
    everything = jnp.concatenate(
        [vector_part, local_squares[None], jnp.zeros((padded - length - 1,), jnp.float32)]
    )
    summed = sum_all(everything.reshape(padded // 128, 128), n_dp, n, 9).reshape(padded)
    vector_grad, weight_squares = summed[:length], summed[length]
    grad_size = jnp.sqrt(weight_squares + jnp.sum(vector_grad * vector_grad))
    clip_factor = jnp.minimum(1.0, clip_level / (grad_size + 1e-06))
    clipped_vectors = clip_factor * vector_grad
    query_new = adamw_step(
        query_weight,
        query_moment,
        query_square,
        clip_factor * query_part,
        rate_matrix * width ** (-0.5),
    )
    shared_new = adamw_step(
        shared_weight,
        shared_moment,
        shared_square,
        clip_factor * shared_piece,
        rate_attention * width ** (-0.5),
    )
    project_new = adamw_step(
        project_weight,
        project_moment,
        project_square,
        clip_factor * project_part,
        rate_attention * width ** (-0.5),
    )
    expand_new = adamw_step(
        expand_weight,
        expand_moment,
        expand_square,
        clip_factor * expand_part,
        rate_matrix * width ** (-0.5),
    )
    shrink_new = adamw_step(
        shrink_weight,
        shrink_moment,
        shrink_square,
        clip_factor * shrink_part,
        rate_matrix * hidden_total ** (-0.5),
    )
    vectors_new = adamw_step(
        vectors_value, vectors_moment, vectors_square, clipped_vectors, rate_vector
    )
    return (
        output_rows,
        grad_rows,
        grad_size,
        *query_new,
        *shared_new,
        *project_new,
        *expand_new,
        *shrink_new,
        *vectors_new,
        clipped_vectors,
        token_rms,
    )


def solution(mesh):
    by_rows = P("dp", None)
    query = P("dp", "tensor")
    shared = P(("dp", "tensor"), None)
    project = P("tensor", "dp")
    return jax.shard_map(
        local,
        mesh=mesh,
        in_specs=(
            *(by_rows,) * 3,
            P(),
            *(query,) * 3,
            *(shared,) * 3,
            *(project,) * 3,
            *(query,) * 3,
            *(project,) * 3,
            *(P(),) * 3,
        ),
        out_specs=(
            *(by_rows,) * 2,
            P(),
            *(query,) * 3,
            *(shared,) * 3,
            *(project,) * 3,
            *(query,) * 3,
            *(project,) * 3,
            *(P(),) * 4,
            P("dp"),
        ),
        check_vma=False,
    )
```

```python
import functools

import jax
import jax.numpy as jnp
from jax import lax
from jax.experimental.layout import Layout, with_layout_constraint
from jax.experimental import pallas as pl
from jax.experimental.pallas import tpu as pltpu
from jax.sharding import PartitionSpec as P

STEP = 10


beta_one = 0.9
beta_two = 0.95
adam_epsilon = 1e-08
decay_rate = 0.1
clip_level = 1.0
norm_epsilon = 1e-05
rate_matrix = 0.6
rate_attention = 2.4
rate_vector = 0.3
masked_score = -1e30
longest = 512

MESH = pl.DeviceIdType.MESH
IN_PLACE = pl.BlockSpec(memory_space=pl.ANY)
IN_VMEM = pl.BlockSpec(memory_space=pltpu.VMEM)
DMA = pltpu.SemaphoreType.DMA
MIB = 2**20


def mul_plain(left, right):
    return jnp.dot(left, right, preferred_element_type=jnp.float32)


def mul_right_t(left, right):
    return lax.dot_general(
        left, right, (((1,), (1,)), ((), ())), preferred_element_type=jnp.float32
    )


def mul_left_t(left, right):
    return lax.dot_general(
        left, right, (((0,), (0,)), ((), ())), preferred_element_type=jnp.float32
    )


def product(left, right, left_dim, right_dim):
    return lax.dot_general(
        left, right, (((left_dim,), (right_dim,)), ((), ())), preferred_element_type=jnp.float32
    )


def layer_norm(values, scaling, offset):
    average = jnp.mean(values, axis=-1, keepdims=True)
    centered = values - average
    variance = jnp.mean(centered * centered, axis=-1, keepdims=True)
    return centered * lax.rsqrt(variance + norm_epsilon) * scaling + offset


def gelu_tanh(values):
    return jax.nn.gelu(values, approximate=True)


def exclusive_sum(table, axis_index):
    return jnp.cumsum(table, axis=axis_index) - table


def segment_ids(seq_lengths, row_count):
    position = jnp.arange(row_count, dtype=jnp.int32)
    starts = jnp.cumsum(seq_lengths) - seq_lengths
    segment = jnp.sum((starts[None, :] <= position[:, None]).astype(jnp.int32), axis=1)
    return (segment, position)


def slot_matrix(starts, amounts, slots, row_count):
    offsets = jnp.arange(slots, dtype=jnp.int32)
    picked = jnp.where(offsets[None, :] < amounts[:, None], starts[:, None] + offsets[None, :], -1)
    position = jnp.arange(row_count, dtype=jnp.int32)
    return (picked.reshape(-1)[:, None] == position[None, :]).astype(jnp.bfloat16)


def turned(x):
    return with_layout_constraint(x.T, Layout(major_to_minor=(0, 1)))


def adamw_step(weight, moment, square, gradient, rate):
    moment_new = beta_one * moment + (1.0 - beta_one) * gradient
    square_new = beta_two * square + (1.0 - beta_two) * gradient * gradient
    moment_hat = moment_new / (1.0 - beta_one**STEP)
    square_hat = square_new / (1.0 - beta_two**STEP)
    weight_new = weight - rate * (
        moment_hat / (jnp.sqrt(square_hat) + adam_epsilon) + decay_rate * weight
    )
    return (weight_new, moment_new, square_new)


def remote(src, dst, send_sem, recv_sem, device):
    return pltpu.make_async_remote_copy(
        src, dst, send_sem, recv_sem, device_id=device, device_id_type=MESH
    )


class Place:
    def __init__(self, n_dp, n):
        self.n, self.chips = n, n_dp // 2
        self.dp, self.t = lax.axis_index("dp"), lax.axis_index("tensor")
        self.core, chip = lax.rem(self.dp, 2), lax.div(self.dp, 2)
        side = round(self.chips**0.5)
        self.side = side if side * side == self.chips else self.chips
        self.pos = self.snake(chip)
        self.sibling = (self.dp + 1 - 2 * self.core, self.t)
        self.after = (self.block(self.ring(self.pos + 1), self.core), self.t)
        self.before = (self.block(self.ring(self.pos - 1), self.core), self.t)
        self.left, self.right = (self.dp, self.t - 1), (self.dp, self.t + 1)

    def snake(self, index):
        row, col = lax.div(index, self.side), lax.rem(index, self.side)
        odd = lax.rem(row, 2)
        return row * self.side + col + odd * (self.side - 1 - 2 * col)

    def ring(self, pos):
        return lax.rem(pos + 2 * self.chips, self.chips)

    def block(self, pos, core):
        return self.snake(pos) * 2 + core

    def greet(self, line=False, line_all=False, ring=False):
        barrier = pltpu.get_barrier_semaphore()
        peers = 0

        def call(device):
            pl.semaphore_signal(barrier, inc=1, device_id=device, device_id_type=MESH)

        if ring:
            for device in (self.sibling, self.after, self.before):
                call(device)
            peers += 3
        if line_all:
            for k in range(1, self.n):
                call((self.dp, lax.rem(self.t + k, self.n)))
            peers += self.n - 1
        elif line:
            pl.when(self.t > 0)(lambda: call(self.left))
            pl.when(self.t < self.n - 1)(lambda: call(self.right))
            peers += (self.t > 0).astype(jnp.int32) + (self.t < self.n - 1).astype(jnp.int32)
        return lambda: pl.semaphore_wait(barrier, peers)


class LineGather:
    @staticmethod
    def sems(n, chunks):
        return [DMA((n - 1, chunks))] * 4 + [DMA]

    def __init__(self, at, chunks, first, place, sems, whole, unit=1.0):
        self.unit = unit
        self.at, self.chunks, self.first, self.place, self.sems = at, chunks, first, place, sems
        self.own = pltpu.make_async_copy(whole[0], whole[1], sems[4])

    def copy(self, h, c, right):
        at = self.at
        dst = self.place(at.t - h if right else at.t + h, c)
        src = self.first(c) if h == 0 else dst
        s, r = self.sems[0:2] if right else self.sems[2:4]
        return remote(src, dst, s.at[h, c], r.at[h, c], at.right if right else at.left)

    def receive(self, h, c, right):
        at = self.at
        dst = self.place(at.t - 1 - h if right else at.t + 1 + h, c)
        s, r = self.sems[0:2] if right else self.sems[2:4]
        remote(dst, dst, s.at[h, c], r.at[h, c], at.left if right else at.right).wait_recv()

    def sends(self, h, right):
        t, n = self.at.t, self.at.n
        return (t >= h) & (t < n - 1) if right else (t + h <= n - 1) & (t > 0)

    def gets(self, h, right):
        return self.at.t - 1 - h >= 0 if right else self.at.t + 1 + h <= self.at.n - 1

    def every(self):
        for h in range(self.at.n - 1):
            for c in range(self.chunks):
                for right in (True, False):
                    yield h, c, right

    def prepare(self):
        self.own.start()

    def prepared(self):
        self.own.wait()

    def start(self):
        for h, c, right in self.every():
            if h == 0:
                pl.when(self.sends(h, right))(lambda: self.copy(h, c, right).start())

    def step(self, h, c, right):
        pl.when(self.gets(h, right))(lambda: self.receive(h, c, right))
        if h + 1 < self.at.n - 1:
            pl.when(self.sends(h + 1, right))(lambda: self.copy(h + 1, c, right).start())

    def steps(self):
        return [
            (self.unit * (which[0] + (which[1] + 1) / self.chunks), functools.partial(self.step, *which))
            for which in self.every()
        ]

    def finish(self):
        for h, c, right in self.every():
            pl.when(self.sends(h, right))(lambda: self.copy(h, c, right).wait_send())


class LineScatter:
    @staticmethod
    def scratch(n, chunks, block, dtype):
        return [pltpu.VMEM((n - 1, *block), dtype)] * 2 + [DMA((n - 1, chunks))] * 4

    def __init__(self, at, chunks, own, out, scratch, unit=1.0):
        self.unit = unit
        self.at, self.chunks, self.own, self.out = at, chunks, own, out
        self.held, self.sems = scratch[:2], scratch[2:6]
        self.rows = self.held[0].shape[1] // chunks

    def parts(self, k, c, right):
        side = 0 if right else 1
        s, r = self.sems[2 * side : 2 * side + 2]
        return self.held[side].at[k, pl.ds(c * self.rows, self.rows)], s.at[k, c], r.at[k, c]

    def send(self, k, c, right, first):
        slot, s, r = self.parts(k, c, right)
        src = self.own(self.target(k, right), c) if first else slot
        return remote(src, slot, s, r, self.at.right if right else self.at.left)

    def receive(self, k, c, right):
        slot, s, r = self.parts(k, c, right)
        remote(slot, slot, s, r, self.at.left if right else self.at.right).wait_recv()

    def target(self, k, right):
        return self.at.n - 1 - k if right else k

    def every(self):
        for k in range(self.at.n - 1):
            for c in range(self.chunks):
                for right in (True, False):
                    yield k, c, right

    def prepare(self):
        pass

    def prepared(self):
        pass

    def start(self):
        t, n = self.at.t, self.at.n
        for k, c, right in self.every():
            first = (t == (0 if right else n - 1)) & (t != self.target(k, right))
            pl.when(first)(lambda: self.send(k, c, right, True).start())

    def add(self, k, c, right):
        self.receive(k, c, right)
        slot = self.parts(k, c, right)[0]
        mine = self.own(self.target(k, right), c)[...]
        slot[...] = (slot[...].astype(jnp.float32) + mine.astype(jnp.float32)).astype(slot.dtype)
        self.send(k, c, right, False).start()

    def step(self, k, c, right):
        t, n, d = self.at.t, self.at.n, self.target(k, right)
        passes = (t > 0) & (t < d) if right else (t < n - 1) & (t > d)
        pl.when(passes)(lambda: self.add(k, c, right))

    def steps(self):
        return [
            (self.unit * (which[0] + (which[1] + 1) / self.chunks), functools.partial(self.step, *which))
            for which in self.every()
        ]

    def finish(self):
        t, n = self.at.t, self.at.n
        for k, c, right in self.every():
            pl.when(t == self.target(k, right))(lambda: self.receive(k, c, right))
        for c in range(self.chunks):
            span = pl.ds(c * self.rows, self.rows)
            self.out[span] = self.own(t, c)[...].astype(self.out.dtype)

        def more(block):
            self.out[...] += block[...].astype(self.out.dtype)

        pl.when(t > 0)(lambda: more(self.held[0].at[n - 1 - t]))
        pl.when(t < n - 1)(lambda: more(self.held[1].at[t]))
        for k, c, right in self.every():
            d = self.target(k, right)
            pl.when(t < d if right else t > d)(lambda: self.send(k, c, right, False).wait_send())


class LineExchange:
    @staticmethod
    def scratch(n, block, dtype):
        return [pltpu.VMEM((n - 1, *block), dtype)] + [DMA((n - 1,))] * 2

    def __init__(self, at, source, out, scratch):
        self.at, self.source, self.out = at, source, out
        self.held = scratch[0]
        self.copies = []
        for k in range(1, at.n):
            p = lax.rem(at.t + k, at.n)
            self.copies.append(
                remote(
                    source(p),
                    self.held.at[k - 1],
                    scratch[1].at[k - 1],
                    scratch[2].at[k - 1],
                    (at.dp, p),
                )
            )

    def prepare(self):
        pass

    def prepared(self):
        pass

    def start(self):
        for copy in self.copies:
            copy.start()

    def steps(self):
        return []

    def finish(self):
        for copy in self.copies:
            copy.wait()
        total = self.source(self.at.t)[...].astype(jnp.float32)
        for k in range(self.at.n - 1):
            total = total + self.held[k].astype(jnp.float32)
        self.out[...] = total.astype(self.out.dtype)


class RingGather:
    @staticmethod
    def sems(chips, chunks):
        hops = chips // 2
        return [DMA((2, hops, chunks))] * 4 + [DMA((chunks,))] * 2 + [DMA]

    def __init__(self, at, chunks, first, place, sems, whole, unit=1.0):
        self.unit = unit
        self.at, self.chunks, self.first, self.place, self.sems = at, chunks, first, place, sems
        self.hops = at.chips // 2
        self.own = pltpu.make_async_copy(whole[0], whole[1], sems[6])

    def every(self):
        for h in range(self.hops):
            for c in range(self.chunks):
                for way in (0, 1):
                    if h < self.hops - 1 or c % 2 == way:
                        yield h, c, way

    def origin(self, steps, way, core):
        return self.at.block(self.at.ring(self.at.pos + (steps if way else -steps)), core)

    def onward(self, h, c, way):
        dst = self.place(self.origin(h, way, self.at.core), c)
        src = self.first(c) if h == 0 else dst
        s, r = self.sems[0:2]
        device = self.at.before if way else self.at.after
        return remote(src, dst, s.at[way, h, c], r.at[way, h, c], device)

    def arrival(self, h, c, way):
        dst = self.place(self.origin(h + 1, way, self.at.core), c)
        s, r = self.sems[0:2]
        device = self.at.after if way else self.at.before
        return remote(dst, dst, s.at[way, h, c], r.at[way, h, c], device)

    def across(self, h, c, way, core):
        dst = self.place(self.origin(h + 1, way, core), c)
        s, r = self.sems[2:4]
        return remote(dst, dst, s.at[way, h, c], r.at[way, h, c], self.at.sibling)

    def across_own(self, c, core):
        dst = self.place(self.origin(0, 0, core), c)
        s, r = self.sems[4:6]
        return remote(self.first(c), dst, s.at[c], r.at[c], self.at.sibling)

    def prepare(self):
        self.own.start()

    def prepared(self):
        self.own.wait()

    def start(self):
        for h, c, way in self.every():
            if h == 0:
                self.onward(h, c, way).start()
        for c in range(self.chunks):
            self.across_own(c, self.at.core).start()

    def step(self, h, c, way):
        self.arrival(h, c, way).wait_recv()
        if (h + 1, c, way) in list(self.every()):
            self.onward(h + 1, c, way).start()
        self.across(h, c, way, self.at.core).start()

    def steps(self):
        when = 0.0
        for h, c, way in self.every():
            when += self.unit / self.chunks / 2
            yield when, functools.partial(self.step, h, c, way)

    def finish(self):
        other = 1 - self.at.core
        for c in range(self.chunks):
            self.across_own(c, other).wait_recv()
            self.across_own(c, self.at.core).wait_send()
        for h, c, way in self.every():
            self.across(h, c, way, other).wait_recv()
            self.across(h, c, way, self.at.core).wait_send()
            self.onward(h, c, way).wait_send()


class RingScatter:
    @staticmethod
    def scratch(chips, chunks, block, dtype):
        hops = chips // 2
        return (
            [pltpu.VMEM((chips, *block), dtype)] * 2
            + [pltpu.VMEM((2, hops, *block), dtype)]
            + [DMA((chips, chunks))] * 3
            + [DMA((2, hops, chunks))] * 2
        )

    def __init__(self, at, chunks, source, out, scratch, unit=1.0):
        self.unit = unit
        self.at, self.chunks, self.source, self.out = at, chunks, source, out
        self.hops = at.chips // 2
        self.mine, self.other, self.held = scratch[:3]
        self.load_sem, self.s1, self.r1, self.s2, self.r2 = scratch[3:8]
        self.rows = self.held.shape[2] // chunks

    def span(self, c):
        return pl.ds(c * self.rows, self.rows)

    def target(self, place, core):
        return self.at.block(self.at.ring(self.at.pos + place), core)

    def load(self, place, c):
        src = self.source(self.target(place, self.at.core), c)
        dst = self.mine.at[place, self.span(c)]
        return pltpu.make_async_copy(src, dst, self.load_sem.at[place, c])

    def across(self, place, c):
        src = self.source(self.target(place, 1 - self.at.core), c)
        dst = self.other.at[place, self.span(c)]
        return remote(src, dst, self.s1.at[place, c], self.r1.at[place, c], self.at.sibling)

    def sent(self, e, c, way):
        return e < self.hops or c % 2 == way

    def onward(self, e, c, way):
        place = self.at.chips - e if way else e
        src, dst = self.mine.at[place, self.span(c)], self.held.at[way, e - 1, self.span(c)]
        device = self.at.before if way else self.at.after
        return remote(src, dst, self.s2.at[way, e - 1, c], self.r2.at[way, e - 1, c], device)

    def arrival(self, e, c, way):
        dst = self.held.at[way, e, self.span(c)]
        device = self.at.after if way else self.at.before
        return remote(dst, dst, self.s2.at[way, e, c], self.r2.at[way, e, c], device)

    def places(self):
        order = []
        for e in range(self.hops, 0, -1):
            order += [e] if e == self.hops else [e, self.at.chips - e]
        return order + [0]

    def prepare(self):
        for place in self.places():
            for c in range(self.chunks):
                self.load(place, c).start()

    def prepared(self):
        for place in self.places():
            for c in range(self.chunks):
                self.load(place, c).wait()

    def start(self):
        for place in self.places():
            for c in range(self.chunks):
                self.across(place, c).start()

    def base(self, place, c):
        self.across(place, c).wait_recv()
        total = self.mine[place, self.span(c)].astype(jnp.float32)
        return total + self.other[place, self.span(c)].astype(jnp.float32)

    def arrived(self, e, c, way):
        self.arrival(e, c, way).wait_recv()
        return self.held[way, e, self.span(c)].astype(jnp.float32)

    def step(self, e, c, way):
        place = self.at.chips - e if way else e
        total = self.base(place, c)
        if e < self.hops and self.sent(e + 1, c, way):
            total += self.arrived(e, c, way)
        self.mine[place, self.span(c)] = total.astype(self.mine.dtype)
        self.onward(e, c, way).start()

    def last(self, c):
        total = self.base(0, c)
        for way in (0, 1):
            if self.sent(1, c, way):
                total += self.arrived(0, c, way)
        self.out[self.span(c)] = total.astype(self.out.dtype)

    def every(self):
        for e in range(self.hops, 0, -1):
            for c in range(self.chunks):
                for way in (0, 1):
                    if self.sent(e, c, way):
                        yield e, c, way

    def steps(self):
        when = 0.0
        for e, c, way in self.every():
            yield when, functools.partial(self.step, e, c, way)
            when += self.unit / self.chunks / 2
        for c in range(self.chunks):
            yield when + self.unit * (c + 1) / self.chunks, functools.partial(self.last, c)

    def finish(self):
        for place in self.places():
            for c in range(self.chunks):
                self.across(place, c).wait_send()
        for e, c, way in self.every():
            self.onward(e, c, way).wait_send()


class ProductScatter(RingScatter):
    @staticmethod
    def scratch(chips, chunks, block, dtype):
        return RingScatter.scratch(chips, chunks, block, dtype) + [pltpu.VMEM((2, *block), dtype)]

    def __init__(self, at, chunks, left, right, out, scratch, unit, cost):
        super().__init__(at, chunks, None, out, scratch[:-1], unit)
        self.left, self.right, self.stage, self.cost = left, right, scratch[-1], cost

    def across(self, place, c):
        src = self.stage.at[self.places().index(place) % 2, self.span(c)]
        dst = self.other.at[place, self.span(c)]
        return remote(src, dst, self.s1.at[place, c], self.r1.at[place, c], self.at.sibling)

    def product(self, place, core):
        block = self.held.shape[2]
        cols = lanes(self.target(place, core), block) if block % 128 == 0 else None
        if cols is None:
            left = self.left[pl.ds(pl.multiple_of(self.target(place, core) * block, block), block)]
            total = product(left, self.right[...], 1, 0)
        else:
            total = product(self.left[:, cols], self.right[...], 0, 0)
        return total.astype(self.mine.dtype)

    def work(self, i, place, here):
        if here:
            self.mine[place] = self.product(place, self.at.core)
            return
        if i >= 2:
            for c in range(self.chunks):
                self.across(self.places()[i - 2], c).wait_send()
        self.stage[i % 2] = self.product(place, 1 - self.at.core)
        for c in range(self.chunks):
            self.across(place, c).start()

    def prepare(self):
        pass

    def prepared(self):
        pass

    def start(self):
        pass

    def steps(self):
        when = 0.0
        for i, place in enumerate(self.places()):
            for here in (False, True):
                yield when, functools.partial(self.work, i, place, here)
                when += self.cost
        for when, step in super().steps():
            place = 0
            if len(step.args) == 3:
                e, _, way = step.args
                place = self.at.chips - e if way else e
            yield max(when, (2 * self.places().index(place) + 2) * self.cost), step

    def finish(self):
        for place in self.places()[-2:]:
            for c in range(self.chunks):
                self.across(place, c).wait_send()
        for e, c, way in self.every():
            self.onward(e, c, way).wait_send()


class LineSwitch:
    @staticmethod
    def sems(n):
        return [DMA((n - 1,))] * 2 + [DMA]

    def __init__(self, at, source, target, sems):
        self.own = pltpu.make_async_copy(source(at.t), target, sems[2])
        self.copies = []
        for k in range(1, at.n):
            p = lax.rem(at.t + k, at.n)
            self.copies.append(
                remote(source(p), target, sems[0].at[k - 1], sems[1].at[k - 1], (at.dp, p))
            )

    def prepare(self):
        self.own.start()

    def prepared(self):
        self.own.wait()

    def start(self):
        for copy in self.copies:
            copy.start()

    def steps(self):
        return []

    def finish(self):
        for copy in self.copies:
            copy.wait()


def run_jobs(met, jobs):
    for job in jobs:
        job.prepare()
    for job in jobs:
        job.prepared()
    met()
    for job in jobs:
        job.start()
    ordered = []
    for i, job in enumerate(jobs):
        ordered += [(when, i, j, step) for j, (when, step) in enumerate(job.steps())]
    for _, _, _, step in sorted(ordered, key=lambda entry: entry[:3]):
        step()
    for job in jobs:
        job.finish()


def rows_of(ref, step):
    return lambda c: ref.at[pl.ds(c * step, step)]


def lanes(index, count):
    return pl.ds(pl.multiple_of(index * count, count), count)


def move(kernel, inputs, in_vmem, outs, out_vmem, scratch, collective_id, name, aliases=None):
    return pl.pallas_call(
        kernel,
        out_shape=tuple(outs),
        in_specs=[IN_VMEM if i < in_vmem else IN_PLACE for i in range(len(inputs))],
        out_specs=tuple(IN_VMEM if i < out_vmem else IN_PLACE for i in range(len(outs))),
        scratch_shapes=scratch,
        compiler_params=pltpu.CompilerParams(
            collective_id=collective_id, has_side_effects=True, vmem_limit_bytes=56 * MIB
        ),
        input_output_aliases=aliases or {},
        name=name,
    )(*inputs)


def line_gather(at, x, out, axis, chunks, sems, unit=1.0):
    rows, cols = x.shape
    step = rows // chunks
    if axis == 0:
        place = lambda b, c: out.at[pl.ds(b * rows + c * step, step)]
        whole = out.at[pl.ds(at.t * rows, rows)]
    else:
        place = lambda b, c: out.at[pl.ds(c * step, step), lanes(b, cols)]
        whole = out.at[:, lanes(at.t, cols)]
    return LineGather(at, chunks, rows_of(x, step), place, sems, (x, whole), unit)


def ring_gather(at, x, out, axis, chunks, sems, unit=1.0):
    rows, cols = x.shape
    step = rows // chunks
    if axis == 0:
        place = lambda b, c: out.at[pl.ds(b * rows + c * step, step)]
        whole = out.at[pl.ds(at.dp * rows, rows)]
    else:
        place = lambda b, c: out.at[pl.ds(c * step, step), lanes(b, cols)]
        whole = out.at[:, lanes(at.dp, cols)]
    return RingGather(at, chunks, rows_of(x, step), place, sems, (x, whole), unit)


def blocks_of(x, out, axis, chunks):
    rows, cols = out.shape
    step = rows // chunks
    if axis == 0:
        return lambda b, c: x.at[pl.ds(pl.multiple_of(b * rows + c * step, step), step)]
    return lambda b, c: x.at[pl.ds(c * step, step), lanes(b, cols)]


def line_exchange(at, x, out, axis, scratch):
    block = blocks_of(x, out, axis, 1)
    return LineExchange(at, lambda p: block(p, 0), out, scratch)


def line_scatter(at, x, out, axis, chunks, scratch, unit=1.0):
    return LineScatter(at, chunks, blocks_of(x, out, axis, chunks), out, scratch, unit)


def ring_scatter(at, x, out, axis, chunks, scratch, unit=1.0):
    return RingScatter(at, chunks, blocks_of(x, out, axis, chunks), out, scratch, unit)


def product_scatter(at, left, right, out, chunks, scratch, unit, cost):
    return ProductScatter(at, chunks, left, right, out, scratch, unit, cost)


def by_lanes(left, n_dp):
    return left if left.shape[1] // n_dp % 128 == 0 else left.T


def like(x, rows, cols, dtype=None):
    return jax.ShapeDtypeStruct((x.shape[0] * rows, x.shape[1] * cols), dtype or x.dtype)


class Parts:
    def __init__(self, refs):
        self.refs = list(refs)

    def take(self, shapes):
        taken, self.refs = self.refs[: len(shapes)], self.refs[len(shapes) :]
        return taken


def gather_lines(n_dp, n, query, project, shared):
    sems = LineGather.sems(n, 1)

    def kernel(a, b, c, a_out, b_out, c_out, *refs):
        parts = Parts(refs)
        at = Place(n_dp, n)
        run_jobs(
            at.greet(line=True),
            [
                line_gather(at, a, a_out, 1, 1, parts.take(sems), 6.0),
                line_gather(at, c, c_out, 0, 1, parts.take(sems), 6.5),
                line_gather(at, b, b_out, 1, 1, parts.take(sems), 12.0),
            ],
        )

    return move(
        kernel,
        (query, project, shared),
        3,
        (like(query, 1, n), like(project, 1, n), like(shared, n, 1)),
        0,
        sems * 3,
        1,
        "gather_lines",
    )


def rows_and_weights(n_dp, n, owned, query, shared):
    chips, chunks = n_dp // 2, 2
    total, cols = owned.shape[0], owned.shape[1] // 2
    rows, half = total // n, total // 2
    switch, line = LineSwitch.sems(n), LineGather.sems(n, chunks)
    ring = RingGather.sems(chips, chunks)

    def kernel(x, a, b, x_out, y_out, a_out, b_out, *refs):
        parts = Parts(refs)
        at = Place(n_dp, n)
        run_jobs(
            at.greet(line_all=True, ring=True),
            [
                LineSwitch(
                    at,
                    lambda p: x.at[pl.ds(pl.multiple_of(p * rows, rows), rows), pl.ds(0, cols)],
                    x_out.at[:, lanes(at.t, cols)],
                    parts.take(switch),
                ),
                ring_gather(at, b, b_out, 0, chunks, parts.take(ring), 4.0),
                ring_gather(at, a, a_out, 0, chunks, parts.take(ring), 22.0),
                line_gather(
                    at,
                    x.at[pl.ds(0, half), pl.ds(cols, cols)],
                    y_out.at[pl.ds(0, half)],
                    1,
                    chunks,
                    parts.take(line),
                    16.0,
                ),
            ],
        )

    return move(
        kernel,
        (owned, query, shared),
        3,
        (
            jax.ShapeDtypeStruct((rows, n * cols), owned.dtype),
            jax.ShapeDtypeStruct((total, n * cols), owned.dtype),
            like(query, n_dp, 1),
            like(shared, n_dp, 1),
        ),
        0,
        switch + ring * 2 + line,
        2,
        "rows_and_weights",
    )


def shared_and_project(n_dp, n, owned, shared_rows, project, gathered):
    chips, chunks = n_dp // 2, 2
    total, cols = owned.shape[0], owned.shape[1] // 2
    half = total // 2
    small, line = LineGather.sems(n, 1), LineGather.sems(n, chunks)
    ring = RingGather.sems(chips, chunks)

    def kernel(y, x, a, _, x_out, a_out, y_out, *refs):
        parts = Parts(refs)
        at = Place(n_dp, n)
        lower = pl.ds(half, half)
        run_jobs(
            at.greet(line=True, ring=True),
            [
                line_gather(at, x, x_out, 0, 1, parts.take(small), 4.0),
                ring_gather(at, a, a_out, 0, chunks, parts.take(ring), 22.0),
                line_gather(
                    at,
                    y.at[lower, pl.ds(cols, cols)],
                    y_out.at[lower],
                    1,
                    chunks,
                    parts.take(line),
                    13.0,
                ),
            ],
        )

    return move(
        kernel,
        (owned, shared_rows, project, gathered),
        3,
        (like(shared_rows, n, 1), like(project, n_dp, 1), like(gathered, 1, 1)),
        0,
        small + ring + line,
        3,
        "shared_and_project",
        {3: 2},
    )


def rows_and_expanded(n_dp, n, x, expand, shrink):
    chips, chunks, halves = n_dp // 2, 4, 2
    line, ring = LineGather.sems(n, chunks), RingGather.sems(chips, halves)

    def kernel(x_ref, a, b, x_out, a_out, b_out, *refs):
        parts = Parts(refs)
        at = Place(n_dp, n)
        run_jobs(
            at.greet(line=True, ring=True),
            [
                line_gather(at, x_ref, x_out, 0, chunks, parts.take(line), 22.0),
                ring_gather(at, a, a_out, 0, halves, parts.take(ring), 44.0),
                ring_gather(at, b, b_out, 0, halves, parts.take(ring), 44.0),
            ],
        )

    return move(
        kernel,
        (x, expand, shrink),
        3,
        (like(x, n, 1), like(expand, n_dp, 1), like(shrink, n_dp, 1)),
        0,
        line + ring * 2,
        4,
        "rows_and_expanded",
    )


def scatter_expanded(n_dp, n, x, expand, shrink):
    chips, chunks = n_dp // 2, 4
    block = (x.shape[0] // n, x.shape[1])
    w_block = (expand.shape[0] // n_dp, expand.shape[1])
    line = LineScatter.scratch(n, chunks, block, x.dtype)
    ring = RingScatter.scratch(chips, chunks, w_block, x.dtype)

    def kernel(x_ref, a, b, x_out, a_out, b_out, *refs):
        parts = Parts(refs)
        at = Place(n_dp, n)
        run_jobs(
            at.greet(line=True, ring=True),
            [
                line_scatter(at, x_ref, x_out, 0, chunks, parts.take(line), 26.0),
                ring_scatter(at, a, a_out, 0, chunks, parts.take(ring), 22.0),
                ring_scatter(at, b, b_out, 0, chunks, parts.take(ring), 22.0),
            ],
        )

    return move(
        kernel,
        (x, expand, shrink),
        1,
        [jax.ShapeDtypeStruct(shape, jnp.float32) for shape in (block, w_block, w_block)],
        3,
        line + ring * 2,
        5,
        "scatter_expanded",
    )


def scatter_shared(n_dp, n, x, result, a, dq, dz, o):
    chips, chunks = n_dp // 2, 4
    block = (x.shape[0] // n, x.shape[1])
    w_block = (a.shape[1] // n_dp, dq.shape[1])
    small = LineExchange.scratch(n, block, x.dtype)
    line = LineGather.sems(n, chunks)
    ring = ProductScatter.scratch(chips, chunks, w_block, x.dtype)

    def kernel(x_ref, y, a_ref, dq_ref, dz_ref, o_ref, x_out, a_out, b_out, y_out, *refs):
        parts = Parts(refs)
        at = Place(n_dp, n)
        run_jobs(
            at.greet(line_all=True, ring=True),
            [
                line_exchange(at, x_ref, x_out, 0, parts.take(small)),
                line_gather(at, y, y_out, 1, chunks, parts.take(line), 22.0),
                product_scatter(at, dz_ref, o_ref, b_out, chunks, parts.take(ring), 24.0, 1.0),
                product_scatter(at, a_ref, dq_ref, a_out, chunks, parts.take(ring), 24.0, 1.0),
            ],
        )

    return move(
        kernel,
        (x, result, by_lanes(a, n_dp), dq, by_lanes(dz, n_dp), o),
        6,
        (
            jax.ShapeDtypeStruct(block, jnp.float32),
            jax.ShapeDtypeStruct(w_block, x.dtype),
            jax.ShapeDtypeStruct(w_block, x.dtype),
            like(result, 1, n),
        ),
        3,
        small + line + ring * 2,
        6,
        "scatter_shared",
    )


def cols_and_shared(n_dp, n, rows, shared):
    chips = n_dp // 2
    count, width = rows.shape
    cols = width // n
    s_block = (shared.shape[0] // n_dp, shared.shape[1])
    switch = LineSwitch.sems(n)
    ring = RingScatter.scratch(chips, 1, s_block, shared.dtype)

    def kernel(x, c, c_out, x_out, *refs):
        parts = Parts(refs)
        at = Place(n_dp, n)
        run_jobs(
            at.greet(line_all=True, ring=True),
            [
                LineSwitch(
                    at,
                    lambda p: x.at[:, lanes(p, cols)],
                    x_out.at[pl.ds(at.t * count, count)],
                    parts.take(switch),
                ),
                ring_scatter(at, c, c_out, 0, 1, parts.take(ring), 4.0),
            ],
        )

    return move(
        kernel,
        (rows, shared),
        1,
        [
            jax.ShapeDtypeStruct(s_block, shared.dtype),
            jax.ShapeDtypeStruct((n * count, cols), rows.dtype),
        ],
        1,
        switch + ring,
        7,
        "cols_and_shared",
    )


def scatter_grads(n_dp, n, query, project, shared):
    w_block = (query.shape[0], query.shape[1] // n)
    s_block = (shared.shape[0] // n, shared.shape[1])
    line = LineScatter.scratch(n, 1, w_block, query.dtype)
    small = LineExchange.scratch(n, s_block, shared.dtype)

    def kernel(a, b, c, a_out, b_out, c_out, *refs):
        parts = Parts(refs)
        at = Place(n_dp, n)
        run_jobs(
            at.greet(line_all=True),
            [
                line_scatter(at, a, a_out, 1, 1, parts.take(line), 12.0),
                line_scatter(at, b, b_out, 1, 1, parts.take(line), 12.0),
                line_exchange(at, c, c_out, 0, parts.take(small)),
            ],
        )

    return move(
        kernel,
        (query, project, shared),
        3,
        [jax.ShapeDtypeStruct(block, jnp.float32) for block in (w_block, w_block, s_block)],
        3,
        line * 2 + small,
        8,
        "scatter_grads",
    )


def fill_bias(bias, seg_row, seg_col, pos_row, pos_col):
    @pl.when(pl.program_id(0) == 0)
    def _():
        allowed = (seg_row[...] == seg_col[...]) & (pos_row[...] >= pos_col[...])
        bias[...] = jnp.where(allowed, 0.0, masked_score)


def attend_kernel(scale, q, k, v, seg_row, seg_col, pos_row, pos_col, o, log_total, bias):
    fill_bias(bias, seg_row, seg_col, pos_row, pos_col)
    scores = product(q[...], k[...], 1, 1) * scale + bias[...]
    row_max = jnp.max(scores, axis=1, keepdims=True)
    expo = jnp.exp(scores - row_max)
    row_total = jnp.sum(expo, axis=1, keepdims=True)
    probs = (expo / row_total).astype(jnp.bfloat16)
    o[...] = product(probs, v[...], 1, 0).astype(jnp.bfloat16)
    log_total[...] = jnp.broadcast_to(row_max + jnp.log(row_total), log_total.shape)


def attend_back_kernel(
    scale, q, do, log_total, k, v, seg_row, seg_col, pos_row, pos_col, dq, dkv, bias, dk, dv
):
    fill_bias(bias, seg_row, seg_col, pos_row, pos_col)

    @pl.when(pl.program_id(0) == 0)
    def _():
        dk[...] = jnp.zeros_like(dk)
        dv[...] = jnp.zeros_like(dv)

    scores = product(q[...], k[...], 1, 1) * scale + bias[...]
    probs = jnp.exp(scores - log_total[:, :1])
    prob_grad = product(do[...], v[...], 1, 1)
    inner = jnp.sum(probs * prob_grad, axis=1, keepdims=True)
    score_grad = (probs * (prob_grad - inner)).astype(jnp.bfloat16)
    dq[...] = (product(score_grad, k[...], 1, 0) * scale).astype(jnp.bfloat16)
    dk[...] += product(score_grad, q[...], 0, 0) * scale
    dv[...] += product(probs.astype(jnp.bfloat16), do[...], 0, 0)

    @pl.when(pl.program_id(0) == pl.num_programs(0) - 1)
    def _():
        dkv[...] = jnp.zeros_like(dkv)
        rows, (keys, size) = q.shape[0], k.shape
        last = (lax.axis_index("tensor") + 1) * rows
        window = pl.ds(pl.multiple_of(jnp.maximum(last - keys, 0), rows), keys)
        dkv[window, pl.ds(0, size)] = dk[...].astype(dkv.dtype)
        dkv[window, pl.ds(size, size)] = dv[...].astype(dkv.dtype)


def attention_specs(rows, keys, size):
    head = pl.BlockSpec((rows, size), lambda h: (0, h))
    whole = lambda *shape: pl.BlockSpec(shape, lambda h: (0, 0))
    masks = [whole(rows, 1), whole(1, keys), whole(rows, 1), whole(1, keys)]
    return head, whole(keys, size), masks


def attend(q, k, v, masks):
    rows, width = q.shape
    keys, size = k.shape
    head, shared, mask_specs = attention_specs(rows, keys, size)
    return pl.pallas_call(
        functools.partial(attend_kernel, size**-0.5),
        grid=(width // size,),
        in_specs=[head, shared, shared, *mask_specs],
        out_specs=(head, head),
        out_shape=(
            jax.ShapeDtypeStruct(q.shape, jnp.bfloat16),
            jax.ShapeDtypeStruct(q.shape, jnp.float32),
        ),
        scratch_shapes=[pltpu.VMEM((rows, keys), jnp.float32)],
        compiler_params=pltpu.CompilerParams(vmem_limit_bytes=32 * MIB),
        name="attend",
    )(q, k, v, *masks)


def attend_back(q, do, log_total, k, v, masks, total):
    rows, width = q.shape
    keys, size = k.shape
    head, shared, mask_specs = attention_specs(rows, keys, size)
    return pl.pallas_call(
        functools.partial(attend_back_kernel, size**-0.5),
        grid=(width // size,),
        in_specs=[head, head, head, shared, shared, *mask_specs],
        out_specs=(head, pl.BlockSpec((total, 2 * size), lambda h: (0, 0))),
        out_shape=(
            jax.ShapeDtypeStruct(q.shape, jnp.bfloat16),
            jax.ShapeDtypeStruct((total, 2 * size), jnp.bfloat16),
        ),
        scratch_shapes=[
            pltpu.VMEM((rows, keys), jnp.float32),
            pltpu.VMEM((keys, size), jnp.float32),
            pltpu.VMEM((keys, size), jnp.float32),
        ],
        compiler_params=pltpu.CompilerParams(vmem_limit_bytes=32 * MIB),
        name="attend_back",
    )(q, do, log_total, k, v, *masks)


def sum_all_kernel(n_dp, n, x_ref, o_ref, from_z, from_dp, part, s1, r1, s2, r2, s3, r3):
    g, t = lax.axis_index("dp"), lax.axis_index("tensor")
    rows = x_ref.shape[0] // n
    barrier = pltpu.get_barrier_semaphore()
    for k in range(1, n):
        pl.semaphore_signal(
            barrier, inc=1, device_id=(g, lax.rem(t + k, n)), device_id_type=MESH
        )
    for k in range(1, n_dp):
        pl.semaphore_signal(
            barrier, inc=1, device_id=(lax.rem(g + k, n_dp), t), device_id_type=MESH
        )
    pl.semaphore_wait(barrier, n - 1 + n_dp - 1)

    def piece(p):
        return pl.ds(pl.multiple_of(p * rows, rows), rows)

    first = []
    for k in range(1, n):
        p = lax.rem(t + k, n)
        first.append(
            pltpu.make_async_remote_copy(
                x_ref.at[piece(p)],
                from_z.at[k - 1],
                s1.at[k - 1],
                r1.at[k - 1],
                device_id=(g, p),
                device_id_type=MESH,
            )
        )
    for copy in first:
        copy.start()
    for copy in first:
        copy.wait()
    total = x_ref[piece(t)]
    for k in range(1, n):
        total = total + from_z[k - 1]
    part[...] = total
    second = []
    for k in range(1, n_dp):
        second.append(
            pltpu.make_async_remote_copy(
                part,
                from_dp.at[g],
                s2.at[k - 1],
                r2.at[k - 1],
                device_id=(lax.rem(g + k, n_dp), t),
                device_id_type=MESH,
            )
        )
    for copy in second:
        copy.start()
    from_dp[g] = part[...]
    for copy in second:
        copy.wait()
    total = from_dp[0]
    for k in range(1, n_dp):
        total = total + from_dp[k]
    o_ref[piece(t)] = total
    third = []
    for k in range(1, n):
        third.append(
            pltpu.make_async_remote_copy(
                o_ref.at[piece(t)],
                o_ref.at[piece(t)],
                s3.at[k - 1],
                r3.at[k - 1],
                device_id=(g, lax.rem(t + k, n)),
                device_id_type=MESH,
            )
        )
    for copy in third:
        copy.start()
    for copy in third:
        copy.wait()


def sum_all(x, n_dp, n, collective_id):
    rows = x.shape[0] // n
    return pl.pallas_call(
        functools.partial(sum_all_kernel, n_dp, n),
        out_shape=jax.ShapeDtypeStruct(x.shape, x.dtype),
        in_specs=[IN_VMEM],
        out_specs=IN_VMEM,
        scratch_shapes=[
            pltpu.VMEM((n - 1, rows, 128), x.dtype),
            pltpu.VMEM((n_dp, rows, 128), x.dtype),
            pltpu.VMEM((rows, 128), x.dtype),
        ]
        + [DMA((n - 1,))] * 2
        + [DMA((n_dp - 1,))] * 2
        + [DMA((n - 1,))] * 2,
        compiler_params=pltpu.CompilerParams(collective_id=collective_id, has_side_effects=True),
        name="sum_all",
    )(x)


def local(
    tokens,
    cotangent,
    lengths,
    counts,
    query_weight,
    query_moment,
    query_square,
    shared_weight,
    shared_moment,
    shared_square,
    project_weight,
    project_moment,
    project_square,
    expand_weight,
    expand_moment,
    expand_square,
    shrink_weight,
    shrink_moment,
    shrink_square,
    vectors_value,
    vectors_moment,
    vectors_square,
):
    device = lax.axis_index("dp")
    n_dp = lax.axis_size("dp")
    t = lax.axis_index("tensor")
    n = lax.axis_size("tensor")
    row_count, width = tokens.shape
    slots = 2 * row_count // n_dp
    part_rows, part_cols = row_count // n, width // n
    send_start = lax.dynamic_index_in_dim(exclusive_sum(counts, 1), device, 0, keepdims=False)
    send_amount = lax.dynamic_index_in_dim(counts, device, 0, keepdims=False)
    recv_start = lax.dynamic_index_in_dim(exclusive_sum(counts, 0), device, 1, keepdims=False)
    recv_amount = lax.dynamic_index_in_dim(counts, device, 1, keepdims=False)
    send_slots = slot_matrix(send_start, send_amount, slots, row_count)
    recv_slots = slot_matrix(recv_start, recv_amount, slots, row_count)

    def low(x):
        return x.astype(jnp.bfloat16)

    def pack(rows, out_slots):
        return low(mul_plain(out_slots, rows)).reshape(n_dp, slots, rows.shape[1])

    def exchange(packed):
        return lax.all_to_all(packed, "dp", split_axis=0, concat_axis=0, tiled=True)

    def unpack(arrived, in_slots):
        return low(mul_left_t(in_slots, arrived.reshape(n_dp * slots, arrived.shape[2])))

    mine_cols = [
        lax.dynamic_slice_in_dim(a, t * part_cols, part_cols, 1) for a in (tokens, cotangent)
    ]
    packed, query_here, project_here, shared_here = lax.optimization_barrier(
        (
            pack(jnp.concatenate(mine_cols, axis=1), send_slots),
            query_weight,
            project_weight,
            shared_weight,
        )
    )
    query_line, project_line, shared_line = gather_lines(
        n_dp, n, low(query_here), low(project_here).T, low(shared_here)
    )
    arrived, query_line, shared_line = lax.optimization_barrier(
        (exchange(packed), query_line, shared_line)
    )
    owned = unpack(arrived, recv_slots)
    owned_rows, owned_grad, query_all, shared_all = rows_and_weights(
        n_dp, n, owned, query_line, shared_line
    )

    head_size = shared_all.shape[1] // 2
    hidden_width = expand_weight.shape[1]
    hidden_total = hidden_width * n
    gain_one = vectors_value[0:width]
    shift_one = vectors_value[width : 2 * width]
    gain_two = vectors_value[2 * width : 3 * width]
    shift_two = vectors_value[3 * width : 4 * width]
    query_bias = vectors_value[4 * width : 5 * width]
    project_bias = vectors_value[5 * width : 6 * width]
    shrink_bias = vectors_value[6 * width : 7 * width]
    expand_bias = lax.dynamic_slice_in_dim(
        vectors_value, 7 * width + t * hidden_width, hidden_width, 0
    )
    value_bias = vectors_value[7 * width + hidden_total : 7 * width + hidden_total + head_size]

    inputs_float = owned_rows.astype(jnp.float32)
    normed_one, norm_one_back = jax.vjp(layer_norm, inputs_float, gain_one, shift_one)
    normed_low = normed_one.astype(jnp.bfloat16)
    queries = (mul_plain(normed_low, query_all) + query_bias).astype(jnp.bfloat16)
    shared_out = mul_plain(normed_low, shared_all) + jnp.concatenate(
        [jnp.zeros((head_size,), jnp.float32), value_bias]
    )
    shared_rows, project_all_t, owned_grad = shared_and_project(
        n_dp, n, owned, low(shared_out), project_line, owned_grad
    )
    window = min(row_count, part_rows + longest)
    window_start = jnp.maximum((t + 1) * part_rows - window, 0)
    shared_window = lax.dynamic_slice_in_dim(shared_rows, window_start, window, 0)
    key_rows, value_rows = shared_window[:, :head_size], shared_window[:, head_size:]
    segment, position = segment_ids(lengths[0], row_count)
    masks = (
        lax.dynamic_slice_in_dim(segment, t * part_rows, part_rows, 0)[:, None],
        lax.dynamic_slice_in_dim(segment, window_start, window, 0)[None, :],
        lax.dynamic_slice_in_dim(position, t * part_rows, part_rows, 0)[:, None],
        lax.dynamic_slice_in_dim(position, window_start, window, 0)[None, :],
    )
    heads_out, log_total = attend(queries, key_rows, value_rows, masks)
    hidden_one = inputs_float + (mul_right_t(heads_out, project_all_t) + project_bias)
    normed_two, norm_two_back = jax.vjp(layer_norm, hidden_one, gain_two, shift_two)

    normed_two_low, expand_cols, shrink_rows_t = rows_and_expanded(
        n_dp, n, low(normed_two), low(expand_weight), low(shrink_weight).T
    )
    expand_pre = mul_plain(normed_two_low, expand_cols) + expand_bias
    activated, gelu_back = jax.vjp(gelu_tanh, expand_pre)
    activated_low = activated.astype(jnp.bfloat16)
    result_part = low(mul_right_t(activated_low, shrink_rows_t))
    own_result = lax.dynamic_slice_in_dim(result_part, t * part_rows, part_rows, 0)
    result_part = lax.dynamic_update_slice_in_dim(
        result_part, low(own_result + (hidden_one + shrink_bias)), t * part_rows, 0
    )
    result_part, owned_grad = lax.optimization_barrier((result_part, owned_grad))
    layer_cols = lax.psum_scatter(result_part, "tensor", scatter_dimension=1, tiled=True)
    shrink_grad_t = low(mul_left_t(owned_grad, activated_low))
    activated_grad = mul_plain(owned_grad, shrink_rows_t)
    expand_pre_grad = gelu_back(activated_grad)[0].astype(jnp.bfloat16)
    expand_grad = low(mul_left_t(normed_two_low, expand_pre_grad))
    expand_bias_grad = jnp.sum(expand_pre_grad.astype(jnp.float32), axis=0)
    normed_two_part = mul_right_t(expand_pre_grad, expand_cols).astype(jnp.bfloat16)

    normed_two_grad, expand_part, shrink_part_t = scatter_expanded(
        n_dp, n, normed_two_part, expand_grad, shrink_grad_t
    )
    shrink_part = turned(shrink_part_t)
    output_cols = unpack(exchange(pack(layer_cols, recv_slots)), send_slots)
    output_float = lax.dynamic_slice_in_dim(owned_grad, t * part_rows, part_rows, 0).astype(
        jnp.float32
    )
    shrink_bias_grad = jnp.sum(output_float, axis=0)
    hidden_from_norm, gain_two_grad, shift_two_grad = norm_two_back(normed_two_grad)
    hidden_grad = output_float + hidden_from_norm
    branch_grad = hidden_grad.astype(jnp.bfloat16)
    project_bias_grad = jnp.sum(branch_grad.astype(jnp.float32), axis=0)
    heads_grad = low(mul_plain(branch_grad, project_all_t))
    query_grad, shared_part = attend_back(
        queries, heads_grad, log_total, key_rows, value_rows, masks, row_count
    )
    shared_grad, query_sum, project_sum, output_rows = scatter_shared(
        n_dp, n, shared_part, output_cols, normed_low, query_grad, branch_grad, heads_out
    )
    shared_grad = low(shared_grad)
    query_bias_grad = jnp.sum(query_grad.astype(jnp.float32), axis=0)
    normed_one_grad = mul_right_t(query_grad, query_all) + mul_right_t(shared_grad, shared_all)
    inputs_from_norm, gain_one_grad, shift_one_grad = norm_one_back(normed_one_grad)
    input_result = (hidden_grad + inputs_from_norm).astype(jnp.bfloat16)
    shared_weight_grad = mul_left_t(normed_low, shared_grad)
    value_bias_grad = jnp.sum(shared_grad[:, head_size:].astype(jnp.float32), axis=0)

    shared_sum, input_cols = cols_and_shared(n_dp, n, input_result, low(shared_weight_grad))
    packed, query_sum, project_sum, shared_sum = lax.optimization_barrier(
        (pack(input_cols, recv_slots), query_sum, project_sum, shared_sum)
    )
    query_part, project_part_t, shared_piece = scatter_grads(
        n_dp, n, query_sum, project_sum, shared_sum
    )
    project_part = turned(project_part_t)
    arrived, query_part = lax.optimization_barrier((exchange(packed), query_part))
    grad_rows = lax.all_gather(unpack(arrived, send_slots), "tensor", axis=1, tiled=True)
    output_back = output_rows.astype(jnp.float32)
    token_rms = jnp.sqrt(jnp.mean(output_back * output_back, axis=1))

    split_part = lax.dynamic_update_slice_in_dim(
        jnp.zeros((hidden_total,), jnp.float32), expand_bias_grad, t * hidden_width, 0
    )
    vector_part = jnp.concatenate(
        [
            gain_one_grad,
            shift_one_grad,
            gain_two_grad,
            shift_two_grad,
            query_bias_grad,
            project_bias_grad,
            shrink_bias_grad,
            split_part,
            value_bias_grad,
        ]
    )
    local_squares = (
        jnp.sum(query_part * query_part)
        + jnp.sum(expand_part * expand_part)
        + jnp.sum(shared_piece * shared_piece)
        + jnp.sum(project_part * project_part)
        + jnp.sum(shrink_part * shrink_part)
    )
    length = vector_part.shape[0]
    unit = n * 8 * 128
    padded = -(-(length + 1) // unit) * unit
    everything = jnp.concatenate(
        [vector_part, local_squares[None], jnp.zeros((padded - length - 1,), jnp.float32)]
    )
    summed = sum_all(everything.reshape(padded // 128, 128), n_dp, n, 9).reshape(padded)
    vector_grad, weight_squares = summed[:length], summed[length]
    grad_size = jnp.sqrt(weight_squares + jnp.sum(vector_grad * vector_grad))
    clip_factor = jnp.minimum(1.0, clip_level / (grad_size + 1e-06))
    clipped_vectors = clip_factor * vector_grad
    query_new = adamw_step(
        query_weight,
        query_moment,
        query_square,
        clip_factor * query_part,
        rate_matrix * width ** (-0.5),
    )
    shared_new = adamw_step(
        shared_weight,
        shared_moment,
        shared_square,
        clip_factor * shared_piece,
        rate_attention * width ** (-0.5),
    )
    project_new = adamw_step(
        project_weight,
        project_moment,
        project_square,
        clip_factor * project_part,
        rate_attention * width ** (-0.5),
    )
    expand_new = adamw_step(
        expand_weight,
        expand_moment,
        expand_square,
        clip_factor * expand_part,
        rate_matrix * width ** (-0.5),
    )
    shrink_new = adamw_step(
        shrink_weight,
        shrink_moment,
        shrink_square,
        clip_factor * shrink_part,
        rate_matrix * hidden_total ** (-0.5),
    )
    vectors_new = adamw_step(
        vectors_value, vectors_moment, vectors_square, clipped_vectors, rate_vector
    )
    return (
        output_rows,
        grad_rows,
        grad_size,
        *query_new,
        *shared_new,
        *project_new,
        *expand_new,
        *shrink_new,
        *vectors_new,
        clipped_vectors,
        token_rms,
    )


def solution(mesh):
    by_rows = P("dp", None)
    query = P("dp", "tensor")
    shared = P(("dp", "tensor"), None)
    project = P("tensor", "dp")
    return jax.shard_map(
        local,
        mesh=mesh,
        in_specs=(
            *(by_rows,) * 3,
            P(),
            *(query,) * 3,
            *(shared,) * 3,
            *(project,) * 3,
            *(query,) * 3,
            *(project,) * 3,
            *(P(),) * 3,
        ),
        out_specs=(
            *(by_rows,) * 2,
            P(),
            *(query,) * 3,
            *(shared,) * 3,
            *(project,) * 3,
            *(query,) * 3,
            *(project,) * 3,
            *(P(),) * 4,
            P("dp"),
        ),
        check_vma=False,
    )
```

```python
import functools

import jax
import jax.numpy as jnp
from jax import lax
from jax.experimental.layout import Layout, with_layout_constraint
from jax.experimental import pallas as pl
from jax.experimental.pallas import tpu as pltpu
from jax.sharding import PartitionSpec as P

STEP = 10


beta_one = 0.9
beta_two = 0.95
adam_epsilon = 1e-08
decay_rate = 0.1
clip_level = 1.0
norm_epsilon = 1e-05
rate_matrix = 0.6
rate_attention = 2.4
rate_vector = 0.3
masked_score = -1e30
longest = 512

MESH = pl.DeviceIdType.MESH
IN_PLACE = pl.BlockSpec(memory_space=pl.ANY)
IN_VMEM = pl.BlockSpec(memory_space=pltpu.VMEM)
DMA = pltpu.SemaphoreType.DMA
MIB = 2**20


def mul_plain(left, right):
    return jnp.dot(left, right, preferred_element_type=jnp.float32)


def mul_right_t(left, right):
    return lax.dot_general(
        left, right, (((1,), (1,)), ((), ())), preferred_element_type=jnp.float32
    )


def mul_left_t(left, right):
    return lax.dot_general(
        left, right, (((0,), (0,)), ((), ())), preferred_element_type=jnp.float32
    )


def product(left, right, left_dim, right_dim):
    return lax.dot_general(
        left, right, (((left_dim,), (right_dim,)), ((), ())), preferred_element_type=jnp.float32
    )


def layer_norm(values, scaling, offset):
    average = jnp.mean(values, axis=-1, keepdims=True)
    centered = values - average
    variance = jnp.mean(centered * centered, axis=-1, keepdims=True)
    return centered * lax.rsqrt(variance + norm_epsilon) * scaling + offset


def gelu_tanh(values):
    return jax.nn.gelu(values, approximate=True)


def exclusive_sum(table, axis_index):
    return jnp.cumsum(table, axis=axis_index) - table


def segment_ids(seq_lengths, row_count):
    position = jnp.arange(row_count, dtype=jnp.int32)
    starts = jnp.cumsum(seq_lengths) - seq_lengths
    segment = jnp.sum((starts[None, :] <= position[:, None]).astype(jnp.int32), axis=1)
    return (segment, position)


def slot_matrix(starts, amounts, slots, row_count):
    offsets = jnp.arange(slots, dtype=jnp.int32)
    picked = jnp.where(offsets[None, :] < amounts[:, None], starts[:, None] + offsets[None, :], -1)
    position = jnp.arange(row_count, dtype=jnp.int32)
    return (picked.reshape(-1)[:, None] == position[None, :]).astype(jnp.bfloat16)


def turned(x):
    return with_layout_constraint(x.T, Layout(major_to_minor=(0, 1)))


def adamw_step(weight, moment, square, gradient, rate):
    moment_new = beta_one * moment + (1.0 - beta_one) * gradient
    square_new = beta_two * square + (1.0 - beta_two) * gradient * gradient
    moment_hat = moment_new / (1.0 - beta_one**STEP)
    square_hat = square_new / (1.0 - beta_two**STEP)
    weight_new = weight - rate * (
        moment_hat / (jnp.sqrt(square_hat) + adam_epsilon) + decay_rate * weight
    )
    return (weight_new, moment_new, square_new)


def remote(src, dst, send_sem, recv_sem, device):
    return pltpu.make_async_remote_copy(
        src, dst, send_sem, recv_sem, device_id=device, device_id_type=MESH
    )


class Place:
    def __init__(self, n_dp, n):
        self.n, self.chips = n, n_dp // 2
        self.dp, self.t = lax.axis_index("dp"), lax.axis_index("tensor")
        self.core, chip = lax.rem(self.dp, 2), lax.div(self.dp, 2)
        side = round(self.chips**0.5)
        self.side = side if side * side == self.chips else self.chips
        self.pos = self.snake(chip)
        self.sibling = (self.dp + 1 - 2 * self.core, self.t)
        self.after = (self.block(self.ring(self.pos + 1), self.core), self.t)
        self.before = (self.block(self.ring(self.pos - 1), self.core), self.t)
        self.left, self.right = (self.dp, self.t - 1), (self.dp, self.t + 1)

    def snake(self, index):
        row, col = lax.div(index, self.side), lax.rem(index, self.side)
        odd = lax.rem(row, 2)
        return row * self.side + col + odd * (self.side - 1 - 2 * col)

    def ring(self, pos):
        return lax.rem(pos + 2 * self.chips, self.chips)

    def block(self, pos, core):
        return self.snake(pos) * 2 + core

    def greet(self, line=False, line_all=False, ring=False):
        barrier = pltpu.get_barrier_semaphore()
        peers = 0

        def call(device):
            pl.semaphore_signal(barrier, inc=1, device_id=device, device_id_type=MESH)

        if ring:
            for device in (self.sibling, self.after, self.before):
                call(device)
            peers += 3
        if line_all:
            for k in range(1, self.n):
                call((self.dp, lax.rem(self.t + k, self.n)))
            peers += self.n - 1
        elif line:
            pl.when(self.t > 0)(lambda: call(self.left))
            pl.when(self.t < self.n - 1)(lambda: call(self.right))
            peers += (self.t > 0).astype(jnp.int32) + (self.t < self.n - 1).astype(jnp.int32)
        return lambda: pl.semaphore_wait(barrier, peers)


class LineGather:
    @staticmethod
    def sems(n, chunks):
        return [DMA((n - 1, chunks))] * 4 + [DMA]

    def __init__(self, at, chunks, first, place, sems, whole, unit=1.0):
        self.unit = unit
        self.at, self.chunks, self.first, self.place, self.sems = at, chunks, first, place, sems
        self.own = pltpu.make_async_copy(whole[0], whole[1], sems[4])

    def copy(self, h, c, right):
        at = self.at
        dst = self.place(at.t - h if right else at.t + h, c)
        src = self.first(c) if h == 0 else dst
        s, r = self.sems[0:2] if right else self.sems[2:4]
        return remote(src, dst, s.at[h, c], r.at[h, c], at.right if right else at.left)

    def receive(self, h, c, right):
        at = self.at
        dst = self.place(at.t - 1 - h if right else at.t + 1 + h, c)
        s, r = self.sems[0:2] if right else self.sems[2:4]
        remote(dst, dst, s.at[h, c], r.at[h, c], at.left if right else at.right).wait_recv()

    def sends(self, h, right):
        t, n = self.at.t, self.at.n
        return (t >= h) & (t < n - 1) if right else (t + h <= n - 1) & (t > 0)

    def gets(self, h, right):
        return self.at.t - 1 - h >= 0 if right else self.at.t + 1 + h <= self.at.n - 1

    def every(self):
        for h in range(self.at.n - 1):
            for c in range(self.chunks):
                for right in (True, False):
                    yield h, c, right

    def prepare(self):
        self.own.start()

    def prepared(self):
        self.own.wait()

    def start(self):
        for h, c, right in self.every():
            if h == 0:
                pl.when(self.sends(h, right))(lambda: self.copy(h, c, right).start())

    def step(self, h, c, right):
        pl.when(self.gets(h, right))(lambda: self.receive(h, c, right))
        if h + 1 < self.at.n - 1:
            pl.when(self.sends(h + 1, right))(lambda: self.copy(h + 1, c, right).start())

    def steps(self):
        return [
            (self.unit * (which[0] + (which[1] + 1) / self.chunks), functools.partial(self.step, *which))
            for which in self.every()
        ]

    def finish(self):
        for h, c, right in self.every():
            pl.when(self.sends(h, right))(lambda: self.copy(h, c, right).wait_send())


class LineScatter:
    @staticmethod
    def scratch(n, chunks, block, dtype):
        return [pltpu.VMEM((n - 1, *block), dtype)] * 2 + [DMA((n - 1, chunks))] * 4

    def __init__(self, at, chunks, own, out, scratch, unit=1.0):
        self.unit = unit
        self.at, self.chunks, self.own, self.out = at, chunks, own, out
        self.held, self.sems = scratch[:2], scratch[2:6]
        self.rows = self.held[0].shape[1] // chunks

    def parts(self, k, c, right):
        side = 0 if right else 1
        s, r = self.sems[2 * side : 2 * side + 2]
        return self.held[side].at[k, pl.ds(c * self.rows, self.rows)], s.at[k, c], r.at[k, c]

    def send(self, k, c, right, first):
        slot, s, r = self.parts(k, c, right)
        src = self.own(self.target(k, right), c) if first else slot
        return remote(src, slot, s, r, self.at.right if right else self.at.left)

    def receive(self, k, c, right):
        slot, s, r = self.parts(k, c, right)
        remote(slot, slot, s, r, self.at.left if right else self.at.right).wait_recv()

    def target(self, k, right):
        return self.at.n - 1 - k if right else k

    def every(self):
        for k in range(self.at.n - 1):
            for c in range(self.chunks):
                for right in (True, False):
                    yield k, c, right

    def prepare(self):
        pass

    def prepared(self):
        pass

    def start(self):
        t, n = self.at.t, self.at.n
        for k, c, right in self.every():
            first = (t == (0 if right else n - 1)) & (t != self.target(k, right))
            pl.when(first)(lambda: self.send(k, c, right, True).start())

    def add(self, k, c, right):
        self.receive(k, c, right)
        slot = self.parts(k, c, right)[0]
        mine = self.own(self.target(k, right), c)[...]
        slot[...] = (slot[...].astype(jnp.float32) + mine.astype(jnp.float32)).astype(slot.dtype)
        self.send(k, c, right, False).start()

    def step(self, k, c, right):
        t, n, d = self.at.t, self.at.n, self.target(k, right)
        passes = (t > 0) & (t < d) if right else (t < n - 1) & (t > d)
        pl.when(passes)(lambda: self.add(k, c, right))

    def steps(self):
        return [
            (self.unit * (which[0] + (which[1] + 1) / self.chunks), functools.partial(self.step, *which))
            for which in self.every()
        ]

    def finish(self):
        t, n = self.at.t, self.at.n
        for k, c, right in self.every():
            pl.when(t == self.target(k, right))(lambda: self.receive(k, c, right))
        for c in range(self.chunks):
            span = pl.ds(c * self.rows, self.rows)
            self.out[span] = self.own(t, c)[...].astype(self.out.dtype)

        def more(block):
            self.out[...] += block[...].astype(self.out.dtype)

        pl.when(t > 0)(lambda: more(self.held[0].at[n - 1 - t]))
        pl.when(t < n - 1)(lambda: more(self.held[1].at[t]))
        for k, c, right in self.every():
            d = self.target(k, right)
            pl.when(t < d if right else t > d)(lambda: self.send(k, c, right, False).wait_send())


class LineExchange:
    @staticmethod
    def scratch(n, block, dtype):
        return [pltpu.VMEM((n - 1, *block), dtype)] + [DMA((n - 1,))] * 2

    def __init__(self, at, source, out, scratch):
        self.at, self.source, self.out = at, source, out
        self.held = scratch[0]
        self.copies = []
        for k in range(1, at.n):
            p = lax.rem(at.t + k, at.n)
            self.copies.append(
                remote(
                    source(p),
                    self.held.at[k - 1],
                    scratch[1].at[k - 1],
                    scratch[2].at[k - 1],
                    (at.dp, p),
                )
            )

    def prepare(self):
        pass

    def prepared(self):
        pass

    def start(self):
        for copy in self.copies:
            copy.start()

    def steps(self):
        return []

    def finish(self):
        for copy in self.copies:
            copy.wait()
        total = self.source(self.at.t)[...].astype(jnp.float32)
        for k in range(self.at.n - 1):
            total = total + self.held[k].astype(jnp.float32)
        self.out[...] = total.astype(self.out.dtype)


class RingGather:
    @staticmethod
    def sems(chips, chunks):
        hops = chips // 2
        return [DMA((2, hops, chunks))] * 4 + [DMA((chunks,))] * 2 + [DMA]

    def __init__(self, at, chunks, first, place, sems, whole, unit=1.0):
        self.unit = unit
        self.at, self.chunks, self.first, self.place, self.sems = at, chunks, first, place, sems
        self.hops = at.chips // 2
        self.own = pltpu.make_async_copy(whole[0], whole[1], sems[6])

    def every(self):
        for h in range(self.hops):
            for c in range(self.chunks):
                for way in (0, 1):
                    if h < self.hops - 1 or c % 2 == way:
                        yield h, c, way

    def origin(self, steps, way, core):
        return self.at.block(self.at.ring(self.at.pos + (steps if way else -steps)), core)

    def onward(self, h, c, way):
        dst = self.place(self.origin(h, way, self.at.core), c)
        src = self.first(c) if h == 0 else dst
        s, r = self.sems[0:2]
        device = self.at.before if way else self.at.after
        return remote(src, dst, s.at[way, h, c], r.at[way, h, c], device)

    def arrival(self, h, c, way):
        dst = self.place(self.origin(h + 1, way, self.at.core), c)
        s, r = self.sems[0:2]
        device = self.at.after if way else self.at.before
        return remote(dst, dst, s.at[way, h, c], r.at[way, h, c], device)

    def across(self, h, c, way, core):
        dst = self.place(self.origin(h + 1, way, core), c)
        s, r = self.sems[2:4]
        return remote(dst, dst, s.at[way, h, c], r.at[way, h, c], self.at.sibling)

    def across_own(self, c, core):
        dst = self.place(self.origin(0, 0, core), c)
        s, r = self.sems[4:6]
        return remote(self.first(c), dst, s.at[c], r.at[c], self.at.sibling)

    def prepare(self):
        self.own.start()

    def prepared(self):
        self.own.wait()

    def start(self):
        for h, c, way in self.every():
            if h == 0:
                self.onward(h, c, way).start()
        for c in range(self.chunks):
            self.across_own(c, self.at.core).start()

    def step(self, h, c, way):
        self.arrival(h, c, way).wait_recv()
        if (h + 1, c, way) in list(self.every()):
            self.onward(h + 1, c, way).start()
        self.across(h, c, way, self.at.core).start()

    def steps(self):
        when = 0.0
        for h, c, way in self.every():
            when += self.unit / self.chunks / 2
            yield when, functools.partial(self.step, h, c, way)

    def finish(self):
        other = 1 - self.at.core
        for c in range(self.chunks):
            self.across_own(c, other).wait_recv()
            self.across_own(c, self.at.core).wait_send()
        for h, c, way in self.every():
            self.across(h, c, way, other).wait_recv()
            self.across(h, c, way, self.at.core).wait_send()
            self.onward(h, c, way).wait_send()


class RingScatter:
    @staticmethod
    def scratch(chips, chunks, block, dtype):
        hops = chips // 2
        return (
            [pltpu.VMEM((chips, *block), dtype)] * 2
            + [pltpu.VMEM((2, hops, *block), dtype)]
            + [DMA((chips, chunks))] * 3
            + [DMA((2, hops, chunks))] * 2
        )

    def __init__(self, at, chunks, source, out, scratch, unit=1.0):
        self.unit = unit
        self.at, self.chunks, self.source, self.out = at, chunks, source, out
        self.hops = at.chips // 2
        self.mine, self.other, self.held = scratch[:3]
        self.load_sem, self.s1, self.r1, self.s2, self.r2 = scratch[3:8]
        self.rows = self.held.shape[2] // chunks

    def span(self, c):
        return pl.ds(c * self.rows, self.rows)

    def target(self, place, core):
        return self.at.block(self.at.ring(self.at.pos + place), core)

    def load(self, place, c):
        src = self.source(self.target(place, self.at.core), c)
        dst = self.mine.at[place, self.span(c)]
        return pltpu.make_async_copy(src, dst, self.load_sem.at[place, c])

    def across(self, place, c):
        src = self.source(self.target(place, 1 - self.at.core), c)
        dst = self.other.at[place, self.span(c)]
        return remote(src, dst, self.s1.at[place, c], self.r1.at[place, c], self.at.sibling)

    def sent(self, e, c, way):
        return e < self.hops or c % 2 == way

    def onward(self, e, c, way):
        place = self.at.chips - e if way else e
        src, dst = self.mine.at[place, self.span(c)], self.held.at[way, e - 1, self.span(c)]
        device = self.at.before if way else self.at.after
        return remote(src, dst, self.s2.at[way, e - 1, c], self.r2.at[way, e - 1, c], device)

    def arrival(self, e, c, way):
        dst = self.held.at[way, e, self.span(c)]
        device = self.at.after if way else self.at.before
        return remote(dst, dst, self.s2.at[way, e, c], self.r2.at[way, e, c], device)

    def places(self):
        order = []
        for e in range(self.hops, 0, -1):
            order += [e] if e == self.hops else [e, self.at.chips - e]
        return order + [0]

    def prepare(self):
        for place in self.places():
            for c in range(self.chunks):
                self.load(place, c).start()

    def prepared(self):
        pass

    def start(self):
        self.send_across(self.places()[:1])

    def send_across(self, places):
        for place in places:
            for c in range(self.chunks):
                self.across(place, c).start()

    def loaded(self, place, c):
        self.load(place, c).wait()

    def base(self, place, c):
        self.loaded(place, c)
        self.across(place, c).wait_recv()
        total = self.mine[place, self.span(c)].astype(jnp.float32)
        return total + self.other[place, self.span(c)].astype(jnp.float32)

    def arrived(self, e, c, way):
        self.arrival(e, c, way).wait_recv()
        return self.held[way, e, self.span(c)].astype(jnp.float32)

    def step(self, e, c, way):
        place = self.at.chips - e if way else e
        total = self.base(place, c)
        if e < self.hops and self.sent(e + 1, c, way):
            total += self.arrived(e, c, way)
        self.mine[place, self.span(c)] = total.astype(self.mine.dtype)
        self.onward(e, c, way).start()

    def last(self, c):
        total = self.base(0, c)
        for way in (0, 1):
            if self.sent(1, c, way):
                total += self.arrived(0, c, way)
        self.out[self.span(c)] = total.astype(self.out.dtype)

    def every(self):
        for e in range(self.hops, 0, -1):
            for c in range(self.chunks):
                for way in (0, 1):
                    if self.sent(e, c, way):
                        yield e, c, way

    def steps(self):
        yield 0.0, functools.partial(self.send_across, self.places()[1:])
        yield from self.sum_steps()

    def sum_steps(self):
        when = 0.0
        for e, c, way in self.every():
            yield when, functools.partial(self.step, e, c, way)
            when += self.unit / self.chunks / 2
        for c in range(self.chunks):
            yield when + self.unit * (c + 1) / self.chunks, functools.partial(self.last, c)

    def finish(self):
        for place in self.places():
            for c in range(self.chunks):
                self.across(place, c).wait_send()
        for e, c, way in self.every():
            self.onward(e, c, way).wait_send()


class ProductScatter(RingScatter):
    @staticmethod
    def scratch(chips, chunks, block, dtype):
        return RingScatter.scratch(chips, chunks, block, dtype) + [pltpu.VMEM((2, *block), dtype)]

    def __init__(self, at, chunks, left, right, out, scratch, unit, cost):
        super().__init__(at, chunks, None, out, scratch[:-1], unit)
        self.left, self.right, self.stage, self.cost = left, right, scratch[-1], cost

    def across(self, place, c):
        src = self.stage.at[self.places().index(place) % 2, self.span(c)]
        dst = self.other.at[place, self.span(c)]
        return remote(src, dst, self.s1.at[place, c], self.r1.at[place, c], self.at.sibling)

    def product(self, place, core):
        block = self.held.shape[2]
        cols = lanes(self.target(place, core), block) if block % 128 == 0 else None
        if cols is None:
            left = self.left[pl.ds(pl.multiple_of(self.target(place, core) * block, block), block)]
            total = product(left, self.right[...], 1, 0)
        else:
            total = product(self.left[:, cols], self.right[...], 0, 0)
        return total.astype(self.mine.dtype)

    def work(self, i, place, here):
        if here:
            self.mine[place] = self.product(place, self.at.core)
            return
        if i >= 2:
            for c in range(self.chunks):
                self.across(self.places()[i - 2], c).wait_send()
        self.stage[i % 2] = self.product(place, 1 - self.at.core)
        for c in range(self.chunks):
            self.across(place, c).start()

    def prepare(self):
        pass

    def start(self):
        pass

    def loaded(self, place, c):
        pass

    def steps(self):
        when = 0.0
        for i, place in enumerate(self.places()):
            for here in (False, True):
                yield when, functools.partial(self.work, i, place, here)
                when += self.cost
        for when, step in self.sum_steps():
            place = 0
            if len(step.args) == 3:
                e, _, way = step.args
                place = self.at.chips - e if way else e
            yield max(when, (2 * self.places().index(place) + 2) * self.cost), step

    def finish(self):
        for place in self.places()[-2:]:
            for c in range(self.chunks):
                self.across(place, c).wait_send()
        for e, c, way in self.every():
            self.onward(e, c, way).wait_send()


class LineSwitch:
    @staticmethod
    def sems(n):
        return [DMA((n - 1,))] * 2 + [DMA]

    def __init__(self, at, source, target, sems):
        self.own = pltpu.make_async_copy(source(at.t), target, sems[2])
        self.copies = []
        for k in range(1, at.n):
            p = lax.rem(at.t + k, at.n)
            self.copies.append(
                remote(source(p), target, sems[0].at[k - 1], sems[1].at[k - 1], (at.dp, p))
            )

    def prepare(self):
        self.own.start()

    def prepared(self):
        self.own.wait()

    def start(self):
        for copy in self.copies:
            copy.start()

    def steps(self):
        return []

    def finish(self):
        for copy in self.copies:
            copy.wait()


class Pieces:
    def __init__(self, ref, begin):
        self.ref, self.begin, self.dtype = ref, begin, ref.dtype

    def __setitem__(self, span, value):
        pieces, _, cols = self.ref.shape
        for k in range(pieces):
            rows = pl.ds(self.begin + span.start, span.size)
            self.ref[k, rows] = value[:, k * cols : (k + 1) * cols]


class Later:
    def __init__(self, job, when):
        self.job, self.when = job, when

    def prepare(self):
        pass

    def prepared(self):
        pass

    def start(self):
        pass

    def steps(self):
        yield self.when, self.job.start

    def finish(self):
        self.job.finish()


class RowProduct:
    @staticmethod
    def scratch(weight):
        return [pltpu.VMEM(weight.shape, weight.dtype), DMA]

    def __init__(self, left, weight, turn, bias, out, scratch, begin, cost):
        self.left, self.turn, self.bias, self.out = left, turn, bias, out
        self.held, self.begin, self.cost = scratch[0], begin, cost
        self.copy = pltpu.make_async_copy(weight, scratch[0], scratch[1])
        self.tile = 256

    def prepare(self):
        self.copy.start()

    def prepared(self):
        pass

    def start(self):
        pass

    def work(self, j):
        span = pl.ds(j * self.tile, self.tile)
        if self.turn:
            total = product(self.left[...], self.held[span], 1, 1)
        else:
            total = product(self.left[...], self.held[:, span], 1, 0)
        if self.bias is not None:
            total += self.bias[:, span]
        self.out[:, span] = total.astype(self.out.dtype)

    def steps(self):
        yield self.begin, self.copy.wait
        for j in range(self.out.shape[1] // self.tile):
            yield self.begin + j * self.cost, functools.partial(self.work, j)

    def finish(self):
        pass


def run_jobs(met, jobs):
    for job in jobs:
        job.prepare()
    for job in jobs:
        job.prepared()
    met()
    for job in jobs:
        job.start()
    ordered = []
    for i, job in enumerate(jobs):
        ordered += [(when, i, j, step) for j, (when, step) in enumerate(job.steps())]
    for _, _, _, step in sorted(ordered, key=lambda entry: entry[:3]):
        step()
    for job in jobs:
        job.finish()


def rows_of(ref, step):
    return lambda c: ref.at[pl.ds(c * step, step)]


def lanes(index, count):
    return pl.ds(pl.multiple_of(index * count, count), count)


def move(kernel, inputs, in_vmem, outs, out_vmem, scratch, collective_id, name, aliases=None):
    return pl.pallas_call(
        kernel,
        out_shape=tuple(outs),
        in_specs=[IN_VMEM if i < in_vmem else IN_PLACE for i in range(len(inputs))],
        out_specs=tuple(IN_VMEM if i < out_vmem else IN_PLACE for i in range(len(outs))),
        scratch_shapes=scratch,
        compiler_params=pltpu.CompilerParams(
            collective_id=collective_id, has_side_effects=True, vmem_limit_bytes=56 * MIB
        ),
        input_output_aliases=aliases or {},
        name=name,
    )(*inputs)


def line_gather(at, x, out, axis, chunks, sems, unit=1.0):
    rows, cols = x.shape
    step = rows // chunks
    if axis == 0:
        place = lambda b, c: out.at[pl.ds(b * rows + c * step, step)]
        whole = out.at[pl.ds(at.t * rows, rows)]
    else:
        place = lambda b, c: out.at[pl.ds(c * step, step), lanes(b, cols)]
        whole = out.at[:, lanes(at.t, cols)]
    return LineGather(at, chunks, rows_of(x, step), place, sems, (x, whole), unit)


def ring_gather(at, x, out, axis, chunks, sems, unit=1.0):
    rows, cols = x.shape
    step = rows // chunks
    if axis == 0:
        place = lambda b, c: out.at[pl.ds(b * rows + c * step, step)]
        whole = out.at[pl.ds(at.dp * rows, rows)]
    else:
        place = lambda b, c: out.at[pl.ds(c * step, step), lanes(b, cols)]
        whole = out.at[:, lanes(at.dp, cols)]
    return RingGather(at, chunks, rows_of(x, step), place, sems, (x, whole), unit)


def blocks_of(x, out, axis, chunks):
    rows, cols = out.shape
    step = rows // chunks
    if axis == 0:
        return lambda b, c: x.at[pl.ds(pl.multiple_of(b * rows + c * step, step), step)]
    return lambda b, c: x.at[pl.ds(c * step, step), lanes(b, cols)]


def line_exchange(at, x, out, axis, scratch):
    block = blocks_of(x, out, axis, 1)
    return LineExchange(at, lambda p: block(p, 0), out, scratch)


def line_scatter(at, x, out, axis, chunks, scratch, unit=1.0):
    return LineScatter(at, chunks, blocks_of(x, out, axis, chunks), out, scratch, unit)


def ring_scatter(at, x, out, axis, chunks, scratch, unit=1.0):
    return RingScatter(at, chunks, blocks_of(x, out, axis, chunks), out, scratch, unit)


def product_scatter(at, left, right, out, chunks, scratch, unit, cost):
    return ProductScatter(at, chunks, left, right, out, scratch, unit, cost)


def by_lanes(left, n_dp):
    return left if left.shape[1] // n_dp % 128 == 0 else left.T


def like(x, rows, cols, dtype=None):
    return jax.ShapeDtypeStruct((x.shape[0] * rows, x.shape[1] * cols), dtype or x.dtype)


class Parts:
    def __init__(self, refs):
        self.refs = list(refs)

    def take(self, shapes):
        taken, self.refs = self.refs[: len(shapes)], self.refs[len(shapes) :]
        return taken


def gather_lines(n_dp, n, query, project, shared):
    low = jnp.bfloat16
    sems = LineGather.sems(n, 1)
    shapes = [
        jax.ShapeDtypeStruct(query.shape, low),
        jax.ShapeDtypeStruct(project.shape[::-1], low),
        jax.ShapeDtypeStruct(shared.shape, low),
    ]

    def kernel(a, b, c, a_out, b_out, c_out, a_low, b_low, c_low, *refs):
        parts = Parts(refs)
        at = Place(n_dp, n)
        met = at.greet(line=True)
        a_low[...] = a[...].astype(low)
        b_low[...] = b[...].T.astype(low)
        c_low[...] = c[...].astype(low)
        run_jobs(
            met,
            [
                line_gather(at, a_low, a_out, 1, 1, parts.take(sems), 6.0),
                line_gather(at, c_low, c_out, 0, 1, parts.take(sems), 6.5),
                line_gather(at, b_low, b_out, 1, 1, parts.take(sems), 12.0),
            ],
        )

    return move(
        kernel,
        (query, project, shared),
        3,
        (like(shapes[0], 1, n), like(shapes[1], 1, n), like(shapes[2], n, 1)),
        0,
        [pltpu.VMEM(x.shape, low) for x in shapes] + sems * 3,
        1,
        "gather_lines",
    )


def rows_and_weights(n_dp, n, owned, query, shared):
    chips, chunks = n_dp // 2, 2
    total, cols = owned.shape[0], owned.shape[1] // 2
    rows, half = total // n, total // 2
    switch, line = LineSwitch.sems(n), LineGather.sems(n, chunks)
    ring = RingGather.sems(chips, chunks)

    def kernel(x, a, b, x_out, y_out, a_out, b_out, *refs):
        parts = Parts(refs)
        at = Place(n_dp, n)
        run_jobs(
            at.greet(line_all=True, ring=True),
            [
                LineSwitch(
                    at,
                    lambda p: x.at[pl.ds(pl.multiple_of(p * rows, rows), rows), pl.ds(0, cols)],
                    x_out.at[:, lanes(at.t, cols)],
                    parts.take(switch),
                ),
                ring_gather(at, b, b_out, 0, chunks, parts.take(ring), 4.0),
                ring_gather(at, a, a_out, 0, chunks, parts.take(ring), 22.0),
                line_gather(
                    at,
                    x.at[pl.ds(0, half), pl.ds(cols, cols)],
                    y_out.at[pl.ds(0, half)],
                    1,
                    chunks,
                    parts.take(line),
                    16.0,
                ),
            ],
        )

    return move(
        kernel,
        (owned, query, shared),
        3,
        (
            jax.ShapeDtypeStruct((rows, n * cols), owned.dtype),
            jax.ShapeDtypeStruct((total, n * cols), owned.dtype),
            like(query, n_dp, 1),
            like(shared, n_dp, 1),
        ),
        0,
        switch + ring * 2 + line,
        2,
        "rows_and_weights",
    )


def shared_and_project(n_dp, n, owned, shared_rows, project, rows, bias, query, gathered):
    chips, chunks = n_dp // 2, 2
    total, cols = owned.shape[0], owned.shape[1] // 2
    half = total // 2
    small, line = LineGather.sems(n, 1), LineGather.sems(n, chunks)
    ring = RingGather.sems(chips, chunks)

    made = RowProduct.scratch(query)

    def kernel(y, x, a, r, b, w, _, q_out, x_out, a_out, y_out, *refs):
        parts = Parts(refs)
        at = Place(n_dp, n)
        lower = pl.ds(half, half)
        run_jobs(
            at.greet(line=True, ring=True),
            [
                RowProduct(r, w, False, b, q_out, parts.take(made), 8.0, 3.0),
                line_gather(at, x, x_out, 0, 1, parts.take(small), 4.0),
                ring_gather(at, a, a_out, 0, chunks, parts.take(ring), 22.0),
                line_gather(
                    at,
                    y.at[lower, pl.ds(cols, cols)],
                    y_out.at[lower],
                    1,
                    chunks,
                    parts.take(line),
                    13.0,
                ),
            ],
        )

    return move(
        kernel,
        (owned, shared_rows, project, rows, bias, query, gathered),
        5,
        (
            jax.ShapeDtypeStruct((rows.shape[0], query.shape[1]), rows.dtype),
            like(shared_rows, n, 1),
            like(project, n_dp, 1),
            like(gathered, 1, 1),
        ),
        1,
        made + small + ring + line,
        3,
        "shared_and_project",
        {6: 3},
    )


def rows_and_expanded(n_dp, n, x, expand, shrink):
    low = jnp.bfloat16
    shapes = [
        jax.ShapeDtypeStruct(expand.shape, low),
        jax.ShapeDtypeStruct(shrink.shape[::-1], low),
    ]
    chips, chunks, halves = n_dp // 2, 4, 2
    line, ring = LineGather.sems(n, chunks), RingGather.sems(chips, halves)

    def kernel(x_ref, a, b, x_out, a_out, b_out, a_low, b_low, *refs):
        parts = Parts(refs)
        at = Place(n_dp, n)
        met = at.greet(line=True, ring=True)
        a_low[...] = a[...].astype(low)
        b_low[...] = b[...].T.astype(low)
        run_jobs(
            met,
            [
                line_gather(at, x_ref, x_out, 0, chunks, parts.take(line), 22.0),
                ring_gather(at, a_low, a_out, 0, halves, parts.take(ring), 44.0),
                ring_gather(at, b_low, b_out, 0, halves, parts.take(ring), 44.0),
            ],
        )

    return move(
        kernel,
        (x, expand, shrink),
        3,
        (like(x, n, 1), like(shapes[0], n_dp, 1), like(shapes[1], n_dp, 1)),
        0,
        [pltpu.VMEM(x.shape, low) for x in shapes] + line + ring * 2,
        4,
        "rows_and_expanded",
    )


def scatter_expanded(n_dp, n, x, expand, shrink):
    chips, chunks = n_dp // 2, 4
    block = (x.shape[0] // n, x.shape[1])
    w_block = (expand.shape[0] // n_dp, expand.shape[1])
    line = LineScatter.scratch(n, chunks, block, x.dtype)
    ring = RingScatter.scratch(chips, chunks, w_block, x.dtype)

    def kernel(x_ref, a, b, x_out, a_out, b_out, *refs):
        parts = Parts(refs)
        at = Place(n_dp, n)
        run_jobs(
            at.greet(line=True, ring=True),
            [
                line_scatter(at, x_ref, x_out, 0, chunks, parts.take(line), 26.0),
                ring_scatter(at, a, a_out, 0, chunks, parts.take(ring), 22.0),
                ring_scatter(at, b, b_out, 0, chunks, parts.take(ring), 22.0),
            ],
        )

    return move(
        kernel,
        (x, expand, shrink),
        1,
        [jax.ShapeDtypeStruct(shape, jnp.float32) for shape in (block, w_block, w_block)],
        3,
        line + ring * 2,
        5,
        "scatter_expanded",
    )


def scatter_shared(n_dp, n, x, result, a, dq, dz, o, query):
    chips, chunks = n_dp // 2, 4
    block = (x.shape[0] // n, x.shape[1])
    w_block = (a.shape[1] // n_dp, dq.shape[1])
    small = LineExchange.scratch(n, block, x.dtype)
    line = LineGather.sems(n, chunks)
    ring = ProductScatter.scratch(chips, chunks, w_block, x.dtype)

    made = RowProduct.scratch(query)

    def kernel(
        x_ref, y, a_ref, dq_ref, dz_ref, o_ref, w, x_out, w_out, r_out, y_out, *refs
    ):
        parts = Parts(refs)
        at = Place(n_dp, n)
        a_out, b_out = Pieces(w_out, 0), Pieces(w_out, w_block[0])
        run_jobs(
            at.greet(line_all=True, ring=True),
            [
                line_exchange(at, x_ref, x_out, 0, parts.take(small)),
                RowProduct(dq_ref, w, True, None, r_out, parts.take(made), 30.0, 4.0),
                line_gather(at, y, y_out, 1, chunks, parts.take(line), 22.0),
                product_scatter(at, dz_ref, o_ref, b_out, chunks, parts.take(ring), 24.0, 1.0),
                product_scatter(at, a_ref, dq_ref, a_out, chunks, parts.take(ring), 24.0, 1.0),
            ],
        )

    return move(
        kernel,
        (x, result, by_lanes(a, n_dp), dq, by_lanes(dz, n_dp), o, query),
        6,
        (
            jax.ShapeDtypeStruct(block, jnp.float32),
            jax.ShapeDtypeStruct((n, 2 * w_block[0], w_block[1] // n), x.dtype),
            jax.ShapeDtypeStruct(dq.shape, jnp.float32),
            like(result, 1, n),
        ),
        3,
        small + made + line + ring * 2,
        6,
        "scatter_shared",
    )


def cols_and_shared(n_dp, n, rows, shared):
    chips = n_dp // 2
    count, width = rows.shape
    cols = width // n
    s_block = (shared.shape[0] // n_dp, shared.shape[1])
    p_block = (s_block[0] // n, s_block[1])
    switch = LineSwitch.sems(n)
    small = LineExchange.scratch(n, p_block, shared.dtype)
    ring = RingScatter.scratch(chips, 1, s_block, shared.dtype)

    def kernel(x, c, c_out, x_out, c_sum, *refs):
        parts = Parts(refs)
        at = Place(n_dp, n)
        run_jobs(
            at.greet(line_all=True, ring=True),
            [
                LineSwitch(
                    at,
                    lambda p: x.at[:, lanes(p, cols)],
                    x_out.at[pl.ds(at.t * count, count)],
                    parts.take(switch),
                ),
                ring_scatter(at, c, c_sum, 0, 1, parts.take(ring), 4.0),
                Later(line_exchange(at, c_sum, c_out, 0, parts.take(small)), 15.0),
            ],
        )

    return move(
        kernel,
        (rows, shared),
        1,
        [
            jax.ShapeDtypeStruct(p_block, jnp.float32),
            jax.ShapeDtypeStruct((n * count, cols), rows.dtype),
        ],
        1,
        [pltpu.VMEM(s_block, shared.dtype)] + switch + ring + small,
        7,
        "cols_and_shared",
    )


def fill_bias(bias, seg_row, seg_col, pos_row, pos_col):
    @pl.when(pl.program_id(0) == 0)
    def _():
        allowed = (seg_row[...] == seg_col[...]) & (pos_row[...] >= pos_col[...])
        bias[...] = jnp.where(allowed, 0.0, masked_score)


def attend_kernel(scale, q, k, v, seg_row, seg_col, pos_row, pos_col, o, log_total, bias):
    fill_bias(bias, seg_row, seg_col, pos_row, pos_col)
    scores = product(q[...], k[...], 1, 1) * scale + bias[...]
    row_max = jnp.max(scores, axis=1, keepdims=True)
    expo = jnp.exp(scores - row_max)
    row_total = jnp.sum(expo, axis=1, keepdims=True)
    probs = (expo / row_total).astype(jnp.bfloat16)
    o[...] = product(probs, v[...], 1, 0).astype(jnp.bfloat16)
    log_total[...] = jnp.broadcast_to(row_max + jnp.log(row_total), log_total.shape)


def attend_back_kernel(
    scale, q, do, log_total, k, v, seg_row, seg_col, pos_row, pos_col, dq, dkv, bias, dk, dv
):
    fill_bias(bias, seg_row, seg_col, pos_row, pos_col)

    @pl.when(pl.program_id(0) == 0)
    def _():
        dk[...] = jnp.zeros_like(dk)
        dv[...] = jnp.zeros_like(dv)

    scores = product(q[...], k[...], 1, 1) * scale + bias[...]
    probs = jnp.exp(scores - log_total[:, :1])
    prob_grad = product(do[...], v[...], 1, 1)
    inner = jnp.sum(probs * prob_grad, axis=1, keepdims=True)
    score_grad = (probs * (prob_grad - inner)).astype(jnp.bfloat16)
    dq[...] = (product(score_grad, k[...], 1, 0) * scale).astype(jnp.bfloat16)
    dk[...] += product(score_grad, q[...], 0, 0) * scale
    dv[...] += product(probs.astype(jnp.bfloat16), do[...], 0, 0)

    @pl.when(pl.program_id(0) == pl.num_programs(0) - 1)
    def _():
        dkv[...] = jnp.zeros_like(dkv)
        rows, (keys, size) = q.shape[0], k.shape
        last = (lax.axis_index("tensor") + 1) * rows
        window = pl.ds(pl.multiple_of(jnp.maximum(last - keys, 0), rows), keys)
        dkv[window, pl.ds(0, size)] = dk[...].astype(dkv.dtype)
        dkv[window, pl.ds(size, size)] = dv[...].astype(dkv.dtype)


def attention_specs(rows, keys, size):
    head = pl.BlockSpec((rows, size), lambda h: (0, h))
    whole = lambda *shape: pl.BlockSpec(shape, lambda h: (0, 0))
    masks = [whole(rows, 1), whole(1, keys), whole(rows, 1), whole(1, keys)]
    return head, whole(keys, size), masks


def attend(q, k, v, masks):
    rows, width = q.shape
    keys, size = k.shape
    head, shared, mask_specs = attention_specs(rows, keys, size)
    return pl.pallas_call(
        functools.partial(attend_kernel, size**-0.5),
        grid=(width // size,),
        in_specs=[head, shared, shared, *mask_specs],
        out_specs=(head, head),
        out_shape=(
            jax.ShapeDtypeStruct(q.shape, jnp.bfloat16),
            jax.ShapeDtypeStruct(q.shape, jnp.float32),
        ),
        scratch_shapes=[pltpu.VMEM((rows, keys), jnp.float32)],
        compiler_params=pltpu.CompilerParams(vmem_limit_bytes=32 * MIB),
        name="attend",
    )(q, k, v, *masks)


def attend_back(q, do, log_total, k, v, masks, total):
    rows, width = q.shape
    keys, size = k.shape
    head, shared, mask_specs = attention_specs(rows, keys, size)
    return pl.pallas_call(
        functools.partial(attend_back_kernel, size**-0.5),
        grid=(width // size,),
        in_specs=[head, head, head, shared, shared, *mask_specs],
        out_specs=(head, pl.BlockSpec((total, 2 * size), lambda h: (0, 0))),
        out_shape=(
            jax.ShapeDtypeStruct(q.shape, jnp.bfloat16),
            jax.ShapeDtypeStruct((total, 2 * size), jnp.bfloat16),
        ),
        scratch_shapes=[
            pltpu.VMEM((rows, keys), jnp.float32),
            pltpu.VMEM((keys, size), jnp.float32),
            pltpu.VMEM((keys, size), jnp.float32),
        ],
        compiler_params=pltpu.CompilerParams(vmem_limit_bytes=32 * MIB),
        name="attend_back",
    )(q, do, log_total, k, v, *masks)


def sum_all_kernel(n_dp, n, x_ref, o_ref, from_z, from_dp, part, s1, r1, s2, r2, s3, r3):
    g, t = lax.axis_index("dp"), lax.axis_index("tensor")
    rows = x_ref.shape[0] // n
    barrier = pltpu.get_barrier_semaphore()
    for k in range(1, n):
        pl.semaphore_signal(
            barrier, inc=1, device_id=(g, lax.rem(t + k, n)), device_id_type=MESH
        )
    for k in range(1, n_dp):
        pl.semaphore_signal(
            barrier, inc=1, device_id=(lax.rem(g + k, n_dp), t), device_id_type=MESH
        )
    pl.semaphore_wait(barrier, n - 1 + n_dp - 1)

    def piece(p):
        return pl.ds(pl.multiple_of(p * rows, rows), rows)

    first = []
    for k in range(1, n):
        p = lax.rem(t + k, n)
        first.append(
            pltpu.make_async_remote_copy(
                x_ref.at[piece(p)],
                from_z.at[k - 1],
                s1.at[k - 1],
                r1.at[k - 1],
                device_id=(g, p),
                device_id_type=MESH,
            )
        )
    for copy in first:
        copy.start()
    for copy in first:
        copy.wait()
    total = x_ref[piece(t)]
    for k in range(1, n):
        total = total + from_z[k - 1]
    part[...] = total
    second = []
    for k in range(1, n_dp):
        second.append(
            pltpu.make_async_remote_copy(
                part,
                from_dp.at[g],
                s2.at[k - 1],
                r2.at[k - 1],
                device_id=(lax.rem(g + k, n_dp), t),
                device_id_type=MESH,
            )
        )
    for copy in second:
        copy.start()
    from_dp[g] = part[...]
    for copy in second:
        copy.wait()
    total = from_dp[0]
    for k in range(1, n_dp):
        total = total + from_dp[k]
    o_ref[piece(t)] = total
    third = []
    for k in range(1, n):
        third.append(
            pltpu.make_async_remote_copy(
                o_ref.at[piece(t)],
                o_ref.at[piece(t)],
                s3.at[k - 1],
                r3.at[k - 1],
                device_id=(g, lax.rem(t + k, n)),
                device_id_type=MESH,
            )
        )
    for copy in third:
        copy.start()
    for copy in third:
        copy.wait()


def sum_all(x, n_dp, n, collective_id):
    rows = x.shape[0] // n
    return pl.pallas_call(
        functools.partial(sum_all_kernel, n_dp, n),
        out_shape=jax.ShapeDtypeStruct(x.shape, x.dtype),
        in_specs=[IN_VMEM],
        out_specs=IN_VMEM,
        scratch_shapes=[
            pltpu.VMEM((n - 1, rows, 128), x.dtype),
            pltpu.VMEM((n_dp, rows, 128), x.dtype),
            pltpu.VMEM((rows, 128), x.dtype),
        ]
        + [DMA((n - 1,))] * 2
        + [DMA((n_dp - 1,))] * 2
        + [DMA((n - 1,))] * 2,
        compiler_params=pltpu.CompilerParams(collective_id=collective_id, has_side_effects=True),
        name="sum_all",
    )(x)


def local(
    tokens,
    cotangent,
    lengths,
    counts,
    query_weight,
    query_moment,
    query_square,
    shared_weight,
    shared_moment,
    shared_square,
    project_weight,
    project_moment,
    project_square,
    expand_weight,
    expand_moment,
    expand_square,
    shrink_weight,
    shrink_moment,
    shrink_square,
    vectors_value,
    vectors_moment,
    vectors_square,
):
    device = lax.axis_index("dp")
    n_dp = lax.axis_size("dp")
    t = lax.axis_index("tensor")
    n = lax.axis_size("tensor")
    row_count, width = tokens.shape
    slots = 2 * row_count // n_dp
    part_rows, part_cols = row_count // n, width // n
    send_start = lax.dynamic_index_in_dim(exclusive_sum(counts, 1), device, 0, keepdims=False)
    send_amount = lax.dynamic_index_in_dim(counts, device, 0, keepdims=False)
    recv_start = lax.dynamic_index_in_dim(exclusive_sum(counts, 0), device, 1, keepdims=False)
    recv_amount = lax.dynamic_index_in_dim(counts, device, 1, keepdims=False)
    send_slots = slot_matrix(send_start, send_amount, slots, row_count)
    recv_slots = slot_matrix(recv_start, recv_amount, slots, row_count)

    def low(x):
        return x.astype(jnp.bfloat16)

    def pack(rows, out_slots):
        return low(mul_plain(out_slots, rows)).reshape(n_dp, slots, rows.shape[1])

    def exchange(packed):
        return lax.all_to_all(packed, "dp", split_axis=0, concat_axis=0, tiled=True)

    def unpack(arrived, in_slots):
        return low(mul_left_t(in_slots, arrived.reshape(n_dp * slots, arrived.shape[2])))

    mine_cols = [
        lax.dynamic_slice_in_dim(a, t * part_cols, part_cols, 1) for a in (tokens, cotangent)
    ]
    packed, query_here, project_here, shared_here = lax.optimization_barrier(
        (
            pack(jnp.concatenate(mine_cols, axis=1), send_slots),
            query_weight,
            project_weight,
            shared_weight,
        )
    )
    query_line, project_line, shared_line = gather_lines(
        n_dp, n, query_here, project_here, shared_here
    )
    arrived, query_line, shared_line = lax.optimization_barrier(
        (exchange(packed), query_line, shared_line)
    )
    owned = unpack(arrived, recv_slots)
    owned_rows, owned_grad, query_all, shared_all = rows_and_weights(
        n_dp, n, owned, query_line, shared_line
    )

    head_size = shared_all.shape[1] // 2
    hidden_width = expand_weight.shape[1]
    hidden_total = hidden_width * n
    gain_one = vectors_value[0:width]
    shift_one = vectors_value[width : 2 * width]
    gain_two = vectors_value[2 * width : 3 * width]
    shift_two = vectors_value[3 * width : 4 * width]
    query_bias = vectors_value[4 * width : 5 * width]
    project_bias = vectors_value[5 * width : 6 * width]
    shrink_bias = vectors_value[6 * width : 7 * width]
    expand_bias = lax.dynamic_slice_in_dim(
        vectors_value, 7 * width + t * hidden_width, hidden_width, 0
    )
    value_bias = vectors_value[7 * width + hidden_total : 7 * width + hidden_total + head_size]

    inputs_float = owned_rows.astype(jnp.float32)
    normed_one, norm_one_back = jax.vjp(layer_norm, inputs_float, gain_one, shift_one)
    normed_low = normed_one.astype(jnp.bfloat16)
    shared_out = mul_plain(normed_low, shared_all) + jnp.concatenate(
        [jnp.zeros((head_size,), jnp.float32), value_bias]
    )
    queries, shared_rows, project_all_t, owned_grad = shared_and_project(
        n_dp,
        n,
        owned,
        low(shared_out),
        project_line,
        normed_low,
        query_bias[None],
        query_all,
        owned_grad,
    )
    window = min(row_count, part_rows + longest)
    window_start = jnp.maximum((t + 1) * part_rows - window, 0)
    shared_window = lax.dynamic_slice_in_dim(shared_rows, window_start, window, 0)
    key_rows, value_rows = shared_window[:, :head_size], shared_window[:, head_size:]
    segment, position = segment_ids(lengths[0], row_count)
    masks = (
        lax.dynamic_slice_in_dim(segment, t * part_rows, part_rows, 0)[:, None],
        lax.dynamic_slice_in_dim(segment, window_start, window, 0)[None, :],
        lax.dynamic_slice_in_dim(position, t * part_rows, part_rows, 0)[:, None],
        lax.dynamic_slice_in_dim(position, window_start, window, 0)[None, :],
    )
    heads_out, log_total = attend(queries, key_rows, value_rows, masks)
    hidden_one = inputs_float + (mul_right_t(heads_out, project_all_t) + project_bias)
    normed_two, norm_two_back = jax.vjp(layer_norm, hidden_one, gain_two, shift_two)

    normed_two_low, expand_cols, shrink_rows_t = rows_and_expanded(
        n_dp, n, low(normed_two), expand_weight, shrink_weight
    )
    expand_pre = mul_plain(normed_two_low, expand_cols) + expand_bias
    activated, gelu_back = jax.vjp(gelu_tanh, expand_pre)
    activated_low = activated.astype(jnp.bfloat16)
    result_part = low(mul_right_t(activated_low, shrink_rows_t))
    own_result = lax.dynamic_slice_in_dim(result_part, t * part_rows, part_rows, 0)
    result_part = lax.dynamic_update_slice_in_dim(
        result_part, low(own_result + (hidden_one + shrink_bias)), t * part_rows, 0
    )
    result_part, owned_grad = lax.optimization_barrier((result_part, owned_grad))
    layer_cols = lax.psum_scatter(result_part, "tensor", scatter_dimension=1, tiled=True)
    shrink_grad_t = low(mul_left_t(owned_grad, activated_low))
    activated_grad = mul_plain(owned_grad, shrink_rows_t)
    expand_pre_grad = gelu_back(activated_grad)[0].astype(jnp.bfloat16)
    expand_grad = low(mul_left_t(normed_two_low, expand_pre_grad))
    expand_bias_grad = jnp.sum(expand_pre_grad.astype(jnp.float32), axis=0)
    normed_two_part = mul_right_t(expand_pre_grad, expand_cols).astype(jnp.bfloat16)

    normed_two_grad, expand_part, shrink_part_t = scatter_expanded(
        n_dp, n, normed_two_part, expand_grad, shrink_grad_t
    )
    shrink_part = turned(shrink_part_t)
    output_cols = unpack(exchange(pack(layer_cols, recv_slots)), send_slots)
    output_float = lax.dynamic_slice_in_dim(owned_grad, t * part_rows, part_rows, 0).astype(
        jnp.float32
    )
    shrink_bias_grad = jnp.sum(output_float, axis=0)
    hidden_from_norm, gain_two_grad, shift_two_grad = norm_two_back(normed_two_grad)
    hidden_grad = output_float + hidden_from_norm
    branch_grad = hidden_grad.astype(jnp.bfloat16)
    project_bias_grad = jnp.sum(branch_grad.astype(jnp.float32), axis=0)
    heads_grad = low(mul_plain(branch_grad, project_all_t))
    query_grad, shared_part = attend_back(
        queries, heads_grad, log_total, key_rows, value_rows, masks, row_count
    )
    shared_grad, weight_sums, normed_one_grad, output_rows = scatter_shared(
        n_dp,
        n,
        shared_part,
        output_cols,
        normed_low,
        query_grad,
        branch_grad,
        heads_out,
        query_all,
    )
    shared_grad = low(shared_grad)
    query_bias_grad = jnp.sum(query_grad.astype(jnp.float32), axis=0)
    normed_one_grad = normed_one_grad + mul_right_t(shared_grad, shared_all)
    inputs_from_norm, gain_one_grad, shift_one_grad = norm_one_back(normed_one_grad)
    input_result = (hidden_grad + inputs_from_norm).astype(jnp.bfloat16)
    shared_weight_grad = mul_left_t(normed_low, shared_grad)
    value_bias_grad = jnp.sum(shared_grad[:, head_size:].astype(jnp.float32), axis=0)

    shared_piece, input_cols = cols_and_shared(n_dp, n, input_result, low(shared_weight_grad))
    input_cols, weight_sums = lax.optimization_barrier((input_cols, weight_sums))
    grads = lax.psum_scatter(
        weight_sums.reshape(-1, part_cols), "tensor", scatter_dimension=0, tiled=True
    )
    back = unpack(exchange(pack(input_cols, recv_slots)), send_slots)
    back, grads = lax.optimization_barrier((back, grads))
    grad_rows = lax.all_gather(back, "tensor", axis=1, tiled=True)
    tall = grads.shape[0] // 2
    query_part = grads[:tall].astype(jnp.float32)
    project_part = turned(grads[tall:].astype(jnp.float32))
    output_back = output_rows.astype(jnp.float32)
    token_rms = jnp.sqrt(jnp.mean(output_back * output_back, axis=1))

    split_part = lax.dynamic_update_slice_in_dim(
        jnp.zeros((hidden_total,), jnp.float32), expand_bias_grad, t * hidden_width, 0
    )
    vector_part = jnp.concatenate(
        [
            gain_one_grad,
            shift_one_grad,
            gain_two_grad,
            shift_two_grad,
            query_bias_grad,
            project_bias_grad,
            shrink_bias_grad,
            split_part,
            value_bias_grad,
        ]
    )
    local_squares = (
        jnp.sum(query_part * query_part)
        + jnp.sum(expand_part * expand_part)
        + jnp.sum(shared_piece * shared_piece)
        + jnp.sum(project_part * project_part)
        + jnp.sum(shrink_part * shrink_part)
    )
    length = vector_part.shape[0]
    unit = n * 8 * 128
    padded = -(-(length + 1) // unit) * unit
    everything = jnp.concatenate(
        [vector_part, local_squares[None], jnp.zeros((padded - length - 1,), jnp.float32)]
    )
    summed = sum_all(everything.reshape(padded // 128, 128), n_dp, n, 8).reshape(padded)
    vector_grad, weight_squares = summed[:length], summed[length]
    grad_size = jnp.sqrt(weight_squares + jnp.sum(vector_grad * vector_grad))
    clip_factor = jnp.minimum(1.0, clip_level / (grad_size + 1e-06))
    clipped_vectors = clip_factor * vector_grad
    query_new = adamw_step(
        query_weight,
        query_moment,
        query_square,
        clip_factor * query_part,
        rate_matrix * width ** (-0.5),
    )
    shared_new = adamw_step(
        shared_weight,
        shared_moment,
        shared_square,
        clip_factor * shared_piece,
        rate_attention * width ** (-0.5),
    )
    project_new = adamw_step(
        project_weight,
        project_moment,
        project_square,
        clip_factor * project_part,
        rate_attention * width ** (-0.5),
    )
    expand_new = adamw_step(
        expand_weight,
        expand_moment,
        expand_square,
        clip_factor * expand_part,
        rate_matrix * width ** (-0.5),
    )
    shrink_new = adamw_step(
        shrink_weight,
        shrink_moment,
        shrink_square,
        clip_factor * shrink_part,
        rate_matrix * hidden_total ** (-0.5),
    )
    vectors_new = adamw_step(
        vectors_value, vectors_moment, vectors_square, clipped_vectors, rate_vector
    )
    return (
        output_rows,
        grad_rows,
        grad_size,
        *query_new,
        *shared_new,
        *project_new,
        *expand_new,
        *shrink_new,
        *vectors_new,
        clipped_vectors,
        token_rms,
    )


def solution(mesh):
    by_rows = P("dp", None)
    query = P("dp", "tensor")
    shared = P(("dp", "tensor"), None)
    project = P("tensor", "dp")
    return jax.shard_map(
        local,
        mesh=mesh,
        in_specs=(
            *(by_rows,) * 3,
            P(),
            *(query,) * 3,
            *(shared,) * 3,
            *(project,) * 3,
            *(query,) * 3,
            *(project,) * 3,
            *(P(),) * 3,
        ),
        out_specs=(
            *(by_rows,) * 2,
            P(),
            *(query,) * 3,
            *(shared,) * 3,
            *(project,) * 3,
            *(query,) * 3,
            *(project,) * 3,
            *(P(),) * 4,
            P("dp"),
        ),
        check_vma=False,
    )
```

```python
import functools

import jax
import jax.numpy as jnp
from jax import lax
from jax.experimental.layout import Layout, with_layout_constraint
from jax.experimental import pallas as pl
from jax.experimental.pallas import tpu as pltpu
from jax.sharding import PartitionSpec as P

STEP = 10


beta_one = 0.9
beta_two = 0.95
adam_epsilon = 1e-08
decay_rate = 0.1
clip_level = 1.0
norm_epsilon = 1e-05
rate_matrix = 0.6
rate_attention = 2.4
rate_vector = 0.3
masked_score = -1e30
longest = 512

MESH = pl.DeviceIdType.MESH
IN_PLACE = pl.BlockSpec(memory_space=pl.ANY)
IN_VMEM = pl.BlockSpec(memory_space=pltpu.VMEM)
DMA = pltpu.SemaphoreType.DMA
MIB = 2**20


def mul_plain(left, right):
    return jnp.dot(left, right, preferred_element_type=jnp.float32)


def mul_right_t(left, right):
    return lax.dot_general(
        left, right, (((1,), (1,)), ((), ())), preferred_element_type=jnp.float32
    )


def mul_left_t(left, right):
    return lax.dot_general(
        left, right, (((0,), (0,)), ((), ())), preferred_element_type=jnp.float32
    )


def product(left, right, left_dim, right_dim):
    return lax.dot_general(
        left, right, (((left_dim,), (right_dim,)), ((), ())), preferred_element_type=jnp.float32
    )


def layer_norm(values, scaling, offset):
    average = jnp.mean(values, axis=-1, keepdims=True)
    centered = values - average
    variance = jnp.mean(centered * centered, axis=-1, keepdims=True)
    return centered * lax.rsqrt(variance + norm_epsilon) * scaling + offset


def gelu_tanh(values):
    return jax.nn.gelu(values, approximate=True)


def exclusive_sum(table, axis_index):
    return jnp.cumsum(table, axis=axis_index) - table


def segment_ids(seq_lengths, row_count):
    position = jnp.arange(row_count, dtype=jnp.int32)
    starts = jnp.cumsum(seq_lengths) - seq_lengths
    segment = jnp.sum((starts[None, :] <= position[:, None]).astype(jnp.int32), axis=1)
    return (segment, position)


def slot_matrix(starts, amounts, slots, row_count):
    offsets = jnp.arange(slots, dtype=jnp.int32)
    picked = jnp.where(offsets[None, :] < amounts[:, None], starts[:, None] + offsets[None, :], -1)
    position = jnp.arange(row_count, dtype=jnp.int32)
    return (picked.reshape(-1)[:, None] == position[None, :]).astype(jnp.bfloat16)


def turned(x):
    return with_layout_constraint(x.T, Layout(major_to_minor=(0, 1)))


def adamw_step(weight, moment, square, gradient, rate):
    moment_new = beta_one * moment + (1.0 - beta_one) * gradient
    square_new = beta_two * square + (1.0 - beta_two) * gradient * gradient
    moment_hat = moment_new / (1.0 - beta_one**STEP)
    square_hat = square_new / (1.0 - beta_two**STEP)
    weight_new = weight - rate * (
        moment_hat / (jnp.sqrt(square_hat) + adam_epsilon) + decay_rate * weight
    )
    return (weight_new, moment_new, square_new)


def remote(src, dst, send_sem, recv_sem, device):
    return pltpu.make_async_remote_copy(
        src, dst, send_sem, recv_sem, device_id=device, device_id_type=MESH
    )


class Place:
    def __init__(self, n_dp, n):
        self.n, self.chips = n, n_dp // 2
        self.dp, self.t = lax.axis_index("dp"), lax.axis_index("tensor")
        self.core, chip = lax.rem(self.dp, 2), lax.div(self.dp, 2)
        side = round(self.chips**0.5)
        self.side = side if side * side == self.chips else self.chips
        self.pos = self.snake(chip)
        self.sibling = (self.dp + 1 - 2 * self.core, self.t)
        self.after = (self.block(self.ring(self.pos + 1), self.core), self.t)
        self.before = (self.block(self.ring(self.pos - 1), self.core), self.t)
        self.left, self.right = (self.dp, self.t - 1), (self.dp, self.t + 1)

    def snake(self, index):
        row, col = lax.div(index, self.side), lax.rem(index, self.side)
        odd = lax.rem(row, 2)
        return row * self.side + col + odd * (self.side - 1 - 2 * col)

    def ring(self, pos):
        return lax.rem(pos + 2 * self.chips, self.chips)

    def block(self, pos, core):
        return self.snake(pos) * 2 + core

    def greet(self, line=False, line_all=False, ring=False):
        barrier = pltpu.get_barrier_semaphore()
        peers = 0

        def call(device):
            pl.semaphore_signal(barrier, inc=1, device_id=device, device_id_type=MESH)

        if ring:
            for device in (self.sibling, self.after, self.before):
                call(device)
            peers += 3
        if line_all:
            for k in range(1, self.n):
                call((self.dp, lax.rem(self.t + k, self.n)))
            peers += self.n - 1
        elif line:
            pl.when(self.t > 0)(lambda: call(self.left))
            pl.when(self.t < self.n - 1)(lambda: call(self.right))
            peers += (self.t > 0).astype(jnp.int32) + (self.t < self.n - 1).astype(jnp.int32)
        return lambda: pl.semaphore_wait(barrier, peers)


class LineGather:
    @staticmethod
    def sems(n, chunks):
        return [DMA((n - 1, chunks))] * 4 + [DMA]

    def __init__(self, at, chunks, first, place, sems, whole, unit=1.0):
        self.unit = unit
        self.at, self.chunks, self.first, self.place, self.sems = at, chunks, first, place, sems
        self.own = pltpu.make_async_copy(whole[0], whole[1], sems[4])

    def copy(self, h, c, right):
        at = self.at
        dst = self.place(at.t - h if right else at.t + h, c)
        src = self.first(c) if h == 0 else dst
        s, r = self.sems[0:2] if right else self.sems[2:4]
        return remote(src, dst, s.at[h, c], r.at[h, c], at.right if right else at.left)

    def receive(self, h, c, right):
        at = self.at
        dst = self.place(at.t - 1 - h if right else at.t + 1 + h, c)
        s, r = self.sems[0:2] if right else self.sems[2:4]
        remote(dst, dst, s.at[h, c], r.at[h, c], at.left if right else at.right).wait_recv()

    def sends(self, h, right):
        t, n = self.at.t, self.at.n
        return (t >= h) & (t < n - 1) if right else (t + h <= n - 1) & (t > 0)

    def gets(self, h, right):
        return self.at.t - 1 - h >= 0 if right else self.at.t + 1 + h <= self.at.n - 1

    def every(self):
        for h in range(self.at.n - 1):
            for c in range(self.chunks):
                for right in (True, False):
                    yield h, c, right

    def prepare(self):
        self.own.start()

    def prepared(self):
        self.own.wait()

    def start(self):
        for h, c, right in self.every():
            if h == 0:
                pl.when(self.sends(h, right))(lambda: self.copy(h, c, right).start())

    def step(self, h, c, right):
        pl.when(self.gets(h, right))(lambda: self.receive(h, c, right))
        if h + 1 < self.at.n - 1:
            pl.when(self.sends(h + 1, right))(lambda: self.copy(h + 1, c, right).start())

    def steps(self):
        return [
            (self.unit * (which[0] + (which[1] + 1) / self.chunks), functools.partial(self.step, *which))
            for which in self.every()
        ]

    def finish(self):
        for h, c, right in self.every():
            pl.when(self.sends(h, right))(lambda: self.copy(h, c, right).wait_send())


class LineScatter:
    @staticmethod
    def scratch(n, chunks, block, dtype):
        return [pltpu.VMEM((n - 1, *block), dtype)] * 2 + [DMA((n - 1, chunks))] * 4

    def __init__(self, at, chunks, own, out, scratch, unit=1.0):
        self.unit = unit
        self.at, self.chunks, self.own, self.out = at, chunks, own, out
        self.held, self.sems = scratch[:2], scratch[2:6]
        self.rows = self.held[0].shape[1] // chunks

    def parts(self, k, c, right):
        side = 0 if right else 1
        s, r = self.sems[2 * side : 2 * side + 2]
        return self.held[side].at[k, pl.ds(c * self.rows, self.rows)], s.at[k, c], r.at[k, c]

    def send(self, k, c, right, first):
        slot, s, r = self.parts(k, c, right)
        src = self.own(self.target(k, right), c) if first else slot
        return remote(src, slot, s, r, self.at.right if right else self.at.left)

    def receive(self, k, c, right):
        slot, s, r = self.parts(k, c, right)
        remote(slot, slot, s, r, self.at.left if right else self.at.right).wait_recv()

    def target(self, k, right):
        return self.at.n - 1 - k if right else k

    def every(self):
        for k in range(self.at.n - 1):
            for c in range(self.chunks):
                for right in (True, False):
                    yield k, c, right

    def prepare(self):
        pass

    def prepared(self):
        pass

    def start(self):
        t, n = self.at.t, self.at.n
        for k, c, right in self.every():
            first = (t == (0 if right else n - 1)) & (t != self.target(k, right))
            pl.when(first)(lambda: self.send(k, c, right, True).start())

    def add(self, k, c, right):
        self.receive(k, c, right)
        slot = self.parts(k, c, right)[0]
        mine = self.own(self.target(k, right), c)[...]
        slot[...] = (slot[...].astype(jnp.float32) + mine.astype(jnp.float32)).astype(slot.dtype)
        self.send(k, c, right, False).start()

    def step(self, k, c, right):
        t, n, d = self.at.t, self.at.n, self.target(k, right)
        passes = (t > 0) & (t < d) if right else (t < n - 1) & (t > d)
        pl.when(passes)(lambda: self.add(k, c, right))

    def steps(self):
        return [
            (self.unit * (which[0] + (which[1] + 1) / self.chunks), functools.partial(self.step, *which))
            for which in self.every()
        ]

    def finish(self):
        t, n = self.at.t, self.at.n
        for k, c, right in self.every():
            pl.when(t == self.target(k, right))(lambda: self.receive(k, c, right))
        for c in range(self.chunks):
            span = pl.ds(c * self.rows, self.rows)
            self.out[span] = self.own(t, c)[...].astype(self.out.dtype)

        def more(block):
            self.out[...] += block[...].astype(self.out.dtype)

        pl.when(t > 0)(lambda: more(self.held[0].at[n - 1 - t]))
        pl.when(t < n - 1)(lambda: more(self.held[1].at[t]))
        for k, c, right in self.every():
            d = self.target(k, right)
            pl.when(t < d if right else t > d)(lambda: self.send(k, c, right, False).wait_send())


class LineExchange:
    @staticmethod
    def scratch(n, block, dtype):
        return [pltpu.VMEM((n - 1, *block), dtype)] + [DMA((n - 1,))] * 2

    def __init__(self, at, source, out, scratch):
        self.at, self.source, self.out = at, source, out
        self.held = scratch[0]
        self.copies = []
        for k in range(1, at.n):
            p = lax.rem(at.t + k, at.n)
            self.copies.append(
                remote(
                    source(p),
                    self.held.at[k - 1],
                    scratch[1].at[k - 1],
                    scratch[2].at[k - 1],
                    (at.dp, p),
                )
            )

    def prepare(self):
        pass

    def prepared(self):
        pass

    def start(self):
        for copy in self.copies:
            copy.start()

    def steps(self):
        return []

    def finish(self):
        for copy in self.copies:
            copy.wait()
        total = self.source(self.at.t)[...].astype(jnp.float32)
        for k in range(self.at.n - 1):
            total = total + self.held[k].astype(jnp.float32)
        self.out[...] = total.astype(self.out.dtype)


class RingGather:
    @staticmethod
    def sems(chips, chunks):
        hops = chips // 2
        return [DMA((2, hops, chunks))] * 4 + [DMA((chunks,))] * 2 + [DMA]

    def __init__(self, at, chunks, first, place, sems, whole, unit=1.0):
        self.unit = unit
        self.at, self.chunks, self.first, self.place, self.sems = at, chunks, first, place, sems
        self.hops = at.chips // 2
        self.own = pltpu.make_async_copy(whole[0], whole[1], sems[6])

    def every(self):
        for h in range(self.hops):
            for c in range(self.chunks):
                for way in (0, 1):
                    if h < self.hops - 1 or c % 2 == way:
                        yield h, c, way

    def origin(self, steps, way, core):
        return self.at.block(self.at.ring(self.at.pos + (steps if way else -steps)), core)

    def onward(self, h, c, way):
        dst = self.place(self.origin(h, way, self.at.core), c)
        src = self.first(c) if h == 0 else dst
        s, r = self.sems[0:2]
        device = self.at.before if way else self.at.after
        return remote(src, dst, s.at[way, h, c], r.at[way, h, c], device)

    def arrival(self, h, c, way):
        dst = self.place(self.origin(h + 1, way, self.at.core), c)
        s, r = self.sems[0:2]
        device = self.at.after if way else self.at.before
        return remote(dst, dst, s.at[way, h, c], r.at[way, h, c], device)

    def across(self, h, c, way, core):
        dst = self.place(self.origin(h + 1, way, core), c)
        s, r = self.sems[2:4]
        return remote(dst, dst, s.at[way, h, c], r.at[way, h, c], self.at.sibling)

    def across_own(self, c, core):
        dst = self.place(self.origin(0, 0, core), c)
        s, r = self.sems[4:6]
        return remote(self.first(c), dst, s.at[c], r.at[c], self.at.sibling)

    def prepare(self):
        self.own.start()

    def prepared(self):
        self.own.wait()

    def start(self):
        for h, c, way in self.every():
            if h == 0:
                self.onward(h, c, way).start()
        for c in range(self.chunks):
            self.across_own(c, self.at.core).start()

    def step(self, h, c, way):
        self.arrival(h, c, way).wait_recv()
        if (h + 1, c, way) in list(self.every()):
            self.onward(h + 1, c, way).start()
        self.across(h, c, way, self.at.core).start()

    def steps(self):
        when = 0.0
        for h, c, way in self.every():
            when += self.unit / self.chunks / 2
            yield when, functools.partial(self.step, h, c, way)

    def finish(self):
        other = 1 - self.at.core
        for c in range(self.chunks):
            self.across_own(c, other).wait_recv()
            self.across_own(c, self.at.core).wait_send()
        for h, c, way in self.every():
            self.across(h, c, way, other).wait_recv()
            self.across(h, c, way, self.at.core).wait_send()
            self.onward(h, c, way).wait_send()


class RingScatter:
    @staticmethod
    def scratch(chips, chunks, block, dtype):
        hops = chips // 2
        return (
            [pltpu.VMEM((chips, *block), dtype)] * 2
            + [pltpu.VMEM((2, hops, *block), dtype)]
            + [DMA((chips, chunks))] * 3
            + [DMA((2, hops, chunks))] * 2
        )

    def __init__(self, at, chunks, source, out, scratch, unit=1.0):
        self.unit = unit
        self.at, self.chunks, self.source, self.out = at, chunks, source, out
        self.hops = at.chips // 2
        self.mine, self.other, self.held = scratch[:3]
        self.load_sem, self.s1, self.r1, self.s2, self.r2 = scratch[3:8]
        self.rows = self.held.shape[2] // chunks

    def span(self, c):
        return pl.ds(c * self.rows, self.rows)

    def target(self, place, core):
        return self.at.block(self.at.ring(self.at.pos + place), core)

    def load(self, place, c):
        src = self.source(self.target(place, self.at.core), c)
        dst = self.mine.at[place, self.span(c)]
        return pltpu.make_async_copy(src, dst, self.load_sem.at[place, c])

    def across(self, place, c):
        src = self.source(self.target(place, 1 - self.at.core), c)
        dst = self.other.at[place, self.span(c)]
        return remote(src, dst, self.s1.at[place, c], self.r1.at[place, c], self.at.sibling)

    def sent(self, e, c, way):
        return e < self.hops or c % 2 == way

    def onward(self, e, c, way):
        place = self.at.chips - e if way else e
        src, dst = self.mine.at[place, self.span(c)], self.held.at[way, e - 1, self.span(c)]
        device = self.at.before if way else self.at.after
        return remote(src, dst, self.s2.at[way, e - 1, c], self.r2.at[way, e - 1, c], device)

    def arrival(self, e, c, way):
        dst = self.held.at[way, e, self.span(c)]
        device = self.at.after if way else self.at.before
        return remote(dst, dst, self.s2.at[way, e, c], self.r2.at[way, e, c], device)

    def places(self):
        order = []
        for e in range(self.hops, 0, -1):
            order += [e] if e == self.hops else [e, self.at.chips - e]
        return order + [0]

    def prepare(self):
        for place in self.places():
            for c in range(self.chunks):
                self.load(place, c).start()

    def prepared(self):
        pass

    def start(self):
        self.send_across(self.places()[:1])

    def send_across(self, places):
        for place in places:
            for c in range(self.chunks):
                self.across(place, c).start()

    def loaded(self, place, c):
        self.load(place, c).wait()

    def base(self, place, c):
        self.loaded(place, c)
        self.across(place, c).wait_recv()
        total = self.mine[place, self.span(c)].astype(jnp.float32)
        return total + self.other[place, self.span(c)].astype(jnp.float32)

    def arrived(self, e, c, way):
        self.arrival(e, c, way).wait_recv()
        return self.held[way, e, self.span(c)].astype(jnp.float32)

    def step(self, e, c, way):
        place = self.at.chips - e if way else e
        total = self.base(place, c)
        if e < self.hops and self.sent(e + 1, c, way):
            total += self.arrived(e, c, way)
        self.mine[place, self.span(c)] = total.astype(self.mine.dtype)
        self.onward(e, c, way).start()

    def last(self, c):
        total = self.base(0, c)
        for way in (0, 1):
            if self.sent(1, c, way):
                total += self.arrived(0, c, way)
        self.out[self.span(c)] = total.astype(self.out.dtype)

    def every(self):
        for e in range(self.hops, 0, -1):
            for c in range(self.chunks):
                for way in (0, 1):
                    if self.sent(e, c, way):
                        yield e, c, way

    def steps(self):
        yield 0.0, functools.partial(self.send_across, self.places()[1:])
        yield from self.sum_steps()

    def sum_steps(self):
        when = 0.0
        for e, c, way in self.every():
            yield when, functools.partial(self.step, e, c, way)
            when += self.unit / self.chunks / 2
        for c in range(self.chunks):
            yield when + self.unit * (c + 1) / self.chunks, functools.partial(self.last, c)

    def finish(self):
        for place in self.places():
            for c in range(self.chunks):
                self.across(place, c).wait_send()
        for e, c, way in self.every():
            self.onward(e, c, way).wait_send()


class ProductScatter(RingScatter):
    @staticmethod
    def scratch(chips, chunks, block, dtype):
        return RingScatter.scratch(chips, chunks, block, dtype) + [pltpu.VMEM((2, *block), dtype)]

    def __init__(self, at, chunks, left, right, out, scratch, unit, cost):
        super().__init__(at, chunks, None, out, scratch[:-1], unit)
        self.left, self.right, self.stage, self.cost = left, right, scratch[-1], cost

    def across(self, place, c):
        src = self.stage.at[self.places().index(place) % 2, self.span(c)]
        dst = self.other.at[place, self.span(c)]
        return remote(src, dst, self.s1.at[place, c], self.r1.at[place, c], self.at.sibling)

    def product(self, place, core):
        block = self.held.shape[2]
        cols = lanes(self.target(place, core), block) if block % 128 == 0 else None
        if cols is None:
            left = self.left[pl.ds(pl.multiple_of(self.target(place, core) * block, block), block)]
            total = product(left, self.right[...], 1, 0)
        else:
            total = product(self.left[:, cols], self.right[...], 0, 0)
        return total.astype(self.mine.dtype)

    def work(self, i, place, here):
        if here:
            self.mine[place] = self.product(place, self.at.core)
            return
        if i >= 2:
            for c in range(self.chunks):
                self.across(self.places()[i - 2], c).wait_send()
        self.stage[i % 2] = self.product(place, 1 - self.at.core)
        for c in range(self.chunks):
            self.across(place, c).start()

    def prepare(self):
        pass

    def start(self):
        pass

    def loaded(self, place, c):
        pass

    def steps(self):
        when = 0.0
        for i, place in enumerate(self.places()):
            for here in (False, True):
                yield when, functools.partial(self.work, i, place, here)
                when += self.cost
        for when, step in self.sum_steps():
            place = 0
            if len(step.args) == 3:
                e, _, way = step.args
                place = self.at.chips - e if way else e
            yield max(when, (2 * self.places().index(place) + 2) * self.cost), step

    def finish(self):
        for place in self.places()[-2:]:
            for c in range(self.chunks):
                self.across(place, c).wait_send()
        for e, c, way in self.every():
            self.onward(e, c, way).wait_send()


class LineSwitch:
    @staticmethod
    def sems(n):
        return [DMA((n - 1,))] * 2 + [DMA]

    def __init__(self, at, source, target, sems):
        self.own = pltpu.make_async_copy(source(at.t), target, sems[2])
        self.copies = []
        for k in range(1, at.n):
            p = lax.rem(at.t + k, at.n)
            self.copies.append(
                remote(source(p), target, sems[0].at[k - 1], sems[1].at[k - 1], (at.dp, p))
            )

    def prepare(self):
        self.own.start()

    def prepared(self):
        self.own.wait()

    def start(self):
        for copy in self.copies:
            copy.start()

    def steps(self):
        return []

    def finish(self):
        for copy in self.copies:
            copy.wait()


class Pieces:
    def __init__(self, ref, begin):
        self.ref, self.begin, self.dtype = ref, begin, ref.dtype

    def __setitem__(self, span, value):
        pieces, _, cols = self.ref.shape
        for k in range(pieces):
            rows = pl.ds(self.begin + span.start, span.size)
            self.ref[k, rows] = value[:, k * cols : (k + 1) * cols]


class Later:
    def __init__(self, job, when):
        self.job, self.when = job, when

    def prepare(self):
        pass

    def prepared(self):
        pass

    def start(self):
        pass

    def steps(self):
        yield self.when, self.job.start

    def finish(self):
        self.job.finish()


class Begun:
    def __init__(self, job, when):
        self.job, self.when = job, when
        self.prepare, self.prepared, self.finish = job.prepare, job.prepared, job.finish

    def start(self):
        pass

    def steps(self):
        yield self.when, self.job.start
        for when, step in self.job.steps():
            yield self.when + when, step


class Ended:
    def __init__(self, job, when):
        self.job, self.when = job, when
        self.prepare, self.prepared, self.start = job.prepare, job.prepared, job.start

    def steps(self):
        yield from self.job.steps()
        yield self.when, self.job.finish

    def finish(self):
        pass


class GatheredProduct:
    @staticmethod
    def scratch(n, block, weight):
        held = pltpu.VMEM((n - 1, 2, *block.shape), block.dtype)
        return [pltpu.VMEM(weight.shape, weight.dtype), DMA, held, DMA((n - 1, 2))]

    def __init__(self, line, own, gathered, weight, bias, out, scratch, begin, cost):
        self.line, self.own, self.gathered, self.bias, self.out = line, own, gathered, bias, out
        self.weight, self.held, self.sems = scratch[0], scratch[2], scratch[3]
        self.copy = pltpu.make_async_copy(weight, scratch[0], scratch[1])
        self.begin, self.cost, self.tile = begin, cost, 512

    def prepare(self):
        pass

    def prepared(self):
        pass

    def start(self):
        pass

    def place(self, h, right):
        rows, t = self.own.shape[0], self.line.at.t
        return pl.ds(pl.multiple_of((t - 1 - h if right else t + 1 + h) * rows, rows), rows)

    def load(self, h, right):
        side = 0 if right else 1
        return pltpu.make_async_copy(
            self.gathered.at[self.place(h, right)], self.held.at[h, side], self.sems.at[h, side]
        )

    def multiply(self, block, rows):
        for j in range(self.out.shape[1] // self.tile):
            span = pl.ds(j * self.tile, self.tile)
            total = product(block[...], self.weight[:, span], 1, 0) + self.bias[:, span]
            self.out[rows, span] = total

    def arrived(self, h, right):
        pl.when(self.line.gets(h, right))(lambda: self.load(h, right).start())

    def work(self, h, right):
        @pl.when(self.line.gets(h, right))
        def _():
            self.load(h, right).wait()
            self.multiply(self.held.at[h, 0 if right else 1], self.place(h, right))

    def mine(self):
        rows = self.own.shape[0]
        self.multiply(self.own, pl.ds(pl.multiple_of(self.line.at.t * rows, rows), rows))

    def steps(self):
        yield self.begin - 4.0, self.copy.start
        yield self.begin, self.copy.wait
        yield self.begin, self.mine
        when = self.begin + self.cost
        for h in range(self.line.at.n - 1):
            come = self.line.unit * (h + 1) + 0.5
            for right in (True, False):
                yield come, functools.partial(self.arrived, h, right)
            when = max(when, come + 1.0)
            for right in (True, False):
                yield when, functools.partial(self.work, h, right)
                when += self.cost

    def finish(self):
        pass


class RowProduct:
    @staticmethod
    def scratch(weight):
        return [pltpu.VMEM(weight.shape, weight.dtype), DMA]

    def __init__(self, left, weight, turn, bias, out, scratch, begin, cost):
        self.left, self.turn, self.bias, self.out = left, turn, bias, out
        self.held, self.begin, self.cost = scratch[0], begin, cost
        self.copy = pltpu.make_async_copy(weight, scratch[0], scratch[1])
        self.tile = 256

    def prepare(self):
        self.copy.start()

    def prepared(self):
        pass

    def start(self):
        pass

    def work(self, j):
        span = pl.ds(j * self.tile, self.tile)
        if self.turn:
            total = product(self.left[...], self.held[span], 1, 1)
        else:
            total = product(self.left[...], self.held[:, span], 1, 0)
        if self.bias is not None:
            total += self.bias[:, span]
        self.out[:, span] = total.astype(self.out.dtype)

    def steps(self):
        yield self.begin, self.copy.wait
        for j in range(self.out.shape[1] // self.tile):
            yield self.begin + j * self.cost, functools.partial(self.work, j)

    def finish(self):
        pass


def run_jobs(met, jobs):
    for job in jobs:
        job.prepare()
    for job in jobs:
        job.prepared()
    met()
    for job in jobs:
        job.start()
    ordered = []
    for i, job in enumerate(jobs):
        ordered += [(when, i, j, step) for j, (when, step) in enumerate(job.steps())]
    for _, _, _, step in sorted(ordered, key=lambda entry: entry[:3]):
        step()
    for job in jobs:
        job.finish()


def rows_of(ref, step):
    return lambda c: ref.at[pl.ds(c * step, step)]


def lanes(index, count):
    return pl.ds(pl.multiple_of(index * count, count), count)


def move(kernel, inputs, in_vmem, outs, out_vmem, scratch, collective_id, name, aliases=None):
    return pl.pallas_call(
        kernel,
        out_shape=tuple(outs),
        in_specs=[IN_VMEM if i < in_vmem else IN_PLACE for i in range(len(inputs))],
        out_specs=tuple(IN_VMEM if i < out_vmem else IN_PLACE for i in range(len(outs))),
        scratch_shapes=scratch,
        compiler_params=pltpu.CompilerParams(
            collective_id=collective_id, has_side_effects=True, vmem_limit_bytes=56 * MIB
        ),
        input_output_aliases=aliases or {},
        name=name,
    )(*inputs)


def line_gather(at, x, out, axis, chunks, sems, unit=1.0):
    rows, cols = x.shape
    step = rows // chunks
    if axis == 0:
        place = lambda b, c: out.at[pl.ds(b * rows + c * step, step)]
        whole = out.at[pl.ds(at.t * rows, rows)]
    else:
        place = lambda b, c: out.at[pl.ds(c * step, step), lanes(b, cols)]
        whole = out.at[:, lanes(at.t, cols)]
    return LineGather(at, chunks, rows_of(x, step), place, sems, (x, whole), unit)


def ring_gather(at, x, out, axis, chunks, sems, unit=1.0):
    rows, cols = x.shape
    step = rows // chunks
    if axis == 0:
        place = lambda b, c: out.at[pl.ds(b * rows + c * step, step)]
        whole = out.at[pl.ds(at.dp * rows, rows)]
    else:
        place = lambda b, c: out.at[pl.ds(c * step, step), lanes(b, cols)]
        whole = out.at[:, lanes(at.dp, cols)]
    return RingGather(at, chunks, rows_of(x, step), place, sems, (x, whole), unit)


def blocks_of(x, out, axis, chunks):
    rows, cols = out.shape
    step = rows // chunks
    if axis == 0:
        return lambda b, c: x.at[pl.ds(pl.multiple_of(b * rows + c * step, step), step)]
    return lambda b, c: x.at[pl.ds(c * step, step), lanes(b, cols)]


def line_exchange(at, x, out, axis, scratch):
    block = blocks_of(x, out, axis, 1)
    return LineExchange(at, lambda p: block(p, 0), out, scratch)


def line_scatter(at, x, out, axis, chunks, scratch, unit=1.0):
    return LineScatter(at, chunks, blocks_of(x, out, axis, chunks), out, scratch, unit)


def ring_scatter(at, x, out, axis, chunks, scratch, unit=1.0):
    return RingScatter(at, chunks, blocks_of(x, out, axis, chunks), out, scratch, unit)


def product_scatter(at, left, right, out, chunks, scratch, unit, cost):
    return ProductScatter(at, chunks, left, right, out, scratch, unit, cost)


def by_lanes(left, n_dp):
    return left if left.shape[1] // n_dp % 128 == 0 else left.T


def like(x, rows, cols, dtype=None):
    return jax.ShapeDtypeStruct((x.shape[0] * rows, x.shape[1] * cols), dtype or x.dtype)


class Parts:
    def __init__(self, refs):
        self.refs = list(refs)

    def take(self, shapes):
        taken, self.refs = self.refs[: len(shapes)], self.refs[len(shapes) :]
        return taken


def gather_lines(n_dp, n, query, project, shared):
    low = jnp.bfloat16
    sems = LineGather.sems(n, 1)
    shapes = [
        jax.ShapeDtypeStruct(query.shape, low),
        jax.ShapeDtypeStruct(project.shape[::-1], low),
        jax.ShapeDtypeStruct(shared.shape, low),
    ]

    def kernel(a, b, c, a_out, b_out, c_out, a_low, b_low, c_low, *refs):
        parts = Parts(refs)
        at = Place(n_dp, n)
        met = at.greet(line=True)
        a_low[...] = a[...].astype(low)
        b_low[...] = b[...].T.astype(low)
        c_low[...] = c[...].astype(low)
        run_jobs(
            met,
            [
                line_gather(at, a_low, a_out, 1, 1, parts.take(sems), 6.0),
                line_gather(at, c_low, c_out, 0, 1, parts.take(sems), 6.5),
                line_gather(at, b_low, b_out, 1, 1, parts.take(sems), 12.0),
            ],
        )

    return move(
        kernel,
        (query, project, shared),
        3,
        (like(shapes[0], 1, n), like(shapes[1], 1, n), like(shapes[2], n, 1)),
        0,
        [pltpu.VMEM(x.shape, low) for x in shapes] + sems * 3,
        1,
        "gather_lines",
    )


def rows_and_weights(n_dp, n, owned, query, shared):
    chips, chunks = n_dp // 2, 2
    total, cols = owned.shape[0], owned.shape[1] // 2
    rows, half = total // n, total // 2
    switch, line = LineSwitch.sems(n), LineGather.sems(n, chunks)
    ring = RingGather.sems(chips, chunks)

    def kernel(x, a, b, x_out, y_out, a_out, b_out, *refs):
        parts = Parts(refs)
        at = Place(n_dp, n)
        run_jobs(
            at.greet(line_all=True, ring=True),
            [
                LineSwitch(
                    at,
                    lambda p: x.at[pl.ds(pl.multiple_of(p * rows, rows), rows), pl.ds(0, cols)],
                    x_out.at[:, lanes(at.t, cols)],
                    parts.take(switch),
                ),
                ring_gather(at, b, b_out, 0, chunks, parts.take(ring), 4.0),
                ring_gather(at, a, a_out, 0, chunks, parts.take(ring), 22.0),
                line_gather(
                    at,
                    x.at[pl.ds(0, half), pl.ds(cols, cols)],
                    y_out.at[pl.ds(0, half)],
                    1,
                    chunks,
                    parts.take(line),
                    16.0,
                ),
            ],
        )

    return move(
        kernel,
        (owned, query, shared),
        3,
        (
            jax.ShapeDtypeStruct((rows, n * cols), owned.dtype),
            jax.ShapeDtypeStruct((total, n * cols), owned.dtype),
            like(query, n_dp, 1),
            like(shared, n_dp, 1),
        ),
        0,
        switch + ring * 2 + line,
        2,
        "rows_and_weights",
    )


def shared_and_project(n_dp, n, owned, shared_rows, project, rows, bias, query, gathered):
    chips, chunks = n_dp // 2, 2
    total, cols = owned.shape[0], owned.shape[1] // 2
    half = total // 2
    small, line = LineGather.sems(n, 1), LineGather.sems(n, chunks)
    ring = RingGather.sems(chips, chunks)

    made = RowProduct.scratch(query)

    def kernel(y, x, a, r, b, w, _, q_out, x_out, a_out, y_out, *refs):
        parts = Parts(refs)
        at = Place(n_dp, n)
        lower = pl.ds(half, half)
        run_jobs(
            at.greet(line=True, ring=True),
            [
                RowProduct(r, w, False, b, q_out, parts.take(made), 8.0, 3.0),
                line_gather(at, x, x_out, 0, 1, parts.take(small), 4.0),
                ring_gather(at, a, a_out, 0, chunks, parts.take(ring), 22.0),
                line_gather(
                    at,
                    y.at[lower, pl.ds(cols, cols)],
                    y_out.at[lower],
                    1,
                    chunks,
                    parts.take(line),
                    13.0,
                ),
            ],
        )

    return move(
        kernel,
        (owned, shared_rows, project, rows, bias, query, gathered),
        5,
        (
            jax.ShapeDtypeStruct((rows.shape[0], query.shape[1]), rows.dtype),
            like(shared_rows, n, 1),
            like(project, n_dp, 1),
            like(gathered, 1, 1),
        ),
        1,
        made + small + ring + line,
        3,
        "shared_and_project",
        {6: 3},
    )


def rows_and_expanded(n_dp, n, x, expand, shrink, bias):
    low = jnp.bfloat16
    shapes = [
        jax.ShapeDtypeStruct(expand.shape, low),
        jax.ShapeDtypeStruct(shrink.shape[::-1], low),
    ]
    chips, chunks, halves = n_dp // 2, 4, 2
    line, ring = LineGather.sems(n, chunks), RingGather.sems(chips, halves)

    full = like(shapes[0], n_dp, 1)
    made = GatheredProduct.scratch(n, x, full)

    def kernel(x_ref, a, b, c, u, x_out, a_out, b_out, a_low, b_low, *refs):
        parts = Parts(refs)
        at = Place(n_dp, n)
        met = at.greet(line=True, ring=True)
        a_low[...] = a[...].astype(low)
        b_low[...] = b[...].T.astype(low)
        line_job = line_gather(at, x_ref, x_out, 0, chunks, parts.take(line), 22.0)
        run_jobs(
            met,
            [
                line_job,
                Ended(
                    ring_gather(at, a_low, a_out, 0, halves, parts.take(ring), 22.0), 35.0
                ),
                Begun(
                    ring_gather(at, b_low, b_out, 0, halves, parts.take(ring), 30.0), 22.5
                ),
                GatheredProduct(
                    line_job, x_ref, x_out, a_out, c, u, parts.take(made), 39.5, 6.0
                ),
            ],
        )

    return move(
        kernel,
        (x, expand, shrink, bias),
        4,
        (
            jax.ShapeDtypeStruct((n * x.shape[0], full.shape[1]), jnp.float32),
            like(x, n, 1),
            full,
            like(shapes[1], n_dp, 1),
        ),
        1,
        [pltpu.VMEM(x.shape, low) for x in shapes] + line + ring * 2 + made,
        4,
        "rows_and_expanded",
    )


def scatter_expanded(n_dp, n, x, expand, shrink):
    chips, chunks = n_dp // 2, 4
    block = (x.shape[0] // n, x.shape[1])
    w_block = (expand.shape[0] // n_dp, expand.shape[1])
    line = LineScatter.scratch(n, chunks, block, x.dtype)
    ring = RingScatter.scratch(chips, chunks, w_block, x.dtype)

    def kernel(x_ref, a, b, x_out, a_out, b_out, *refs):
        parts = Parts(refs)
        at = Place(n_dp, n)
        run_jobs(
            at.greet(line=True, ring=True),
            [
                line_scatter(at, x_ref, x_out, 0, chunks, parts.take(line), 26.0),
                ring_scatter(at, a, a_out, 0, chunks, parts.take(ring), 22.0),
                ring_scatter(at, b, b_out, 0, chunks, parts.take(ring), 22.0),
            ],
        )

    return move(
        kernel,
        (x, expand, shrink),
        1,
        [jax.ShapeDtypeStruct(shape, jnp.float32) for shape in (block, w_block, w_block)],
        3,
        line + ring * 2,
        5,
        "scatter_expanded",
    )


def scatter_shared(n_dp, n, x, result, a, dq, dz, o, query):
    chips, chunks = n_dp // 2, 4
    block = (x.shape[0] // n, x.shape[1])
    w_block = (a.shape[1] // n_dp, dq.shape[1])
    small = LineExchange.scratch(n, block, x.dtype)
    line = LineGather.sems(n, chunks)
    ring = ProductScatter.scratch(chips, chunks, w_block, x.dtype)

    made = RowProduct.scratch(query)

    def kernel(
        x_ref, y, a_ref, dq_ref, dz_ref, o_ref, w, x_out, w_out, r_out, y_out, *refs
    ):
        parts = Parts(refs)
        at = Place(n_dp, n)
        a_out, b_out = Pieces(w_out, 0), Pieces(w_out, w_block[0])
        run_jobs(
            at.greet(line_all=True, ring=True),
            [
                line_exchange(at, x_ref, x_out, 0, parts.take(small)),
                RowProduct(dq_ref, w, True, None, r_out, parts.take(made), 30.0, 4.0),
                line_gather(at, y, y_out, 1, chunks, parts.take(line), 22.0),
                product_scatter(at, dz_ref, o_ref, b_out, chunks, parts.take(ring), 24.0, 1.0),
                product_scatter(at, a_ref, dq_ref, a_out, chunks, parts.take(ring), 24.0, 1.0),
            ],
        )

    return move(
        kernel,
        (x, result, by_lanes(a, n_dp), dq, by_lanes(dz, n_dp), o, query),
        6,
        (
            jax.ShapeDtypeStruct(block, jnp.float32),
            jax.ShapeDtypeStruct((n, 2 * w_block[0], w_block[1] // n), x.dtype),
            jax.ShapeDtypeStruct(dq.shape, jnp.float32),
            like(result, 1, n),
        ),
        3,
        small + made + line + ring * 2,
        6,
        "scatter_shared",
    )


def cols_and_shared(n_dp, n, rows, shared):
    chips = n_dp // 2
    count, width = rows.shape
    cols = width // n
    s_block = (shared.shape[0] // n_dp, shared.shape[1])
    p_block = (s_block[0] // n, s_block[1])
    switch = LineSwitch.sems(n)
    small = LineExchange.scratch(n, p_block, shared.dtype)
    ring = RingScatter.scratch(chips, 1, s_block, shared.dtype)

    def kernel(x, c, c_out, x_out, c_sum, *refs):
        parts = Parts(refs)
        at = Place(n_dp, n)
        run_jobs(
            at.greet(line_all=True, ring=True),
            [
                LineSwitch(
                    at,
                    lambda p: x.at[:, lanes(p, cols)],
                    x_out.at[pl.ds(at.t * count, count)],
                    parts.take(switch),
                ),
                ring_scatter(at, c, c_sum, 0, 1, parts.take(ring), 4.0),
                Later(line_exchange(at, c_sum, c_out, 0, parts.take(small)), 15.0),
            ],
        )

    return move(
        kernel,
        (rows, shared),
        1,
        [
            jax.ShapeDtypeStruct(p_block, jnp.float32),
            jax.ShapeDtypeStruct((n * count, cols), rows.dtype),
        ],
        1,
        [pltpu.VMEM(s_block, shared.dtype)] + switch + ring + small,
        7,
        "cols_and_shared",
    )


def fill_bias(bias, seg_row, seg_col, pos_row, pos_col):
    @pl.when(pl.program_id(0) == 0)
    def _():
        allowed = (seg_row[...] == seg_col[...]) & (pos_row[...] >= pos_col[...])
        bias[...] = jnp.where(allowed, 0.0, masked_score)


def attend_kernel(scale, q, k, v, seg_row, seg_col, pos_row, pos_col, o, log_total, bias):
    fill_bias(bias, seg_row, seg_col, pos_row, pos_col)
    scores = product(q[...], k[...], 1, 1) * scale + bias[...]
    row_max = jnp.max(scores, axis=1, keepdims=True)
    expo = jnp.exp(scores - row_max)
    row_total = jnp.sum(expo, axis=1, keepdims=True)
    probs = (expo / row_total).astype(jnp.bfloat16)
    o[...] = product(probs, v[...], 1, 0).astype(jnp.bfloat16)
    log_total[...] = jnp.broadcast_to(row_max + jnp.log(row_total), log_total.shape)


def attend_back_kernel(
    scale, q, do, log_total, k, v, seg_row, seg_col, pos_row, pos_col, dq, dkv, bias, dk, dv
):
    fill_bias(bias, seg_row, seg_col, pos_row, pos_col)

    @pl.when(pl.program_id(0) == 0)
    def _():
        dk[...] = jnp.zeros_like(dk)
        dv[...] = jnp.zeros_like(dv)

    scores = product(q[...], k[...], 1, 1) * scale + bias[...]
    probs = jnp.exp(scores - log_total[:, :1])
    prob_grad = product(do[...], v[...], 1, 1)
    inner = jnp.sum(probs * prob_grad, axis=1, keepdims=True)
    score_grad = (probs * (prob_grad - inner)).astype(jnp.bfloat16)
    dq[...] = (product(score_grad, k[...], 1, 0) * scale).astype(jnp.bfloat16)
    dk[...] += product(score_grad, q[...], 0, 0) * scale
    dv[...] += product(probs.astype(jnp.bfloat16), do[...], 0, 0)

    @pl.when(pl.program_id(0) == pl.num_programs(0) - 1)
    def _():
        dkv[...] = jnp.zeros_like(dkv)
        rows, (keys, size) = q.shape[0], k.shape
        last = (lax.axis_index("tensor") + 1) * rows
        window = pl.ds(pl.multiple_of(jnp.maximum(last - keys, 0), rows), keys)
        dkv[window, pl.ds(0, size)] = dk[...].astype(dkv.dtype)
        dkv[window, pl.ds(size, size)] = dv[...].astype(dkv.dtype)


def attention_specs(rows, keys, size):
    head = pl.BlockSpec((rows, size), lambda h: (0, h))
    whole = lambda *shape: pl.BlockSpec(shape, lambda h: (0, 0))
    masks = [whole(rows, 1), whole(1, keys), whole(rows, 1), whole(1, keys)]
    return head, whole(keys, size), masks


def attend(q, k, v, masks):
    rows, width = q.shape
    keys, size = k.shape
    head, shared, mask_specs = attention_specs(rows, keys, size)
    return pl.pallas_call(
        functools.partial(attend_kernel, size**-0.5),
        grid=(width // size,),
        in_specs=[head, shared, shared, *mask_specs],
        out_specs=(head, head),
        out_shape=(
            jax.ShapeDtypeStruct(q.shape, jnp.bfloat16),
            jax.ShapeDtypeStruct(q.shape, jnp.float32),
        ),
        scratch_shapes=[pltpu.VMEM((rows, keys), jnp.float32)],
        compiler_params=pltpu.CompilerParams(vmem_limit_bytes=32 * MIB),
        name="attend",
    )(q, k, v, *masks)


def attend_back(q, do, log_total, k, v, masks, total):
    rows, width = q.shape
    keys, size = k.shape
    head, shared, mask_specs = attention_specs(rows, keys, size)
    return pl.pallas_call(
        functools.partial(attend_back_kernel, size**-0.5),
        grid=(width // size,),
        in_specs=[head, head, head, shared, shared, *mask_specs],
        out_specs=(head, pl.BlockSpec((total, 2 * size), lambda h: (0, 0))),
        out_shape=(
            jax.ShapeDtypeStruct(q.shape, jnp.bfloat16),
            jax.ShapeDtypeStruct((total, 2 * size), jnp.bfloat16),
        ),
        scratch_shapes=[
            pltpu.VMEM((rows, keys), jnp.float32),
            pltpu.VMEM((keys, size), jnp.float32),
            pltpu.VMEM((keys, size), jnp.float32),
        ],
        compiler_params=pltpu.CompilerParams(vmem_limit_bytes=32 * MIB),
        name="attend_back",
    )(q, do, log_total, k, v, *masks)


def sum_all_kernel(n_dp, n, x_ref, o_ref, from_z, from_dp, part, s1, r1, s2, r2, s3, r3):
    g, t = lax.axis_index("dp"), lax.axis_index("tensor")
    rows = x_ref.shape[0] // n
    barrier = pltpu.get_barrier_semaphore()
    for k in range(1, n):
        pl.semaphore_signal(
            barrier, inc=1, device_id=(g, lax.rem(t + k, n)), device_id_type=MESH
        )
    for k in range(1, n_dp):
        pl.semaphore_signal(
            barrier, inc=1, device_id=(lax.rem(g + k, n_dp), t), device_id_type=MESH
        )
    pl.semaphore_wait(barrier, n - 1 + n_dp - 1)

    def piece(p):
        return pl.ds(pl.multiple_of(p * rows, rows), rows)

    first = []
    for k in range(1, n):
        p = lax.rem(t + k, n)
        first.append(
            pltpu.make_async_remote_copy(
                x_ref.at[piece(p)],
                from_z.at[k - 1],
                s1.at[k - 1],
                r1.at[k - 1],
                device_id=(g, p),
                device_id_type=MESH,
            )
        )
    for copy in first:
        copy.start()
    for copy in first:
        copy.wait()
    total = x_ref[piece(t)]
    for k in range(1, n):
        total = total + from_z[k - 1]
    part[...] = total
    second = []
    for k in range(1, n_dp):
        second.append(
            pltpu.make_async_remote_copy(
                part,
                from_dp.at[g],
                s2.at[k - 1],
                r2.at[k - 1],
                device_id=(lax.rem(g + k, n_dp), t),
                device_id_type=MESH,
            )
        )
    for copy in second:
        copy.start()
    from_dp[g] = part[...]
    for copy in second:
        copy.wait()
    total = from_dp[0]
    for k in range(1, n_dp):
        total = total + from_dp[k]
    o_ref[piece(t)] = total
    third = []
    for k in range(1, n):
        third.append(
            pltpu.make_async_remote_copy(
                o_ref.at[piece(t)],
                o_ref.at[piece(t)],
                s3.at[k - 1],
                r3.at[k - 1],
                device_id=(g, lax.rem(t + k, n)),
                device_id_type=MESH,
            )
        )
    for copy in third:
        copy.start()
    for copy in third:
        copy.wait()


def sum_all(x, n_dp, n, collective_id):
    rows = x.shape[0] // n
    return pl.pallas_call(
        functools.partial(sum_all_kernel, n_dp, n),
        out_shape=jax.ShapeDtypeStruct(x.shape, x.dtype),
        in_specs=[IN_VMEM],
        out_specs=IN_VMEM,
        scratch_shapes=[
            pltpu.VMEM((n - 1, rows, 128), x.dtype),
            pltpu.VMEM((n_dp, rows, 128), x.dtype),
            pltpu.VMEM((rows, 128), x.dtype),
        ]
        + [DMA((n - 1,))] * 2
        + [DMA((n_dp - 1,))] * 2
        + [DMA((n - 1,))] * 2,
        compiler_params=pltpu.CompilerParams(collective_id=collective_id, has_side_effects=True),
        name="sum_all",
    )(x)


def local(
    tokens,
    cotangent,
    lengths,
    counts,
    query_weight,
    query_moment,
    query_square,
    shared_weight,
    shared_moment,
    shared_square,
    project_weight,
    project_moment,
    project_square,
    expand_weight,
    expand_moment,
    expand_square,
    shrink_weight,
    shrink_moment,
    shrink_square,
    vectors_value,
    vectors_moment,
    vectors_square,
):
    device = lax.axis_index("dp")
    n_dp = lax.axis_size("dp")
    t = lax.axis_index("tensor")
    n = lax.axis_size("tensor")
    row_count, width = tokens.shape
    slots = 2 * row_count // n_dp
    part_rows, part_cols = row_count // n, width // n
    send_start = lax.dynamic_index_in_dim(exclusive_sum(counts, 1), device, 0, keepdims=False)
    send_amount = lax.dynamic_index_in_dim(counts, device, 0, keepdims=False)
    recv_start = lax.dynamic_index_in_dim(exclusive_sum(counts, 0), device, 1, keepdims=False)
    recv_amount = lax.dynamic_index_in_dim(counts, device, 1, keepdims=False)
    send_slots = slot_matrix(send_start, send_amount, slots, row_count)
    recv_slots = slot_matrix(recv_start, recv_amount, slots, row_count)

    def low(x):
        return x.astype(jnp.bfloat16)

    def pack(rows, out_slots):
        return low(mul_plain(out_slots, rows)).reshape(n_dp, slots, rows.shape[1])

    def exchange(packed):
        return lax.all_to_all(packed, "dp", split_axis=0, concat_axis=0, tiled=True)

    def unpack(arrived, in_slots):
        return low(mul_left_t(in_slots, arrived.reshape(n_dp * slots, arrived.shape[2])))

    mine_cols = [
        lax.dynamic_slice_in_dim(a, t * part_cols, part_cols, 1) for a in (tokens, cotangent)
    ]
    packed, query_here, project_here, shared_here = lax.optimization_barrier(
        (
            pack(jnp.concatenate(mine_cols, axis=1), send_slots),
            query_weight,
            project_weight,
            shared_weight,
        )
    )
    query_line, project_line, shared_line = gather_lines(
        n_dp, n, query_here, project_here, shared_here
    )
    arrived, query_line, shared_line = lax.optimization_barrier(
        (exchange(packed), query_line, shared_line)
    )
    owned = unpack(arrived, recv_slots)
    owned_rows, owned_grad, query_all, shared_all = rows_and_weights(
        n_dp, n, owned, query_line, shared_line
    )

    head_size = shared_all.shape[1] // 2
    hidden_width = expand_weight.shape[1]
    hidden_total = hidden_width * n
    gain_one = vectors_value[0:width]
    shift_one = vectors_value[width : 2 * width]
    gain_two = vectors_value[2 * width : 3 * width]
    shift_two = vectors_value[3 * width : 4 * width]
    query_bias = vectors_value[4 * width : 5 * width]
    project_bias = vectors_value[5 * width : 6 * width]
    shrink_bias = vectors_value[6 * width : 7 * width]
    expand_bias = lax.dynamic_slice_in_dim(
        vectors_value, 7 * width + t * hidden_width, hidden_width, 0
    )
    value_bias = vectors_value[7 * width + hidden_total : 7 * width + hidden_total + head_size]

    inputs_float = owned_rows.astype(jnp.float32)
    normed_one, norm_one_back = jax.vjp(layer_norm, inputs_float, gain_one, shift_one)
    normed_low = normed_one.astype(jnp.bfloat16)
    shared_out = mul_plain(normed_low, shared_all) + jnp.concatenate(
        [jnp.zeros((head_size,), jnp.float32), value_bias]
    )
    queries, shared_rows, project_all_t, owned_grad = shared_and_project(
        n_dp,
        n,
        owned,
        low(shared_out),
        project_line,
        normed_low,
        query_bias[None],
        query_all,
        owned_grad,
    )
    window = min(row_count, part_rows + longest)
    window_start = jnp.maximum((t + 1) * part_rows - window, 0)
    shared_window = lax.dynamic_slice_in_dim(shared_rows, window_start, window, 0)
    key_rows, value_rows = shared_window[:, :head_size], shared_window[:, head_size:]
    segment, position = segment_ids(lengths[0], row_count)
    masks = (
        lax.dynamic_slice_in_dim(segment, t * part_rows, part_rows, 0)[:, None],
        lax.dynamic_slice_in_dim(segment, window_start, window, 0)[None, :],
        lax.dynamic_slice_in_dim(position, t * part_rows, part_rows, 0)[:, None],
        lax.dynamic_slice_in_dim(position, window_start, window, 0)[None, :],
    )
    heads_out, log_total = attend(queries, key_rows, value_rows, masks)
    hidden_one = inputs_float + (mul_right_t(heads_out, project_all_t) + project_bias)
    normed_two, norm_two_back = jax.vjp(layer_norm, hidden_one, gain_two, shift_two)

    expand_pre, normed_two_low, expand_cols, shrink_rows_t = rows_and_expanded(
        n_dp, n, low(normed_two), expand_weight, shrink_weight, expand_bias[None]
    )
    activated, gelu_back = jax.vjp(gelu_tanh, expand_pre)
    activated_low = activated.astype(jnp.bfloat16)
    result_part = low(mul_right_t(activated_low, shrink_rows_t))
    own_result = lax.dynamic_slice_in_dim(result_part, t * part_rows, part_rows, 0)
    result_part = lax.dynamic_update_slice_in_dim(
        result_part, low(own_result + (hidden_one + shrink_bias)), t * part_rows, 0
    )
    result_part, owned_grad = lax.optimization_barrier((result_part, owned_grad))
    layer_cols = lax.psum_scatter(result_part, "tensor", scatter_dimension=1, tiled=True)
    shrink_grad_t = low(mul_left_t(owned_grad, activated_low))
    activated_grad = mul_plain(owned_grad, shrink_rows_t)
    expand_pre_grad = gelu_back(activated_grad)[0].astype(jnp.bfloat16)
    expand_grad = low(mul_left_t(normed_two_low, expand_pre_grad))
    expand_bias_grad = jnp.sum(expand_pre_grad.astype(jnp.float32), axis=0)
    normed_two_part = mul_right_t(expand_pre_grad, expand_cols).astype(jnp.bfloat16)

    normed_two_grad, expand_part, shrink_part_t = scatter_expanded(
        n_dp, n, normed_two_part, expand_grad, shrink_grad_t
    )
    shrink_part = turned(shrink_part_t)
    output_cols = unpack(exchange(pack(layer_cols, recv_slots)), send_slots)
    output_float = lax.dynamic_slice_in_dim(owned_grad, t * part_rows, part_rows, 0).astype(
        jnp.float32
    )
    shrink_bias_grad = jnp.sum(output_float, axis=0)
    hidden_from_norm, gain_two_grad, shift_two_grad = norm_two_back(normed_two_grad)
    hidden_grad = output_float + hidden_from_norm
    branch_grad = hidden_grad.astype(jnp.bfloat16)
    project_bias_grad = jnp.sum(branch_grad.astype(jnp.float32), axis=0)
    heads_grad = low(mul_plain(branch_grad, project_all_t))
    query_grad, shared_part = attend_back(
        queries, heads_grad, log_total, key_rows, value_rows, masks, row_count
    )
    shared_grad, weight_sums, normed_one_grad, output_rows = scatter_shared(
        n_dp,
        n,
        shared_part,
        output_cols,
        normed_low,
        query_grad,
        branch_grad,
        heads_out,
        query_all,
    )
    shared_grad = low(shared_grad)
    query_bias_grad = jnp.sum(query_grad.astype(jnp.float32), axis=0)
    normed_one_grad = normed_one_grad + mul_right_t(shared_grad, shared_all)
    inputs_from_norm, gain_one_grad, shift_one_grad = norm_one_back(normed_one_grad)
    input_result = (hidden_grad + inputs_from_norm).astype(jnp.bfloat16)
    shared_weight_grad = mul_left_t(normed_low, shared_grad)
    value_bias_grad = jnp.sum(shared_grad[:, head_size:].astype(jnp.float32), axis=0)

    shared_piece, input_cols = cols_and_shared(n_dp, n, input_result, low(shared_weight_grad))
    input_cols, weight_sums = lax.optimization_barrier((input_cols, weight_sums))
    grads = lax.psum_scatter(
        weight_sums.reshape(-1, part_cols), "tensor", scatter_dimension=0, tiled=True
    )
    back = unpack(exchange(pack(input_cols, recv_slots)), send_slots)
    back, grads = lax.optimization_barrier((back, grads))
    grad_rows = lax.all_gather(back, "tensor", axis=1, tiled=True)
    tall = grads.shape[0] // 2
    query_part = grads[:tall].astype(jnp.float32)
    project_part = turned(grads[tall:].astype(jnp.float32))
    output_back = output_rows.astype(jnp.float32)
    token_rms = jnp.sqrt(jnp.mean(output_back * output_back, axis=1))

    split_part = lax.dynamic_update_slice_in_dim(
        jnp.zeros((hidden_total,), jnp.float32), expand_bias_grad, t * hidden_width, 0
    )
    vector_part = jnp.concatenate(
        [
            gain_one_grad,
            shift_one_grad,
            gain_two_grad,
            shift_two_grad,
            query_bias_grad,
            project_bias_grad,
            shrink_bias_grad,
            split_part,
            value_bias_grad,
        ]
    )
    local_squares = (
        jnp.sum(query_part * query_part)
        + jnp.sum(expand_part * expand_part)
        + jnp.sum(shared_piece * shared_piece)
        + jnp.sum(project_part * project_part)
        + jnp.sum(shrink_part * shrink_part)
    )
    length = vector_part.shape[0]
    unit = n * 8 * 128
    padded = -(-(length + 1) // unit) * unit
    everything = jnp.concatenate(
        [vector_part, local_squares[None], jnp.zeros((padded - length - 1,), jnp.float32)]
    )
    summed = sum_all(everything.reshape(padded // 128, 128), n_dp, n, 8).reshape(padded)
    vector_grad, weight_squares = summed[:length], summed[length]
    grad_size = jnp.sqrt(weight_squares + jnp.sum(vector_grad * vector_grad))
    clip_factor = jnp.minimum(1.0, clip_level / (grad_size + 1e-06))
    clipped_vectors = clip_factor * vector_grad
    query_new = adamw_step(
        query_weight,
        query_moment,
        query_square,
        clip_factor * query_part,
        rate_matrix * width ** (-0.5),
    )
    shared_new = adamw_step(
        shared_weight,
        shared_moment,
        shared_square,
        clip_factor * shared_piece,
        rate_attention * width ** (-0.5),
    )
    project_new = adamw_step(
        project_weight,
        project_moment,
        project_square,
        clip_factor * project_part,
        rate_attention * width ** (-0.5),
    )
    expand_new = adamw_step(
        expand_weight,
        expand_moment,
        expand_square,
        clip_factor * expand_part,
        rate_matrix * width ** (-0.5),
    )
    shrink_new = adamw_step(
        shrink_weight,
        shrink_moment,
        shrink_square,
        clip_factor * shrink_part,
        rate_matrix * hidden_total ** (-0.5),
    )
    vectors_new = adamw_step(
        vectors_value, vectors_moment, vectors_square, clipped_vectors, rate_vector
    )
    return (
        output_rows,
        grad_rows,
        grad_size,
        *query_new,
        *shared_new,
        *project_new,
        *expand_new,
        *shrink_new,
        *vectors_new,
        clipped_vectors,
        token_rms,
    )


def solution(mesh):
    by_rows = P("dp", None)
    query = P("dp", "tensor")
    shared = P(("dp", "tensor"), None)
    project = P("tensor", "dp")
    return jax.shard_map(
        local,
        mesh=mesh,
        in_specs=(
            *(by_rows,) * 3,
            P(),
            *(query,) * 3,
            *(shared,) * 3,
            *(project,) * 3,
            *(query,) * 3,
            *(project,) * 3,
            *(P(),) * 3,
        ),
        out_specs=(
            *(by_rows,) * 2,
            P(),
            *(query,) * 3,
            *(shared,) * 3,
            *(project,) * 3,
            *(query,) * 3,
            *(project,) * 3,
            *(P(),) * 4,
            P("dp"),
        ),
        check_vma=False,
    )
```

```python
import functools

import jax
import jax.numpy as jnp
from jax import lax
from jax.experimental.layout import Layout, with_layout_constraint
from jax.experimental import pallas as pl
from jax.experimental.pallas import tpu as pltpu
from jax.sharding import PartitionSpec as P

STEP = 10


beta_one = 0.9
beta_two = 0.95
adam_epsilon = 1e-08
decay_rate = 0.1
clip_level = 1.0
norm_epsilon = 1e-05
rate_matrix = 0.6
rate_attention = 2.4
rate_vector = 0.3
masked_score = -1e30
longest = 512

MESH = pl.DeviceIdType.MESH
IN_PLACE = pl.BlockSpec(memory_space=pl.ANY)
IN_VMEM = pl.BlockSpec(memory_space=pltpu.VMEM)
DMA = pltpu.SemaphoreType.DMA
MIB = 2**20


def mul_plain(left, right):
    return jnp.dot(left, right, preferred_element_type=jnp.float32)


def mul_right_t(left, right):
    return lax.dot_general(
        left, right, (((1,), (1,)), ((), ())), preferred_element_type=jnp.float32
    )


def mul_left_t(left, right):
    return lax.dot_general(
        left, right, (((0,), (0,)), ((), ())), preferred_element_type=jnp.float32
    )


def product(left, right, left_dim, right_dim):
    return lax.dot_general(
        left, right, (((left_dim,), (right_dim,)), ((), ())), preferred_element_type=jnp.float32
    )


def layer_norm(values, scaling, offset):
    average = jnp.mean(values, axis=-1, keepdims=True)
    centered = values - average
    variance = jnp.mean(centered * centered, axis=-1, keepdims=True)
    return centered * lax.rsqrt(variance + norm_epsilon) * scaling + offset


def gelu_tanh(values):
    return jax.nn.gelu(values, approximate=True)


def exclusive_sum(table, axis_index):
    return jnp.cumsum(table, axis=axis_index) - table


def segment_ids(seq_lengths, row_count):
    position = jnp.arange(row_count, dtype=jnp.int32)
    starts = jnp.cumsum(seq_lengths) - seq_lengths
    segment = jnp.sum((starts[None, :] <= position[:, None]).astype(jnp.int32), axis=1)
    return (segment, position)


def slot_matrix(starts, amounts, slots, row_count):
    offsets = jnp.arange(slots, dtype=jnp.int32)
    picked = jnp.where(offsets[None, :] < amounts[:, None], starts[:, None] + offsets[None, :], -1)
    position = jnp.arange(row_count, dtype=jnp.int32)
    return (picked.reshape(-1)[:, None] == position[None, :]).astype(jnp.bfloat16)


def turned(x):
    return with_layout_constraint(x.T, Layout(major_to_minor=(0, 1)))


def adamw_step(weight, moment, square, gradient, rate):
    moment_new = beta_one * moment + (1.0 - beta_one) * gradient
    square_new = beta_two * square + (1.0 - beta_two) * gradient * gradient
    moment_hat = moment_new / (1.0 - beta_one**STEP)
    square_hat = square_new / (1.0 - beta_two**STEP)
    weight_new = weight - rate * (
        moment_hat / (jnp.sqrt(square_hat) + adam_epsilon) + decay_rate * weight
    )
    return (weight_new, moment_new, square_new)


def remote(src, dst, send_sem, recv_sem, device):
    return pltpu.make_async_remote_copy(
        src, dst, send_sem, recv_sem, device_id=device, device_id_type=MESH
    )


class Place:
    def __init__(self, n_dp, n):
        self.n, self.chips = n, n_dp // 2
        self.dp, self.t = lax.axis_index("dp"), lax.axis_index("tensor")
        self.core, chip = lax.rem(self.dp, 2), lax.div(self.dp, 2)
        side = round(self.chips**0.5)
        self.side = side if side * side == self.chips else self.chips
        self.pos = self.snake(chip)
        self.sibling = (self.dp + 1 - 2 * self.core, self.t)
        self.after = (self.block(self.ring(self.pos + 1), self.core), self.t)
        self.before = (self.block(self.ring(self.pos - 1), self.core), self.t)
        self.left, self.right = (self.dp, self.t - 1), (self.dp, self.t + 1)

    def snake(self, index):
        row, col = lax.div(index, self.side), lax.rem(index, self.side)
        odd = lax.rem(row, 2)
        return row * self.side + col + odd * (self.side - 1 - 2 * col)

    def ring(self, pos):
        return lax.rem(pos + 2 * self.chips, self.chips)

    def block(self, pos, core):
        return self.snake(pos) * 2 + core

    def greet(self, line=False, line_all=False, ring=False):
        barrier = pltpu.get_barrier_semaphore()
        peers = 0

        def call(device):
            pl.semaphore_signal(barrier, inc=1, device_id=device, device_id_type=MESH)

        if ring:
            for device in (self.sibling, self.after, self.before):
                call(device)
            peers += 3
        if line_all:
            for k in range(1, self.n):
                call((self.dp, lax.rem(self.t + k, self.n)))
            peers += self.n - 1
        elif line:
            pl.when(self.t > 0)(lambda: call(self.left))
            pl.when(self.t < self.n - 1)(lambda: call(self.right))
            peers += (self.t > 0).astype(jnp.int32) + (self.t < self.n - 1).astype(jnp.int32)
        return lambda: pl.semaphore_wait(barrier, peers)


class LineGather:
    @staticmethod
    def sems(n, chunks):
        return [DMA((n - 1, chunks))] * 4 + [DMA]

    def __init__(self, at, chunks, first, place, sems, whole, unit=1.0):
        self.unit = unit
        self.at, self.chunks, self.first, self.place, self.sems = at, chunks, first, place, sems
        self.own = pltpu.make_async_copy(whole[0], whole[1], sems[4])

    def copy(self, h, c, right):
        at = self.at
        dst = self.place(at.t - h if right else at.t + h, c)
        src = self.first(c) if h == 0 else dst
        s, r = self.sems[0:2] if right else self.sems[2:4]
        return remote(src, dst, s.at[h, c], r.at[h, c], at.right if right else at.left)

    def receive(self, h, c, right):
        at = self.at
        dst = self.place(at.t - 1 - h if right else at.t + 1 + h, c)
        s, r = self.sems[0:2] if right else self.sems[2:4]
        remote(dst, dst, s.at[h, c], r.at[h, c], at.left if right else at.right).wait_recv()

    def sends(self, h, right):
        t, n = self.at.t, self.at.n
        return (t >= h) & (t < n - 1) if right else (t + h <= n - 1) & (t > 0)

    def gets(self, h, right):
        return self.at.t - 1 - h >= 0 if right else self.at.t + 1 + h <= self.at.n - 1

    def every(self):
        for h in range(self.at.n - 1):
            for c in range(self.chunks):
                for right in (True, False):
                    yield h, c, right

    def prepare(self):
        self.own.start()

    def prepared(self):
        self.own.wait()

    def start(self):
        for h, c, right in self.every():
            if h == 0:
                pl.when(self.sends(h, right))(lambda: self.copy(h, c, right).start())

    def step(self, h, c, right):
        pl.when(self.gets(h, right))(lambda: self.receive(h, c, right))
        if h + 1 < self.at.n - 1:
            pl.when(self.sends(h + 1, right))(lambda: self.copy(h + 1, c, right).start())

    def steps(self):
        return [
            (self.unit * (which[0] + (which[1] + 1) / self.chunks), functools.partial(self.step, *which))
            for which in self.every()
        ]

    def finish(self):
        for h, c, right in self.every():
            pl.when(self.sends(h, right))(lambda: self.copy(h, c, right).wait_send())


class LineScatter:
    @staticmethod
    def scratch(n, chunks, block, dtype):
        return [pltpu.VMEM((n - 1, *block), dtype)] * 2 + [DMA((n - 1, chunks))] * 4

    def __init__(self, at, chunks, own, out, scratch, unit=1.0):
        self.unit = unit
        self.at, self.chunks, self.own, self.out = at, chunks, own, out
        self.held, self.sems = scratch[:2], scratch[2:6]
        self.rows = self.held[0].shape[1] // chunks

    def parts(self, k, c, right):
        side = 0 if right else 1
        s, r = self.sems[2 * side : 2 * side + 2]
        return self.held[side].at[k, pl.ds(c * self.rows, self.rows)], s.at[k, c], r.at[k, c]

    def send(self, k, c, right, first):
        slot, s, r = self.parts(k, c, right)
        src = self.own(self.target(k, right), c) if first else slot
        return remote(src, slot, s, r, self.at.right if right else self.at.left)

    def receive(self, k, c, right):
        slot, s, r = self.parts(k, c, right)
        remote(slot, slot, s, r, self.at.left if right else self.at.right).wait_recv()

    def target(self, k, right):
        return self.at.n - 1 - k if right else k

    def every(self):
        for k in range(self.at.n - 1):
            for c in range(self.chunks):
                for right in (True, False):
                    yield k, c, right

    def prepare(self):
        pass

    def prepared(self):
        pass

    def start(self):
        t, n = self.at.t, self.at.n
        for k, c, right in self.every():
            first = (t == (0 if right else n - 1)) & (t != self.target(k, right))
            pl.when(first)(lambda: self.send(k, c, right, True).start())

    def add(self, k, c, right):
        self.receive(k, c, right)
        slot = self.parts(k, c, right)[0]
        mine = self.own(self.target(k, right), c)[...]
        slot[...] = (slot[...].astype(jnp.float32) + mine.astype(jnp.float32)).astype(slot.dtype)
        self.send(k, c, right, False).start()

    def step(self, k, c, right):
        t, n, d = self.at.t, self.at.n, self.target(k, right)
        passes = (t > 0) & (t < d) if right else (t < n - 1) & (t > d)
        pl.when(passes)(lambda: self.add(k, c, right))

    def steps(self):
        return [
            (self.unit * (which[0] + (which[1] + 1) / self.chunks), functools.partial(self.step, *which))
            for which in self.every()
        ]

    def finish(self):
        t, n = self.at.t, self.at.n
        for k, c, right in self.every():
            pl.when(t == self.target(k, right))(lambda: self.receive(k, c, right))
        for c in range(self.chunks):
            span = pl.ds(c * self.rows, self.rows)
            self.out[span] = self.own(t, c)[...].astype(self.out.dtype)

        def more(block):
            self.out[...] += block[...].astype(self.out.dtype)

        pl.when(t > 0)(lambda: more(self.held[0].at[n - 1 - t]))
        pl.when(t < n - 1)(lambda: more(self.held[1].at[t]))
        for k, c, right in self.every():
            d = self.target(k, right)
            pl.when(t < d if right else t > d)(lambda: self.send(k, c, right, False).wait_send())


class LineExchange:
    @staticmethod
    def scratch(n, block, dtype):
        return [pltpu.VMEM((n - 1, *block), dtype)] + [DMA((n - 1,))] * 2

    def __init__(self, at, source, out, scratch):
        self.at, self.source, self.out = at, source, out
        self.held = scratch[0]
        self.copies = []
        for k in range(1, at.n):
            p = lax.rem(at.t + k, at.n)
            self.copies.append(
                remote(
                    source(p),
                    self.held.at[k - 1],
                    scratch[1].at[k - 1],
                    scratch[2].at[k - 1],
                    (at.dp, p),
                )
            )

    def prepare(self):
        pass

    def prepared(self):
        pass

    def start(self):
        for copy in self.copies:
            copy.start()

    def steps(self):
        return []

    def finish(self):
        for copy in self.copies:
            copy.wait()
        total = self.source(self.at.t)[...].astype(jnp.float32)
        for k in range(self.at.n - 1):
            total = total + self.held[k].astype(jnp.float32)
        self.out[...] = total.astype(self.out.dtype)


class RingGather:
    @staticmethod
    def sems(chips, chunks):
        hops = chips // 2
        return [DMA((2, hops, chunks))] * 4 + [DMA((chunks,))] * 2 + [DMA]

    def __init__(self, at, chunks, first, place, sems, whole, unit=1.0):
        self.unit = unit
        self.at, self.chunks, self.first, self.place, self.sems = at, chunks, first, place, sems
        self.hops = at.chips // 2
        self.own = pltpu.make_async_copy(whole[0], whole[1], sems[6])

    def every(self):
        for h in range(self.hops):
            for c in range(self.chunks):
                for way in (0, 1):
                    if h < self.hops - 1 or c % 2 == way:
                        yield h, c, way

    def origin(self, steps, way, core):
        return self.at.block(self.at.ring(self.at.pos + (steps if way else -steps)), core)

    def onward(self, h, c, way):
        dst = self.place(self.origin(h, way, self.at.core), c)
        src = self.first(c) if h == 0 else dst
        s, r = self.sems[0:2]
        device = self.at.before if way else self.at.after
        return remote(src, dst, s.at[way, h, c], r.at[way, h, c], device)

    def arrival(self, h, c, way):
        dst = self.place(self.origin(h + 1, way, self.at.core), c)
        s, r = self.sems[0:2]
        device = self.at.after if way else self.at.before
        return remote(dst, dst, s.at[way, h, c], r.at[way, h, c], device)

    def across(self, h, c, way, core):
        dst = self.place(self.origin(h + 1, way, core), c)
        s, r = self.sems[2:4]
        return remote(dst, dst, s.at[way, h, c], r.at[way, h, c], self.at.sibling)

    def across_own(self, c, core):
        dst = self.place(self.origin(0, 0, core), c)
        s, r = self.sems[4:6]
        return remote(self.first(c), dst, s.at[c], r.at[c], self.at.sibling)

    def prepare(self):
        self.own.start()

    def prepared(self):
        self.own.wait()

    def start(self):
        for h, c, way in self.every():
            if h == 0:
                self.onward(h, c, way).start()
        for c in range(self.chunks):
            self.across_own(c, self.at.core).start()

    def step(self, h, c, way):
        self.arrival(h, c, way).wait_recv()
        if (h + 1, c, way) in list(self.every()):
            self.onward(h + 1, c, way).start()
        self.across(h, c, way, self.at.core).start()

    def steps(self):
        when = 0.0
        for h, c, way in self.every():
            when += self.unit / self.chunks / 2
            yield when, functools.partial(self.step, h, c, way)

    def finish(self):
        other = 1 - self.at.core
        for c in range(self.chunks):
            self.across_own(c, other).wait_recv()
            self.across_own(c, self.at.core).wait_send()
        for h, c, way in self.every():
            self.across(h, c, way, other).wait_recv()
            self.across(h, c, way, self.at.core).wait_send()
            self.onward(h, c, way).wait_send()


class RingScatter:
    @staticmethod
    def scratch(chips, chunks, block, dtype):
        hops = chips // 2
        return (
            [pltpu.VMEM((chips, *block), dtype)] * 2
            + [pltpu.VMEM((2, hops, *block), dtype)]
            + [DMA((chips, chunks))] * 3
            + [DMA((2, hops, chunks))] * 2
        )

    def __init__(self, at, chunks, source, out, scratch, unit=1.0):
        self.unit = unit
        self.at, self.chunks, self.source, self.out = at, chunks, source, out
        self.hops = at.chips // 2
        self.mine, self.other, self.held = scratch[:3]
        self.load_sem, self.s1, self.r1, self.s2, self.r2 = scratch[3:8]
        self.rows = self.held.shape[2] // chunks

    def span(self, c):
        return pl.ds(c * self.rows, self.rows)

    def target(self, place, core):
        return self.at.block(self.at.ring(self.at.pos + place), core)

    def load(self, place, c):
        src = self.source(self.target(place, self.at.core), c)
        dst = self.mine.at[place, self.span(c)]
        return pltpu.make_async_copy(src, dst, self.load_sem.at[place, c])

    def across(self, place, c):
        src = self.source(self.target(place, 1 - self.at.core), c)
        dst = self.other.at[place, self.span(c)]
        return remote(src, dst, self.s1.at[place, c], self.r1.at[place, c], self.at.sibling)

    def sent(self, e, c, way):
        return e < self.hops or c % 2 == way

    def onward(self, e, c, way):
        place = self.at.chips - e if way else e
        src, dst = self.mine.at[place, self.span(c)], self.held.at[way, e - 1, self.span(c)]
        device = self.at.before if way else self.at.after
        return remote(src, dst, self.s2.at[way, e - 1, c], self.r2.at[way, e - 1, c], device)

    def arrival(self, e, c, way):
        dst = self.held.at[way, e, self.span(c)]
        device = self.at.after if way else self.at.before
        return remote(dst, dst, self.s2.at[way, e, c], self.r2.at[way, e, c], device)

    def places(self):
        order = []
        for e in range(self.hops, 0, -1):
            order += [e] if e == self.hops else [e, self.at.chips - e]
        return order + [0]

    def prepare(self):
        for place in self.places():
            for c in range(self.chunks):
                self.load(place, c).start()

    def prepared(self):
        pass

    def start(self):
        self.send_across(self.places()[:1])

    def send_across(self, places):
        for place in places:
            for c in range(self.chunks):
                self.across(place, c).start()

    def loaded(self, place, c):
        self.load(place, c).wait()

    def base(self, place, c):
        self.loaded(place, c)
        self.across(place, c).wait_recv()
        total = self.mine[place, self.span(c)].astype(jnp.float32)
        return total + self.other[place, self.span(c)].astype(jnp.float32)

    def arrived(self, e, c, way):
        self.arrival(e, c, way).wait_recv()
        return self.held[way, e, self.span(c)].astype(jnp.float32)

    def step(self, e, c, way):
        place = self.at.chips - e if way else e
        total = self.base(place, c)
        if e < self.hops and self.sent(e + 1, c, way):
            total += self.arrived(e, c, way)
        self.mine[place, self.span(c)] = total.astype(self.mine.dtype)
        self.onward(e, c, way).start()

    def last(self, c):
        total = self.base(0, c)
        for way in (0, 1):
            if self.sent(1, c, way):
                total += self.arrived(0, c, way)
        self.out[self.span(c)] = total.astype(self.out.dtype)

    def every(self):
        for e in range(self.hops, 0, -1):
            for c in range(self.chunks):
                for way in (0, 1):
                    if self.sent(e, c, way):
                        yield e, c, way

    def steps(self):
        yield 0.0, functools.partial(self.send_across, self.places()[1:])
        yield from self.sum_steps()

    def sum_steps(self):
        when = 0.0
        for e, c, way in self.every():
            yield when, functools.partial(self.step, e, c, way)
            when += self.unit / self.chunks / 2
        for c in range(self.chunks):
            yield when + self.unit * (c + 1) / self.chunks, functools.partial(self.last, c)

    def finish(self):
        for place in self.places():
            for c in range(self.chunks):
                self.across(place, c).wait_send()
        for e, c, way in self.every():
            self.onward(e, c, way).wait_send()


class ProductScatter(RingScatter):
    @staticmethod
    def scratch(chips, chunks, block, dtype):
        return RingScatter.scratch(chips, chunks, block, dtype) + [pltpu.VMEM((2, *block), dtype)]

    def __init__(self, at, chunks, left, right, out, scratch, unit, cost):
        super().__init__(at, chunks, None, out, scratch[:-1], unit)
        self.left, self.right, self.stage, self.cost = left, right, scratch[-1], cost

    def across(self, place, c):
        src = self.stage.at[self.places().index(place) % 2, self.span(c)]
        dst = self.other.at[place, self.span(c)]
        return remote(src, dst, self.s1.at[place, c], self.r1.at[place, c], self.at.sibling)

    def product(self, place, core):
        block = self.held.shape[2]
        cols = lanes(self.target(place, core), block) if block % 128 == 0 else None
        if cols is None:
            left = self.left[pl.ds(pl.multiple_of(self.target(place, core) * block, block), block)]
            total = product(left, self.right[...], 1, 0)
        else:
            total = product(self.left[:, cols], self.right[...], 0, 0)
        return total.astype(self.mine.dtype)

    def work(self, i, place, here):
        if here:
            self.mine[place] = self.product(place, self.at.core)
            return
        if i >= 2:
            for c in range(self.chunks):
                self.across(self.places()[i - 2], c).wait_send()
        self.stage[i % 2] = self.product(place, 1 - self.at.core)
        for c in range(self.chunks):
            self.across(place, c).start()

    def prepare(self):
        pass

    def start(self):
        pass

    def loaded(self, place, c):
        pass

    def steps(self):
        when = 0.0
        for i, place in enumerate(self.places()):
            for here in (False, True):
                yield when, functools.partial(self.work, i, place, here)
                when += self.cost
        for when, step in self.sum_steps():
            place = 0
            if len(step.args) == 3:
                e, _, way = step.args
                place = self.at.chips - e if way else e
            yield max(when, (2 * self.places().index(place) + 2) * self.cost), step

    def finish(self):
        for place in self.places()[-2:]:
            for c in range(self.chunks):
                self.across(place, c).wait_send()
        for e, c, way in self.every():
            self.onward(e, c, way).wait_send()


class LineSwitch:
    @staticmethod
    def sems(n):
        return [DMA((n - 1,))] * 2 + [DMA]

    def __init__(self, at, source, target, sems):
        self.own = pltpu.make_async_copy(source(at.t), target, sems[2])
        self.copies = []
        for k in range(1, at.n):
            p = lax.rem(at.t + k, at.n)
            self.copies.append(
                remote(source(p), target, sems[0].at[k - 1], sems[1].at[k - 1], (at.dp, p))
            )

    def prepare(self):
        self.own.start()

    def prepared(self):
        self.own.wait()

    def start(self):
        for copy in self.copies:
            copy.start()

    def steps(self):
        return []

    def finish(self):
        for copy in self.copies:
            copy.wait()


class Pieces:
    def __init__(self, ref, begin):
        self.ref, self.begin, self.dtype = ref, begin, ref.dtype

    def __setitem__(self, span, value):
        pieces, _, cols = self.ref.shape
        for k in range(pieces):
            rows = pl.ds(self.begin + span.start, span.size)
            self.ref[k, rows] = value[:, k * cols : (k + 1) * cols]


class Later:
    def __init__(self, job, when):
        self.job, self.when = job, when

    def prepare(self):
        pass

    def prepared(self):
        pass

    def start(self):
        pass

    def steps(self):
        yield self.when, self.job.start

    def finish(self):
        self.job.finish()


class Begun:
    def __init__(self, job, when):
        self.job, self.when = job, when
        self.prepare, self.prepared, self.finish = job.prepare, job.prepared, job.finish

    def start(self):
        pass

    def steps(self):
        yield self.when, self.job.start
        for when, step in self.job.steps():
            yield self.when + when, step


class Ended:
    def __init__(self, job, when):
        self.job, self.when = job, when
        self.prepare, self.prepared, self.start = job.prepare, job.prepared, job.start

    def steps(self):
        yield from self.job.steps()
        yield self.when, self.job.finish

    def finish(self):
        pass


class GatheredProduct:
    @staticmethod
    def scratch(n, block, weight):
        held = pltpu.VMEM((n - 1, 2, *block.shape), block.dtype)
        return [pltpu.VMEM(weight.shape, weight.dtype), DMA, held, DMA((n - 1, 2))]

    def __init__(self, line, own, gathered, weight, bias, out, scratch, begin, cost):
        self.line, self.own, self.gathered, self.bias, self.out = line, own, gathered, bias, out
        self.weight, self.held, self.sems = scratch[0], scratch[2], scratch[3]
        self.copy = pltpu.make_async_copy(weight, scratch[0], scratch[1])
        self.begin, self.cost, self.tile = begin, cost, 512

    def prepare(self):
        pass

    def prepared(self):
        pass

    def start(self):
        pass

    def place(self, h, right):
        rows, t = self.own.shape[0], self.line.at.t
        return pl.ds(pl.multiple_of((t - 1 - h if right else t + 1 + h) * rows, rows), rows)

    def load(self, h, right):
        side = 0 if right else 1
        return pltpu.make_async_copy(
            self.gathered.at[self.place(h, right)], self.held.at[h, side], self.sems.at[h, side]
        )

    def multiply(self, block, rows):
        for j in range(self.out.shape[1] // self.tile):
            span = pl.ds(j * self.tile, self.tile)
            total = product(block[...], self.weight[:, span], 1, 0) + self.bias[:, span]
            self.out[rows, span] = total

    def arrived(self, h, right):
        pl.when(self.line.gets(h, right))(lambda: self.load(h, right).start())

    def work(self, h, right):
        @pl.when(self.line.gets(h, right))
        def _():
            self.load(h, right).wait()
            self.multiply(self.held.at[h, 0 if right else 1], self.place(h, right))

    def mine(self):
        rows = self.own.shape[0]
        self.multiply(self.own, pl.ds(pl.multiple_of(self.line.at.t * rows, rows), rows))

    def steps(self):
        yield self.begin - 4.0, self.copy.start
        yield self.begin, self.copy.wait
        yield self.begin, self.mine
        when = self.begin + self.cost
        for h in range(self.line.at.n - 1):
            come = self.line.unit * (h + 1) + 0.5
            for right in (True, False):
                yield come, functools.partial(self.arrived, h, right)
            when = max(when, come + 1.0)
            for right in (True, False):
                yield when, functools.partial(self.work, h, right)
                when += self.cost

    def finish(self):
        pass


class RowProduct:
    @staticmethod
    def scratch(weight):
        return [pltpu.VMEM(weight.shape, weight.dtype), DMA]

    def __init__(self, left, weight, turn, bias, out, scratch, begin, cost):
        self.left, self.turn, self.bias, self.out = left, turn, bias, out
        self.held, self.begin, self.cost = scratch[0], begin, cost
        self.copy = pltpu.make_async_copy(weight, scratch[0], scratch[1])
        self.tile = 256

    def prepare(self):
        self.copy.start()

    def prepared(self):
        pass

    def start(self):
        pass

    def work(self, j):
        span = pl.ds(j * self.tile, self.tile)
        if self.turn:
            total = product(self.left[...], self.held[span], 1, 1)
        else:
            total = product(self.left[...], self.held[:, span], 1, 0)
        if self.bias is not None:
            total += self.bias[:, span]
        self.out[:, span] = total.astype(self.out.dtype)

    def steps(self):
        yield self.begin, self.copy.wait
        for j in range(self.out.shape[1] // self.tile):
            yield self.begin + j * self.cost, functools.partial(self.work, j)

    def finish(self):
        pass


def run_jobs(met, jobs):
    for job in jobs:
        job.prepare()
    for job in jobs:
        job.prepared()
    met()
    for job in jobs:
        job.start()
    ordered = []
    for i, job in enumerate(jobs):
        ordered += [(when, i, j, step) for j, (when, step) in enumerate(job.steps())]
    for _, _, _, step in sorted(ordered, key=lambda entry: entry[:3]):
        step()
    for job in jobs:
        job.finish()


def rows_of(ref, step):
    return lambda c: ref.at[pl.ds(c * step, step)]


def lanes(index, count):
    return pl.ds(pl.multiple_of(index * count, count), count)


def move(kernel, inputs, in_vmem, outs, out_vmem, scratch, collective_id, name, aliases=None):
    return pl.pallas_call(
        kernel,
        out_shape=tuple(outs),
        in_specs=[IN_VMEM if i < in_vmem else IN_PLACE for i in range(len(inputs))],
        out_specs=tuple(IN_VMEM if i < out_vmem else IN_PLACE for i in range(len(outs))),
        scratch_shapes=scratch,
        compiler_params=pltpu.CompilerParams(
            collective_id=collective_id, has_side_effects=True, vmem_limit_bytes=56 * MIB
        ),
        input_output_aliases=aliases or {},
        name=name,
    )(*inputs)


def line_gather(at, x, out, axis, chunks, sems, unit=1.0):
    rows, cols = x.shape
    step = rows // chunks
    if axis == 0:
        place = lambda b, c: out.at[pl.ds(b * rows + c * step, step)]
        whole = out.at[pl.ds(at.t * rows, rows)]
    else:
        place = lambda b, c: out.at[pl.ds(c * step, step), lanes(b, cols)]
        whole = out.at[:, lanes(at.t, cols)]
    return LineGather(at, chunks, rows_of(x, step), place, sems, (x, whole), unit)


def ring_gather(at, x, out, axis, chunks, sems, unit=1.0):
    rows, cols = x.shape
    step = rows // chunks
    if axis == 0:
        place = lambda b, c: out.at[pl.ds(b * rows + c * step, step)]
        whole = out.at[pl.ds(at.dp * rows, rows)]
    else:
        place = lambda b, c: out.at[pl.ds(c * step, step), lanes(b, cols)]
        whole = out.at[:, lanes(at.dp, cols)]
    return RingGather(at, chunks, rows_of(x, step), place, sems, (x, whole), unit)


def blocks_of(x, out, axis, chunks):
    rows, cols = out.shape
    step = rows // chunks
    if axis == 0:
        return lambda b, c: x.at[pl.ds(pl.multiple_of(b * rows + c * step, step), step)]
    return lambda b, c: x.at[pl.ds(c * step, step), lanes(b, cols)]


def line_exchange(at, x, out, axis, scratch):
    block = blocks_of(x, out, axis, 1)
    return LineExchange(at, lambda p: block(p, 0), out, scratch)


def line_scatter(at, x, out, axis, chunks, scratch, unit=1.0):
    return LineScatter(at, chunks, blocks_of(x, out, axis, chunks), out, scratch, unit)


def ring_scatter(at, x, out, axis, chunks, scratch, unit=1.0):
    return RingScatter(at, chunks, blocks_of(x, out, axis, chunks), out, scratch, unit)


def product_scatter(at, left, right, out, chunks, scratch, unit, cost):
    return ProductScatter(at, chunks, left, right, out, scratch, unit, cost)


def by_lanes(left, n_dp):
    return left if left.shape[1] // n_dp % 128 == 0 else left.T


def like(x, rows, cols, dtype=None):
    return jax.ShapeDtypeStruct((x.shape[0] * rows, x.shape[1] * cols), dtype or x.dtype)


class Parts:
    def __init__(self, refs):
        self.refs = list(refs)

    def take(self, shapes):
        taken, self.refs = self.refs[: len(shapes)], self.refs[len(shapes) :]
        return taken


def gather_lines(n_dp, n, query, project, shared):
    low = jnp.bfloat16
    sems = LineGather.sems(n, 1)
    shapes = [
        jax.ShapeDtypeStruct(query.shape, low),
        jax.ShapeDtypeStruct(project.shape[::-1], low),
        jax.ShapeDtypeStruct(shared.shape, low),
    ]

    def kernel(a, b, c, a_out, b_out, c_out, a_low, b_low, c_low, *refs):
        parts = Parts(refs)
        at = Place(n_dp, n)
        met = at.greet(line=True)
        a_low[...] = a[...].astype(low)
        b_low[...] = b[...].T.astype(low)
        c_low[...] = c[...].astype(low)
        run_jobs(
            met,
            [
                line_gather(at, a_low, a_out, 1, 1, parts.take(sems), 6.0),
                line_gather(at, c_low, c_out, 0, 1, parts.take(sems), 6.5),
                line_gather(at, b_low, b_out, 1, 1, parts.take(sems), 12.0),
            ],
        )

    return move(
        kernel,
        (query, project, shared),
        3,
        (like(shapes[0], 1, n), like(shapes[1], 1, n), like(shapes[2], n, 1)),
        0,
        [pltpu.VMEM(x.shape, low) for x in shapes] + sems * 3,
        1,
        "gather_lines",
    )


def rows_and_weights(n_dp, n, owned, query, shared):
    chips, chunks = n_dp // 2, 2
    total, cols = owned.shape[0], owned.shape[1] // 2
    rows, half = total // n, total // 2
    switch, line = LineSwitch.sems(n), LineGather.sems(n, chunks)
    ring = RingGather.sems(chips, chunks)

    def kernel(x, a, b, x_out, y_out, a_out, b_out, *refs):
        parts = Parts(refs)
        at = Place(n_dp, n)
        run_jobs(
            at.greet(line_all=True, ring=True),
            [
                LineSwitch(
                    at,
                    lambda p: x.at[pl.ds(pl.multiple_of(p * rows, rows), rows), pl.ds(0, cols)],
                    x_out.at[:, lanes(at.t, cols)],
                    parts.take(switch),
                ),
                ring_gather(at, b, b_out, 0, chunks, parts.take(ring), 4.0),
                ring_gather(at, a, a_out, 0, chunks, parts.take(ring), 22.0),
                line_gather(
                    at,
                    x.at[pl.ds(0, half), pl.ds(cols, cols)],
                    y_out.at[pl.ds(0, half)],
                    1,
                    chunks,
                    parts.take(line),
                    16.0,
                ),
            ],
        )

    return move(
        kernel,
        (owned, query, shared),
        3,
        (
            jax.ShapeDtypeStruct((rows, n * cols), owned.dtype),
            jax.ShapeDtypeStruct((total, n * cols), owned.dtype),
            like(query, n_dp, 1),
            like(shared, n_dp, 1),
        ),
        0,
        switch + ring * 2 + line,
        2,
        "rows_and_weights",
    )


def shared_and_project(n_dp, n, owned, shared_rows, project, rows, bias, query, gathered):
    chips, chunks = n_dp // 2, 2
    total, cols = owned.shape[0], owned.shape[1] // 2
    half = total // 2
    small, line = LineGather.sems(n, 1), LineGather.sems(n, chunks)
    ring = RingGather.sems(chips, chunks)

    made = RowProduct.scratch(query)

    def kernel(y, x, a, r, b, w, _, q_out, x_out, a_out, y_out, *refs):
        parts = Parts(refs)
        at = Place(n_dp, n)
        lower = pl.ds(half, half)
        run_jobs(
            at.greet(line=True, ring=True),
            [
                RowProduct(r, w, False, b, q_out, parts.take(made), 8.0, 3.0),
                line_gather(at, x, x_out, 0, 1, parts.take(small), 4.0),
                ring_gather(at, a, a_out, 0, chunks, parts.take(ring), 22.0),
                line_gather(
                    at,
                    y.at[lower, pl.ds(cols, cols)],
                    y_out.at[lower],
                    1,
                    chunks,
                    parts.take(line),
                    13.0,
                ),
            ],
        )

    return move(
        kernel,
        (owned, shared_rows, project, rows, bias, query, gathered),
        5,
        (
            jax.ShapeDtypeStruct((rows.shape[0], query.shape[1]), rows.dtype),
            like(shared_rows, n, 1),
            like(project, n_dp, 1),
            like(gathered, 1, 1),
        ),
        1,
        made + small + ring + line,
        3,
        "shared_and_project",
        {6: 3},
    )


def rows_and_expanded(n_dp, n, x, expand, shrink, bias):
    low = jnp.bfloat16
    shapes = [
        jax.ShapeDtypeStruct(expand.shape, low),
        jax.ShapeDtypeStruct(shrink.shape[::-1], low),
    ]
    chips, chunks, halves = n_dp // 2, 4, 2
    line, ring = LineGather.sems(n, chunks), RingGather.sems(chips, halves)

    full = like(shapes[0], n_dp, 1)
    made = GatheredProduct.scratch(n, x, full)

    def kernel(x_ref, a, b, c, u, x_out, a_out, b_out, a_low, b_low, *refs):
        parts = Parts(refs)
        at = Place(n_dp, n)
        met = at.greet(line=True, ring=True)
        a_low[...] = a[...].astype(low)
        b_low[...] = b[...].T.astype(low)
        line_job = line_gather(at, x_ref, x_out, 0, chunks, parts.take(line), 22.0)
        run_jobs(
            met,
            [
                line_job,
                Ended(
                    ring_gather(at, a_low, a_out, 0, halves, parts.take(ring), 22.0), 35.0
                ),
                Begun(
                    ring_gather(at, b_low, b_out, 0, halves, parts.take(ring), 30.0), 22.5
                ),
                GatheredProduct(
                    line_job, x_ref, x_out, a_out, c, u, parts.take(made), 39.5, 6.0
                ),
            ],
        )

    return move(
        kernel,
        (x, expand, shrink, bias),
        4,
        (
            jax.ShapeDtypeStruct((n * x.shape[0], full.shape[1]), jnp.float32),
            like(x, n, 1),
            full,
            like(shapes[1], n_dp, 1),
        ),
        1,
        [pltpu.VMEM(x.shape, low) for x in shapes] + line + ring * 2 + made,
        4,
        "rows_and_expanded",
    )


def scatter_expanded(n_dp, n, x, expand, shrink):
    chips, chunks = n_dp // 2, 4
    block = (x.shape[0] // n, x.shape[1])
    w_block = (expand.shape[0] // n_dp, expand.shape[1])
    line = LineScatter.scratch(n, chunks, block, x.dtype)
    ring = RingScatter.scratch(chips, chunks, w_block, x.dtype)

    def kernel(x_ref, a, b, x_out, a_out, b_out, *refs):
        parts = Parts(refs)
        at = Place(n_dp, n)
        run_jobs(
            at.greet(line=True, ring=True),
            [
                line_scatter(at, x_ref, x_out, 0, chunks, parts.take(line), 26.0),
                ring_scatter(at, a, a_out, 0, chunks, parts.take(ring), 22.0),
                ring_scatter(at, b, b_out, 0, chunks, parts.take(ring), 22.0),
            ],
        )

    return move(
        kernel,
        (x, expand, shrink),
        1,
        [jax.ShapeDtypeStruct(shape, jnp.float32) for shape in (block, w_block, w_block)],
        3,
        line + ring * 2,
        5,
        "scatter_expanded",
    )


def scatter_shared(n_dp, n, x, result, a, dq, dz, o, query):
    chips, chunks = n_dp // 2, 4
    block = (x.shape[0] // n, x.shape[1])
    w_block = (a.shape[1] // n_dp, dq.shape[1])
    small = LineExchange.scratch(n, block, x.dtype)
    line = LineGather.sems(n, chunks)
    ring = ProductScatter.scratch(chips, chunks, w_block, x.dtype)

    made = RowProduct.scratch(query)

    def kernel(
        x_ref, y, a_ref, dq_ref, dz_ref, o_ref, w, x_out, w_out, r_out, y_out, *refs
    ):
        parts = Parts(refs)
        at = Place(n_dp, n)
        a_out, b_out = Pieces(w_out, 0), Pieces(w_out, w_block[0])
        run_jobs(
            at.greet(line_all=True, ring=True),
            [
                line_exchange(at, x_ref, x_out, 0, parts.take(small)),
                RowProduct(dq_ref, w, True, None, r_out, parts.take(made), 30.0, 4.0),
                line_gather(at, y, y_out, 1, chunks, parts.take(line), 22.0),
                product_scatter(at, dz_ref, o_ref, b_out, chunks, parts.take(ring), 24.0, 1.0),
                product_scatter(at, a_ref, dq_ref, a_out, chunks, parts.take(ring), 24.0, 1.0),
            ],
        )

    return move(
        kernel,
        (x, result, by_lanes(a, n_dp), dq, by_lanes(dz, n_dp), o, query),
        6,
        (
            jax.ShapeDtypeStruct(block, jnp.float32),
            jax.ShapeDtypeStruct((n, 2 * w_block[0], w_block[1] // n), x.dtype),
            jax.ShapeDtypeStruct(dq.shape, jnp.float32),
            like(result, 1, n),
        ),
        3,
        small + made + line + ring * 2,
        6,
        "scatter_shared",
    )


def cols_and_shared(n_dp, n, rows, shared):
    chips = n_dp // 2
    count, width = rows.shape
    cols = width // n
    s_block = (shared.shape[0] // n_dp, shared.shape[1])
    p_block = (s_block[0] // n, s_block[1])
    switch = LineSwitch.sems(n)
    small = LineExchange.scratch(n, p_block, shared.dtype)
    ring = RingScatter.scratch(chips, 1, s_block, shared.dtype)

    def kernel(x, c, c_out, x_out, c_sum, *refs):
        parts = Parts(refs)
        at = Place(n_dp, n)
        run_jobs(
            at.greet(line_all=True, ring=True),
            [
                LineSwitch(
                    at,
                    lambda p: x.at[:, lanes(p, cols)],
                    x_out.at[pl.ds(at.t * count, count)],
                    parts.take(switch),
                ),
                ring_scatter(at, c, c_sum, 0, 1, parts.take(ring), 4.0),
                Later(line_exchange(at, c_sum, c_out, 0, parts.take(small)), 15.0),
            ],
        )

    return move(
        kernel,
        (rows, shared),
        1,
        [
            jax.ShapeDtypeStruct(p_block, jnp.float32),
            jax.ShapeDtypeStruct((n * count, cols), rows.dtype),
        ],
        1,
        [pltpu.VMEM(s_block, shared.dtype)] + switch + ring + small,
        7,
        "cols_and_shared",
    )


def fill_bias(bias, seg_row, seg_col, pos_row, pos_col):
    @pl.when(pl.program_id(0) == 0)
    def _():
        allowed = (seg_row[...] == seg_col[...]) & (pos_row[...] >= pos_col[...])
        bias[...] = jnp.where(allowed, 0.0, masked_score)


def attend_kernel(scale, q, k, v, seg_row, seg_col, pos_row, pos_col, o, log_total, bias):
    fill_bias(bias, seg_row, seg_col, pos_row, pos_col)
    scores = product(q[...], k[...], 1, 1) * scale + bias[...]
    row_max = jnp.max(scores, axis=1, keepdims=True)
    expo = jnp.exp(scores - row_max)
    row_total = jnp.sum(expo, axis=1, keepdims=True)
    probs = (expo / row_total).astype(jnp.bfloat16)
    o[...] = product(probs, v[...], 1, 0).astype(jnp.bfloat16)
    log_total[...] = jnp.broadcast_to(row_max + jnp.log(row_total), log_total.shape)


def attend_back_kernel(
    scale, q, do, log_total, k, v, seg_row, seg_col, pos_row, pos_col, dq, dkv, bias, dk, dv
):
    fill_bias(bias, seg_row, seg_col, pos_row, pos_col)

    @pl.when(pl.program_id(0) == 0)
    def _():
        dk[...] = jnp.zeros_like(dk)
        dv[...] = jnp.zeros_like(dv)

    scores = product(q[...], k[...], 1, 1) * scale + bias[...]
    probs = jnp.exp(scores - log_total[:, :1])
    prob_grad = product(do[...], v[...], 1, 1)
    inner = jnp.sum(probs * prob_grad, axis=1, keepdims=True)
    score_grad = (probs * (prob_grad - inner)).astype(jnp.bfloat16)
    dq[...] = (product(score_grad, k[...], 1, 0) * scale).astype(jnp.bfloat16)
    dk[...] += product(score_grad, q[...], 0, 0) * scale
    dv[...] += product(probs.astype(jnp.bfloat16), do[...], 0, 0)

    @pl.when(pl.program_id(0) == pl.num_programs(0) - 1)
    def _():
        dkv[...] = jnp.zeros_like(dkv)
        rows, (keys, size) = q.shape[0], k.shape
        last = (lax.axis_index("tensor") + 1) * rows
        window = pl.ds(pl.multiple_of(jnp.maximum(last - keys, 0), rows), keys)
        dkv[window, pl.ds(0, size)] = dk[...].astype(dkv.dtype)
        dkv[window, pl.ds(size, size)] = dv[...].astype(dkv.dtype)


def attention_specs(rows, keys, size):
    head = pl.BlockSpec((rows, size), lambda h: (0, h))
    whole = lambda *shape: pl.BlockSpec(shape, lambda h: (0, 0))
    masks = [whole(rows, 1), whole(1, keys), whole(rows, 1), whole(1, keys)]
    return head, whole(keys, size), masks


def attend(q, k, v, masks):
    rows, width = q.shape
    keys, size = k.shape
    head, shared, mask_specs = attention_specs(rows, keys, size)
    return pl.pallas_call(
        functools.partial(attend_kernel, size**-0.5),
        grid=(width // size,),
        in_specs=[head, shared, shared, *mask_specs],
        out_specs=(head, head),
        out_shape=(
            jax.ShapeDtypeStruct(q.shape, jnp.bfloat16),
            jax.ShapeDtypeStruct(q.shape, jnp.float32),
        ),
        scratch_shapes=[pltpu.VMEM((rows, keys), jnp.float32)],
        compiler_params=pltpu.CompilerParams(vmem_limit_bytes=32 * MIB),
        name="attend",
    )(q, k, v, *masks)


def attend_back(q, do, log_total, k, v, masks, total):
    rows, width = q.shape
    keys, size = k.shape
    head, shared, mask_specs = attention_specs(rows, keys, size)
    return pl.pallas_call(
        functools.partial(attend_back_kernel, size**-0.5),
        grid=(width // size,),
        in_specs=[head, head, head, shared, shared, *mask_specs],
        out_specs=(head, pl.BlockSpec((total, 2 * size), lambda h: (0, 0))),
        out_shape=(
            jax.ShapeDtypeStruct(q.shape, jnp.bfloat16),
            jax.ShapeDtypeStruct((total, 2 * size), jnp.bfloat16),
        ),
        scratch_shapes=[
            pltpu.VMEM((rows, keys), jnp.float32),
            pltpu.VMEM((keys, size), jnp.float32),
            pltpu.VMEM((keys, size), jnp.float32),
        ],
        compiler_params=pltpu.CompilerParams(vmem_limit_bytes=32 * MIB),
        name="attend_back",
    )(q, do, log_total, k, v, *masks)


def sum_all_kernel(n_dp, n, x_ref, o_ref, from_z, from_dp, part, s1, r1, s2, r2, s3, r3):
    g, t = lax.axis_index("dp"), lax.axis_index("tensor")
    rows = x_ref.shape[0] // n
    barrier = pltpu.get_barrier_semaphore()
    for k in range(1, n):
        pl.semaphore_signal(
            barrier, inc=1, device_id=(g, lax.rem(t + k, n)), device_id_type=MESH
        )
    for k in range(1, n_dp):
        pl.semaphore_signal(
            barrier, inc=1, device_id=(lax.rem(g + k, n_dp), t), device_id_type=MESH
        )
    pl.semaphore_wait(barrier, n - 1 + n_dp - 1)

    def piece(p):
        return pl.ds(pl.multiple_of(p * rows, rows), rows)

    first = []
    for k in range(1, n):
        p = lax.rem(t + k, n)
        first.append(
            pltpu.make_async_remote_copy(
                x_ref.at[piece(p)],
                from_z.at[k - 1],
                s1.at[k - 1],
                r1.at[k - 1],
                device_id=(g, p),
                device_id_type=MESH,
            )
        )
    for copy in first:
        copy.start()
    for copy in first:
        copy.wait()
    total = x_ref[piece(t)]
    for k in range(1, n):
        total = total + from_z[k - 1]
    part[...] = total
    second = []
    for k in range(1, n_dp):
        second.append(
            pltpu.make_async_remote_copy(
                part,
                from_dp.at[g],
                s2.at[k - 1],
                r2.at[k - 1],
                device_id=(lax.rem(g + k, n_dp), t),
                device_id_type=MESH,
            )
        )
    for copy in second:
        copy.start()
    from_dp[g] = part[...]
    for copy in second:
        copy.wait()
    total = from_dp[0]
    for k in range(1, n_dp):
        total = total + from_dp[k]
    o_ref[piece(t)] = total
    third = []
    for k in range(1, n):
        third.append(
            pltpu.make_async_remote_copy(
                o_ref.at[piece(t)],
                o_ref.at[piece(t)],
                s3.at[k - 1],
                r3.at[k - 1],
                device_id=(g, lax.rem(t + k, n)),
                device_id_type=MESH,
            )
        )
    for copy in third:
        copy.start()
    for copy in third:
        copy.wait()


def sum_all(x, n_dp, n, collective_id):
    rows = x.shape[0] // n
    return pl.pallas_call(
        functools.partial(sum_all_kernel, n_dp, n),
        out_shape=jax.ShapeDtypeStruct(x.shape, x.dtype),
        in_specs=[IN_VMEM],
        out_specs=IN_VMEM,
        scratch_shapes=[
            pltpu.VMEM((n - 1, rows, 128), x.dtype),
            pltpu.VMEM((n_dp, rows, 128), x.dtype),
            pltpu.VMEM((rows, 128), x.dtype),
        ]
        + [DMA((n - 1,))] * 2
        + [DMA((n_dp - 1,))] * 2
        + [DMA((n - 1,))] * 2,
        compiler_params=pltpu.CompilerParams(collective_id=collective_id, has_side_effects=True),
        name="sum_all",
    )(x)


def local(
    tokens,
    cotangent,
    lengths,
    counts,
    query_weight,
    query_moment,
    query_square,
    shared_weight,
    shared_moment,
    shared_square,
    project_weight,
    project_moment,
    project_square,
    expand_weight,
    expand_moment,
    expand_square,
    shrink_weight,
    shrink_moment,
    shrink_square,
    vectors_value,
    vectors_moment,
    vectors_square,
):
    device = lax.axis_index("dp")
    n_dp = lax.axis_size("dp")
    t = lax.axis_index("tensor")
    n = lax.axis_size("tensor")
    row_count, width = tokens.shape
    slots = 2 * row_count // n_dp
    part_rows, part_cols = row_count // n, width // n
    send_start = lax.dynamic_index_in_dim(exclusive_sum(counts, 1), device, 0, keepdims=False)
    send_amount = lax.dynamic_index_in_dim(counts, device, 0, keepdims=False)
    recv_start = lax.dynamic_index_in_dim(exclusive_sum(counts, 0), device, 1, keepdims=False)
    recv_amount = lax.dynamic_index_in_dim(counts, device, 1, keepdims=False)
    send_slots = slot_matrix(send_start, send_amount, slots, row_count)
    recv_slots = slot_matrix(recv_start, recv_amount, slots, row_count)

    def low(x):
        return x.astype(jnp.bfloat16)

    def pack(rows, out_slots):
        return low(mul_plain(out_slots, rows)).reshape(n_dp, slots, rows.shape[1])

    def exchange(packed):
        return lax.all_to_all(packed, "dp", split_axis=0, concat_axis=0, tiled=True)

    def unpack(arrived, in_slots):
        return low(mul_left_t(in_slots, arrived.reshape(n_dp * slots, arrived.shape[2])))

    mine_cols = [
        lax.dynamic_slice_in_dim(a, t * part_cols, part_cols, 1) for a in (tokens, cotangent)
    ]
    packed, query_here, project_here, shared_here = lax.optimization_barrier(
        (
            pack(jnp.concatenate(mine_cols, axis=1), send_slots),
            query_weight,
            project_weight,
            shared_weight,
        )
    )
    query_line, project_line, shared_line = gather_lines(
        n_dp, n, query_here, project_here, shared_here
    )
    arrived, query_line, shared_line = lax.optimization_barrier(
        (exchange(packed), query_line, shared_line)
    )
    owned = unpack(arrived, recv_slots)
    owned_rows, owned_grad, query_all, shared_all = rows_and_weights(
        n_dp, n, owned, query_line, shared_line
    )

    head_size = shared_all.shape[1] // 2
    hidden_width = expand_weight.shape[1]
    hidden_total = hidden_width * n
    gain_one = vectors_value[0:width]
    shift_one = vectors_value[width : 2 * width]
    gain_two = vectors_value[2 * width : 3 * width]
    shift_two = vectors_value[3 * width : 4 * width]
    query_bias = vectors_value[4 * width : 5 * width]
    project_bias = vectors_value[5 * width : 6 * width]
    shrink_bias = vectors_value[6 * width : 7 * width]
    expand_bias = lax.dynamic_slice_in_dim(
        vectors_value, 7 * width + t * hidden_width, hidden_width, 0
    )
    value_bias = vectors_value[7 * width + hidden_total : 7 * width + hidden_total + head_size]

    inputs_float = owned_rows.astype(jnp.float32)
    normed_one, norm_one_back = jax.vjp(layer_norm, inputs_float, gain_one, shift_one)
    normed_low = normed_one.astype(jnp.bfloat16)
    shared_out = mul_plain(normed_low, shared_all) + jnp.concatenate(
        [jnp.zeros((head_size,), jnp.float32), value_bias]
    )
    queries, shared_rows, project_all_t, owned_grad = shared_and_project(
        n_dp,
        n,
        owned,
        low(shared_out),
        project_line,
        normed_low,
        query_bias[None],
        query_all,
        owned_grad,
    )
    window = min(row_count, part_rows + longest)
    window_start = jnp.maximum((t + 1) * part_rows - window, 0)
    shared_window = lax.dynamic_slice_in_dim(shared_rows, window_start, window, 0)
    key_rows, value_rows = shared_window[:, :head_size], shared_window[:, head_size:]
    segment, position = segment_ids(lengths[0], row_count)
    masks = (
        lax.dynamic_slice_in_dim(segment, t * part_rows, part_rows, 0)[:, None],
        lax.dynamic_slice_in_dim(segment, window_start, window, 0)[None, :],
        lax.dynamic_slice_in_dim(position, t * part_rows, part_rows, 0)[:, None],
        lax.dynamic_slice_in_dim(position, window_start, window, 0)[None, :],
    )
    heads_out, log_total = attend(queries, key_rows, value_rows, masks)
    hidden_one = inputs_float + (mul_right_t(heads_out, project_all_t) + project_bias)
    normed_two, norm_two_back = jax.vjp(layer_norm, hidden_one, gain_two, shift_two)

    expand_pre, normed_two_low, expand_cols, shrink_rows_t = rows_and_expanded(
        n_dp, n, low(normed_two), expand_weight, shrink_weight, expand_bias[None]
    )
    activated, gelu_back = jax.vjp(gelu_tanh, expand_pre)
    activated_low = activated.astype(jnp.bfloat16)
    pieces = []
    for k in range(n):
        span = slice(k * part_cols, (k + 1) * part_cols)
        piece = low(mul_right_t(activated_low, shrink_rows_t[span]))
        own_piece = lax.dynamic_slice_in_dim(piece, t * part_rows, part_rows, 0)
        own_piece = low(own_piece + (hidden_one[:, span] + shrink_bias[span]))
        pieces.append(lax.dynamic_update_slice_in_dim(piece, own_piece, t * part_rows, 0))
    result_part = jnp.concatenate(pieces)
    result_part, owned_grad = lax.optimization_barrier((result_part, owned_grad))
    layer_cols = lax.psum_scatter(result_part, "tensor", scatter_dimension=0, tiled=True)
    shrink_grad_t = low(mul_left_t(owned_grad, activated_low))
    activated_grad = mul_plain(owned_grad, shrink_rows_t)
    expand_pre_grad = gelu_back(activated_grad)[0].astype(jnp.bfloat16)
    expand_grad = low(mul_left_t(normed_two_low, expand_pre_grad))
    expand_bias_grad = jnp.sum(expand_pre_grad.astype(jnp.float32), axis=0)
    normed_two_part = mul_right_t(expand_pre_grad, expand_cols).astype(jnp.bfloat16)

    normed_two_grad, expand_part, shrink_part_t = scatter_expanded(
        n_dp, n, normed_two_part, expand_grad, shrink_grad_t
    )
    shrink_part = turned(shrink_part_t)
    output_cols = unpack(exchange(pack(layer_cols, recv_slots)), send_slots)
    output_float = lax.dynamic_slice_in_dim(owned_grad, t * part_rows, part_rows, 0).astype(
        jnp.float32
    )
    shrink_bias_grad = jnp.sum(output_float, axis=0)
    hidden_from_norm, gain_two_grad, shift_two_grad = norm_two_back(normed_two_grad)
    hidden_grad = output_float + hidden_from_norm
    branch_grad = hidden_grad.astype(jnp.bfloat16)
    project_bias_grad = jnp.sum(branch_grad.astype(jnp.float32), axis=0)
    heads_grad = low(mul_plain(branch_grad, project_all_t))
    query_grad, shared_part = attend_back(
        queries, heads_grad, log_total, key_rows, value_rows, masks, row_count
    )
    shared_grad, weight_sums, normed_one_grad, output_rows = scatter_shared(
        n_dp,
        n,
        shared_part,
        output_cols,
        normed_low,
        query_grad,
        branch_grad,
        heads_out,
        query_all,
    )
    shared_grad = low(shared_grad)
    query_bias_grad = jnp.sum(query_grad.astype(jnp.float32), axis=0)
    normed_one_grad = normed_one_grad + mul_right_t(shared_grad, shared_all)
    inputs_from_norm, gain_one_grad, shift_one_grad = norm_one_back(normed_one_grad)
    input_result = (hidden_grad + inputs_from_norm).astype(jnp.bfloat16)
    shared_weight_grad = mul_left_t(normed_low, shared_grad)
    value_bias_grad = jnp.sum(shared_grad[:, head_size:].astype(jnp.float32), axis=0)

    shared_piece, input_cols = cols_and_shared(n_dp, n, input_result, low(shared_weight_grad))
    input_cols, weight_sums = lax.optimization_barrier((input_cols, weight_sums))
    grads = lax.psum_scatter(
        weight_sums.reshape(-1, part_cols), "tensor", scatter_dimension=0, tiled=True
    )
    back = unpack(exchange(pack(input_cols, recv_slots)), send_slots)
    back, grads = lax.optimization_barrier((back, grads))
    grad_rows = lax.all_gather(back, "tensor", axis=1, tiled=True)
    tall = grads.shape[0] // 2
    query_part = grads[:tall].astype(jnp.float32)
    project_part = turned(grads[tall:].astype(jnp.float32))
    output_back = output_rows.astype(jnp.float32)
    token_rms = jnp.sqrt(jnp.mean(output_back * output_back, axis=1))

    split_part = lax.dynamic_update_slice_in_dim(
        jnp.zeros((hidden_total,), jnp.float32), expand_bias_grad, t * hidden_width, 0
    )
    vector_part = jnp.concatenate(
        [
            gain_one_grad,
            shift_one_grad,
            gain_two_grad,
            shift_two_grad,
            query_bias_grad,
            project_bias_grad,
            shrink_bias_grad,
            split_part,
            value_bias_grad,
        ]
    )
    local_squares = (
        jnp.sum(query_part * query_part)
        + jnp.sum(expand_part * expand_part)
        + jnp.sum(shared_piece * shared_piece)
        + jnp.sum(project_part * project_part)
        + jnp.sum(shrink_part * shrink_part)
    )
    length = vector_part.shape[0]
    unit = n * 8 * 128
    padded = -(-(length + 1) // unit) * unit
    everything = jnp.concatenate(
        [vector_part, local_squares[None], jnp.zeros((padded - length - 1,), jnp.float32)]
    )
    summed = sum_all(everything.reshape(padded // 128, 128), n_dp, n, 8).reshape(padded)
    vector_grad, weight_squares = summed[:length], summed[length]
    grad_size = jnp.sqrt(weight_squares + jnp.sum(vector_grad * vector_grad))
    clip_factor = jnp.minimum(1.0, clip_level / (grad_size + 1e-06))
    clipped_vectors = clip_factor * vector_grad
    query_new = adamw_step(
        query_weight,
        query_moment,
        query_square,
        clip_factor * query_part,
        rate_matrix * width ** (-0.5),
    )
    shared_new = adamw_step(
        shared_weight,
        shared_moment,
        shared_square,
        clip_factor * shared_piece,
        rate_attention * width ** (-0.5),
    )
    project_new = adamw_step(
        project_weight,
        project_moment,
        project_square,
        clip_factor * project_part,
        rate_attention * width ** (-0.5),
    )
    expand_new = adamw_step(
        expand_weight,
        expand_moment,
        expand_square,
        clip_factor * expand_part,
        rate_matrix * width ** (-0.5),
    )
    shrink_new = adamw_step(
        shrink_weight,
        shrink_moment,
        shrink_square,
        clip_factor * shrink_part,
        rate_matrix * hidden_total ** (-0.5),
    )
    vectors_new = adamw_step(
        vectors_value, vectors_moment, vectors_square, clipped_vectors, rate_vector
    )
    return (
        output_rows,
        grad_rows,
        grad_size,
        *query_new,
        *shared_new,
        *project_new,
        *expand_new,
        *shrink_new,
        *vectors_new,
        clipped_vectors,
        token_rms,
    )


def solution(mesh):
    by_rows = P("dp", None)
    query = P("dp", "tensor")
    shared = P(("dp", "tensor"), None)
    project = P("tensor", "dp")
    return jax.shard_map(
        local,
        mesh=mesh,
        in_specs=(
            *(by_rows,) * 3,
            P(),
            *(query,) * 3,
            *(shared,) * 3,
            *(project,) * 3,
            *(query,) * 3,
            *(project,) * 3,
            *(P(),) * 3,
        ),
        out_specs=(
            *(by_rows,) * 2,
            P(),
            *(query,) * 3,
            *(shared,) * 3,
            *(project,) * 3,
            *(query,) * 3,
            *(project,) * 3,
            *(P(),) * 4,
            P("dp"),
        ),
        check_vma=False,
    )
```
